512 devices in a mesh: chan: 16 (over z_hi, y, core), tm: 32 (over x, z_lo).
Axes of the slice: x: 4, y: 4, z: 16 (z_hi: 2, z_lo: 8; z = z_hi * 8 + z_lo), core: 2. Of those that a mesh axis runs over, the one named last changes fastest.
Arguments:
- signal: bfloat16 [4096, 131072], P('chan', 'tm'), may hold values from -6 to 6
- spatial: float32 [4096, 64], P('chan'), may hold values from -0.09375 to 0.09375
- temporal: float32 [64, 128], replicated, may hold values from -0.5 to 0.5
- activations: float32 [64, 131072], P(None, 'tm'), may hold values from 0 to 1
- threshold: float32 [64], replicated, may hold values from 0.05 to 0.5
- step_size: float32 [1], replicated, may hold values from 0.06 to 0.12
Outputs:
- refined: float32 [64, 131072], P(None, 'tm')
The draws below stay inside these ranges and needn't reach their ends.
All inputs are finite; a program needn't handle non-finite values.
Results may differ from the reference program's by a relative error of at most 0.0003.
Values sent between devices are 32-bit elements; how exact they have to be, the bound alone decides.
No kernel may reach another device: no remote copies, remote signals or barrier semaphores. Data moves between devices by JAX's collectives and lax.ppermute only.
A program may use at most 64 MiB of HBM per device.

```python
import math
import jax
import jax.numpy as jnp
from jax import lax

CHANNELS = 4096
ATOMS = 64
ATOM_LEN = 128
TIME_DEV = 4096
ITERS = 2
SAMPLES = 131072
N_TM = 32


def shard_levels(rng, shape, cuts, low, largest):
    factor_of, own = 1.0, jax.random.fold_in(rng, 6)
    for position, blocks in cuts:
        heights = jnp.exp(jax.random.uniform(jax.random.fold_in(own, position), (blocks,), jnp.float32, low / len(cuts), largest / len(cuts)))
        factor_of = factor_of * jnp.repeat(heights, shape[position] // blocks).reshape([-1 if axis == position else 1 for axis in range(len(shape))])
    return factor_of


def bell_draw(rng, dims, scale, most, shards=(), held_as=jnp.bfloat16):
    entries = scale * jax.random.normal(rng, dims, jnp.float32)
    if shards:
        entries = entries * shard_levels(rng, dims, shards, -0.22, 0.18)
    return jnp.clip(entries, -most, most).astype(held_as)


def setup_inputs(seed: int = 0) -> dict:
    key_list = jax.random.split(jax.random.key(seed), 7)
    signal = bell_draw(key_list[0], (CHANNELS, SAMPLES), 1.0, 6.0, ((0, 16), (1, 32)))
    spatial = bell_draw(key_list[1], (CHANNELS, ATOMS), CHANNELS ** -0.5, 0.09375, ((0, 16),), jnp.float32)
    temporal = bell_draw(key_list[2], (ATOMS, ATOM_LEN), ATOM_LEN ** -0.5, 0.5, (), jnp.float32)
    activations = jnp.clip(1.0 * jax.random.uniform(key_list[3], (ATOMS, SAMPLES), jnp.float32) ** shard_levels(key_list[3], (ATOMS, SAMPLES), ((1, 32),), -0.2, 0.2), 0.0, 1.0)
    threshold = jnp.clip(jnp.exp(jax.random.uniform(key_list[4], (ATOMS,), jnp.float32, math.log(0.05), math.log(0.5))), 0.05, 0.5)
    step_size = jnp.clip(jax.random.uniform(key_list[5], (1,), jnp.float32, 0.06, 0.12), 0.06, 0.12)
    return {"signal": signal, "spatial": spatial, "temporal": temporal, "activations": activations, "threshold": threshold, "step_size": step_size}


def make_bands(temporal):
    length = temporal.shape[1]
    positions = jnp.arange(length, dtype=jnp.int32)
    offsets = positions[None, :] - positions[:, None]
    lookup_table = temporal[:, offsets % length]
    current_band = jnp.where(offsets[None] >= 0, lookup_table, 0.0)
    carry_band = jnp.where(offsets[None] < 0, lookup_table, 0.0)
    return current_band, carry_band


def conv_blocks(field, left_rim, current_band, carry_band):
    atoms, width = field.shape
    length = current_band.shape[1]
    blocks = field.reshape(atoms, width // length, length)
    before = jnp.concatenate([left_rim[:, None, :], blocks[:, :-1]], axis=1)
    result = jnp.einsum("kja,kab->kjb", blocks, current_band, precision=lax.Precision.HIGHEST)
    result = result + jnp.einsum("kja,kab->kjb", before, carry_band, precision=lax.Precision.HIGHEST)
    return result.reshape(atoms, width)


def corr_blocks(field, right_rim, current_band, carry_band):
    atoms, width = field.shape
    length = current_band.shape[1]
    blocks = field.reshape(atoms, width // length, length)
    after = jnp.concatenate([blocks[:, 1:], right_rim[:, None, :]], axis=1)
    result = jnp.einsum("kjb,kab->kja", blocks, current_band, precision=lax.Precision.HIGHEST)
    result = result + jnp.einsum("kjb,kab->kja", after, carry_band, precision=lax.Precision.HIGHEST)
    return result.reshape(atoms, width)


def reference(signal, spatial, temporal, activations, threshold, step_size):
    current_band, carry_band = make_bands(temporal)
    atoms = temporal.shape[0]
    length = temporal.shape[1]
    zero_rim = jnp.zeros((atoms, length), jnp.float32)
    point = activations
    previous = activations
    inertia = 1.0
    for iteration in range(ITERS):
        rebuilt = conv_blocks(point, zero_rim, current_band, carry_band)

        def project(block_index):
            first_column = block_index * TIME_DEV
            signal_piece = lax.dynamic_slice_in_dim(signal, first_column, TIME_DEV, 1).astype(jnp.float32)
            rebuilt_piece = lax.dynamic_slice_in_dim(rebuilt, first_column, TIME_DEV, 1)
            residual = jnp.dot(spatial, rebuilt_piece, precision=lax.Precision.HIGHEST, preferred_element_type=jnp.float32) - signal_piece
            return jnp.dot(spatial.T, residual, precision=lax.Precision.HIGHEST, preferred_element_type=jnp.float32)

        pieces = lax.map(project, jnp.arange(N_TM, dtype=jnp.int32))
        projected = jnp.transpose(pieces, (1, 0, 2)).reshape(atoms, SAMPLES)
        gradient = corr_blocks(projected, zero_rim, current_band, carry_band)
        update = jnp.maximum(point - step_size[0] * (gradient + threshold[:, None]), 0.0)
        inertia_next = (1.0 + (1.0 + 4.0 * inertia * inertia) ** 0.5) / 2.0
        point = update + ((inertia - 1.0) / inertia_next) * (update - previous)
        previous = update
        inertia = inertia_next
    return previous
```

```python
import jax
import jax.numpy as jnp
from jax import lax
from jax.experimental import pallas as pl
from jax.experimental.pallas import tpu as pltpu
from jax.sharding import Mesh, PartitionSpec as P

ATOMS = 64
LENGTH = 128
CHUNK = 512
HALF = CHUNK // 2
CHUNKS = 8
LANES = 2 * ATOMS
ROWS = ATOMS + 8
GROUP = 16
HIGHEST = lax.Precision.HIGHEST
F32 = jnp.float32
VMEM = pl.BlockSpec(memory_space=pltpu.VMEM)
SMEM = pl.BlockSpec(memory_space=pltpu.SMEM)


def cost(flops, bytes_accessed):
    return pl.CostEstimate(flops=flops, bytes_accessed=bytes_accessed, transcendentals=0)


def project_body(half_ref, spatial_ref, signal_ref, out_ref, parts_ref, gram_ref):
    @pl.when(pl.program_id(0) == 0)
    def _():
        spatial = spatial_ref[...]
        high = spatial.astype(jnp.bfloat16)
        low = (spatial - high.astype(F32)).astype(jnp.bfloat16)
        parts_ref[:, :ATOMS] = high
        parts_ref[:, ATOMS:] = low
        gram = lax.dot_general(
            spatial, spatial, (((0,), (0,)), ((), ())), precision=HIGHEST, preferred_element_type=F32
        )
        gram_ref[...] = jnp.concatenate([gram[8 * i : 8 * i + 8] for i in range(8)], axis=1)

    product = lax.dot_general(
        parts_ref[...], signal_ref[...], (((0,), (0,)), ((), ())), preferred_element_type=F32
    )
    out_ref[0, :ATOMS] = product[:ATOMS] + product[ATOMS:]
    out_ref[0, ATOMS:] = gram_ref[...]


def project_half(half, spatial, signal):
    channels, width = signal.shape
    count = width // (2 * CHUNK)
    return pl.pallas_call(
        project_body,
        grid_spec=pltpu.PrefetchScalarGridSpec(
            num_scalar_prefetch=1,
            grid=(count,),
            in_specs=[
                pl.BlockSpec((channels, ATOMS), lambda i, half: (0, 0)),
                pl.BlockSpec((channels, CHUNK), lambda i, half: (0, half[0] * count + i)),
            ],
            out_specs=pl.BlockSpec((1, ROWS, CHUNK), lambda i, half: (i, 0, 0)),
            scratch_shapes=[pltpu.VMEM((channels, LANES), jnp.bfloat16), pltpu.VMEM((8, CHUNK), F32)],
        ),
        out_shape=jax.ShapeDtypeStruct((count, ROWS, CHUNK), F32),
        cost_estimate=cost(2 * channels * LANES * width // 2, channels * width),
    )(half, spatial, signal)


def spread_taps(temporal_ref, taps_ref):
    temporal = temporal_ref[...]
    columns = jnp.concatenate([temporal, temporal], axis=0).T
    for tap in range(LENGTH):
        taps_ref[tap] = jnp.broadcast_to(columns[tap : tap + 1], (8, LANES))


def filter_rows(source_ref, shifted_ref, taps_ref, outputs, reverse, emit):
    inputs = outputs + 15
    for b in range(8):
        start = b + 1 if reverse else b
        shifted_ref[b, :inputs] = source_ref[start : start + 8 * inputs].reshape(inputs, 8, LANES)
    for first in range(0, outputs, GROUP):
        count = min(GROUP, outputs - first)

        def add_taps(b, sums):
            sums = list(sums)
            taps = [taps_ref[LENGTH - 1 - 8 * a - b if reverse else 8 * a + b] for a in range(16)]
            for j in range(count + 15):
                value = shifted_ref[b, first + j]
                for a in range(max(0, j - count + 1), min(16, j + 1)):
                    sums[j - a] = sums[j - a] + value * taps[a]
            return tuple(sums)

        zeros = tuple(jnp.zeros((8, LANES), F32) for _ in range(count))
        sums = lax.fori_loop(0, 8, add_taps, zeros)
        emit(8 * first, jnp.concatenate(sums, axis=0))


def rebuild_body(
    place_ref, temporal_ref, before_ref, first_ref, second_ref, after_ref, edge_ref,
    rebuilt_ref, point_ref, taps_ref, wide_ref, rows_ref, shifted_ref,
):
    place = place_ref[0]
    spread_taps(temporal_ref, taps_ref)
    edge = edge_ref[...]
    before = jnp.where(place == 0, edge, before_ref[...])
    after = jnp.where(place == CHUNKS - 1, edge, after_ref[...])
    first, second = first_ref[...], second_ref[...]
    for lane, piece in enumerate((before, first, second)):
        wide_ref[:ATOMS, lane * HALF : (lane + 1) * HALF] = piece
    for lane, piece in enumerate((first, second, after)):
        wide_ref[ATOMS:, lane * HALF : (lane + 1) * HALF] = piece
    rows_ref[...] = wide_ref[...].T
    point_ref[...] = rows_ref[LENGTH : LENGTH + CHUNK]

    def emit(row, values):
        rebuilt_ref[row : row + values.shape[0]] = values

    filter_rows(rows_ref, shifted_ref, taps_ref, 80, True, emit)


def rebuild(place, temporal, activations, edge):
    atoms, width = activations.shape
    last = width // HALF - 1
    block = (atoms, HALF)
    return pl.pallas_call(
        rebuild_body,
        grid_spec=pltpu.PrefetchScalarGridSpec(
            num_scalar_prefetch=1,
            grid=(1,),
            in_specs=[
                pl.BlockSpec((ATOMS, LENGTH), lambda i, place: (0, 0)),
                pl.BlockSpec(block, lambda i, place: (0, jnp.maximum(2 * place[0] - 1, 0))),
                pl.BlockSpec(block, lambda i, place: (0, 2 * place[0])),
                pl.BlockSpec(block, lambda i, place: (0, 2 * place[0] + 1)),
                pl.BlockSpec(block, lambda i, place: (0, jnp.minimum(2 * place[0] + 2, last))),
                pl.BlockSpec(block, lambda i, place: (0, 0)),
            ],
            out_specs=[
                pl.BlockSpec((640, LANES), lambda i, place: (0, 0)),
                pl.BlockSpec((512, LANES), lambda i, place: (0, 0)),
            ],
            scratch_shapes=[
                pltpu.VMEM((LENGTH, 8, LANES), F32),
                pltpu.VMEM((LANES, 768), F32),
                pltpu.VMEM((768, LANES), F32),
                pltpu.VMEM((8, 95, 8, LANES), F32),
            ],
        ),
        out_shape=[
            jax.ShapeDtypeStruct((640, LANES), F32),
            jax.ShapeDtypeStruct((512, LANES), F32),
        ],
        cost_estimate=cost(2 * 640 * LANES * LENGTH, 2**20),
    )(place, temporal, activations, activations, activations, activations, edge)


def steps_body(
    where_ref, step_ref, mine_ref, left_ref, right_ref, rebuilt_ref, point_ref, temporal_ref,
    threshold_ref, out_ref, taps_ref, wide_ref, cross_ref, proj_ref, next_ref, shifted_ref, mix_ref,
):
    begin, total = where_ref[0], where_ref[1]
    rate = step_ref[0]
    spread_taps(temporal_ref, taps_ref)
    gram_rows = mine_ref[ATOMS:]
    gram = jnp.concatenate([gram_rows[:, ATOMS * i : ATOMS * (i + 1)] for i in range(8)], axis=0)
    mix_ref[...] = jnp.zeros_like(mix_ref)
    mix_ref[:ATOMS, :ATOMS] = gram
    mix_ref[ATOMS:, ATOMS:] = gram
    mine = mine_ref[:ATOMS]
    wide_ref[:ATOMS, :128] = left_ref[...]
    wide_ref[:ATOMS, 128:640] = mine
    wide_ref[ATOMS:, :384] = mine[:, 128:]
    wide_ref[ATOMS:, 384:] = right_ref[...]
    cross_ref[...] = wide_ref[...].T

    segment = lax.broadcasted_iota(jnp.int32, (1, LANES), 1) // ATOMS * HALF + begin

    def sample(first, rows):
        return lax.broadcasted_iota(jnp.int32, (rows, 1), 0) + first + segment

    def mixed(rebuilt):
        return jnp.dot(rebuilt, mix_ref[...], precision=HIGHEST, preferred_element_type=F32)

    shrink = threshold_ref[...]

    proj = mixed(rebuilt_ref[...]) - cross_ref[...]
    proj_ref[...] = jnp.where(sample(-128, 640) < total, proj, 0.0)

    inertia = 1.0
    inertia_next = (1.0 + (1.0 + 4.0 * inertia * inertia) ** 0.5) / 2.0
    momentum = (inertia - 1.0) / inertia_next

    def first_step(row, gradient):
        count = gradient.shape[0]
        point = point_ref[row : row + count]
        update = jnp.maximum(point - rate * (gradient + shrink), 0.0)
        point = update + momentum * (update - point)
        next_ref[row : row + count] = jnp.where(sample(row - 128, count) >= 0, point, 0.0)

    filter_rows(proj_ref, shifted_ref, taps_ref, 64, False, first_step)

    def second_rebuilt(row, values):
        cross_part = cross_ref[128 + row : 128 + row + values.shape[0]]
        proj = mixed(values) - cross_part
        proj_ref[row : row + values.shape[0]] = jnp.where(
            sample(row, values.shape[0]) < total, proj, 0.0
        )

    filter_rows(next_ref, shifted_ref, taps_ref, 48, True, second_rebuilt)

    def second_step(row, gradient):
        count = gradient.shape[0]
        point = next_ref[128 + row : 128 + row + count]
        update = jnp.maximum(point - rate * (gradient + shrink), 0.0)
        columns = update.T
        out_ref[:, row : row + count] = columns[:ATOMS]
        out_ref[:, HALF + row : HALF + row + count] = columns[ATOMS:]

    filter_rows(proj_ref, shifted_ref, taps_ref, 32, False, second_step)


def steps(where, step_size, mine, left, right, rebuilt, point, temporal, threshold):
    return pl.pallas_call(
        steps_body,
        in_specs=[SMEM, SMEM] + [VMEM] * 7,
        out_specs=VMEM,
        out_shape=jax.ShapeDtypeStruct((ATOMS, CHUNK), F32),
        scratch_shapes=[
            pltpu.VMEM((LENGTH, 8, LANES), F32),
            pltpu.VMEM((LANES, 640), F32),
            pltpu.VMEM((640, LANES), F32),
            pltpu.VMEM((640, LANES), F32),
            pltpu.VMEM((512, LANES), F32),
            pltpu.VMEM((8, 79, 8, LANES), F32),
            pltpu.VMEM((LANES, LANES), F32),
        ],
        cost_estimate=cost(2 * 1152 * LANES * LENGTH, 2**20),
    )(where, step_size, mine, left, right, rebuilt, point, temporal, threshold)


def place_body(half_ref, mine_ref, other_ref, out_ref):
    first = pl.program_id(0) // 4 == half_ref[0]
    out_ref[...] = jnp.where(first, mine_ref[0], other_ref[0])


def place_chunks(half, mine, other):
    count = mine.shape[0]
    block = (1, ATOMS, CHUNK)
    return pl.pallas_call(
        place_body,
        grid_spec=pltpu.PrefetchScalarGridSpec(
            num_scalar_prefetch=1,
            grid=(2 * count,),
            in_specs=[pl.BlockSpec(block, lambda i, half: (i % count, 0, 0))] * 2,
            out_specs=pl.BlockSpec((ATOMS, CHUNK), lambda i, half: (0, i)),
        ),
        out_shape=jax.ShapeDtypeStruct((ATOMS, 2 * count * CHUNK), F32),
        cost_estimate=cost(0, 3 * 2**20),
    )(half, mine, other)


def solution(mesh):
    blocks = mesh.shape["tm"]
    split = Mesh(mesh.devices.reshape(2, 4, 2, blocks), ("zh", "y", "c", "tm"))
    swap = [(0, 1), (1, 0)]
    line = ("y", "c", "tm")

    def device(y, c, tm):
        return (y * 2 + c) * blocks + tm

    order = [device(q % 4, q // 4, tm) for tm in range(blocks) for q in range(CHUNKS)]
    to_next = list(zip(order[:-1], order[1:]))
    to_previous = list(zip(order[1:], order[:-1]))
    rims = []
    for tm in range(blocks - 1):
        last, first = device(3, 1, tm), device(0, 0, tm + 1)
        rims += [(last, first), (first, last)]

    def per_device(signal, spatial, temporal, activations, threshold, step_size):
        half = lax.axis_index("c").astype(jnp.int32)
        place = half * 4 + lax.axis_index("y").astype(jnp.int32)
        time_block = lax.axis_index("tm").astype(jnp.int32)
        width = activations.shape[1]

        away = project_half((1 - half)[None], spatial, signal)
        arrived = lax.ppermute(away, "c", swap)
        kept = project_half(half[None], spatial, signal)
        pieces = lax.all_to_all(kept + arrived, "y", 0, 0, tiled=True)
        group_sum = jnp.sum(pieces, axis=0)
        other_sum = lax.ppermute(group_sum, "zh", swap)

        edge = jnp.where(place == 0, activations[:, :HALF], activations[:, width - HALF :])
        edge = lax.ppermute(edge, line, rims)
        rebuilt, point = rebuild(place[None], temporal, activations, edge)

        mine = group_sum + other_sum
        right = lax.ppermute(mine[:ATOMS, :256], line, to_previous)
        left = lax.ppermute(mine[:ATOMS, CHUNK - 128 :], line, to_next)
        where = jnp.stack([time_block * width + place * CHUNK, jnp.int32(blocks * width)])
        shrink = jnp.concatenate([threshold, threshold])[None, :]
        update = steps(where, step_size, mine, left, right, rebuilt, point, temporal, shrink)

        gathered = lax.all_gather(update, "y", axis=0)
        other = lax.ppermute(gathered, "c", swap)
        return place_chunks(half[None], gathered, other)

    chan = ("zh", "y", "c")
    in_specs = (P(chan, "tm"), P(chan, None), P(), P(None, "tm"), P(), P())
    return jax.shard_map(
        per_device, mesh=split, in_specs=in_specs, out_specs=P(None, "tm"), check_vma=False
    )
```

```python
import jax
import jax.numpy as jnp
from jax import lax
from jax.experimental import pallas as pl
from jax.experimental.pallas import tpu as pltpu
from jax.sharding import Mesh, PartitionSpec as P

ATOMS = 64
LENGTH = 128
CHUNK = 512
CHUNKS = 8
QUARTER = 4
LANES = 2 * ATOMS
ROWS = ATOMS + 8
SEGMENT = 56
SIDE = 8 * SEGMENT
WINDOW = 2 * SIDE
PHASE = SEGMENT // 4
REACH = 46
HIGHEST = lax.Precision.HIGHEST
F32 = jnp.float32
VMEM = pl.BlockSpec(memory_space=pltpu.VMEM)
SMEM = pl.BlockSpec(memory_space=pltpu.SMEM)
ANY = pl.BlockSpec(memory_space=pl.ANY)


def cost(flops, bytes_accessed):
    return pl.CostEstimate(flops=flops, bytes_accessed=bytes_accessed, transcendentals=0)


def params(mebibytes):
    return pltpu.CompilerParams(vmem_limit_bytes=mebibytes * 2**20)


def project_body(half_ref, spatial_ref, signal_ref, out_ref, block_ref, sems):
    def fetch(i):
        column = pl.multiple_of((half_ref[0] * QUARTER + i) * CHUNK, CHUNK)
        return pltpu.make_async_copy(
            signal_ref.at[:, pl.ds(column, CHUNK)], block_ref.at[i], sems.at[i]
        )

    for i in range(QUARTER):
        fetch(i).start()
    spatial = spatial_ref[...]
    high = spatial.astype(jnp.bfloat16)
    low = (spatial - high.astype(F32)).astype(jnp.bfloat16)
    parts = jnp.concatenate([high, low], axis=0)
    gram = lax.dot_general(
        spatial, spatial, (((1,), (1,)), ((), ())), precision=HIGHEST, preferred_element_type=F32
    )
    gram = jnp.concatenate([gram[8 * i : 8 * i + 8] for i in range(8)], axis=1)
    for i in range(QUARTER):
        out_ref[i, ATOMS:] = gram
    for i in range(QUARTER):
        fetch(i).wait()
        product = jnp.dot(parts, block_ref[i], preferred_element_type=F32)
        out_ref[i, :ATOMS] = product[:ATOMS] + product[ATOMS:]


def project_half(half, spatial, signal):
    channels, width = signal.shape
    return pl.pallas_call(
        project_body,
        in_specs=[SMEM, VMEM, ANY],
        out_specs=VMEM,
        out_shape=jax.ShapeDtypeStruct((QUARTER, ROWS, CHUNK), F32),
        scratch_shapes=[
            pltpu.VMEM((QUARTER, channels, CHUNK), jnp.bfloat16),
            pltpu.SemaphoreType.DMA((QUARTER,)),
        ],
        compiler_params=params(8),
        cost_estimate=cost(2 * channels * LANES * width // 2, channels * width),
    )(half, spatial, signal)


def to_segments(wide_ref, out_ref):
    columns = wide_ref[...].T
    for s in range(8):
        out_ref[pl.ds(s, SEGMENT, stride=8)] = columns[s * SEGMENT : (s + 1) * SEGMENT]


def spread_taps(temporal_ref, taps_ref):
    temporal = temporal_ref[...]
    columns = jnp.concatenate([temporal, temporal], axis=0).T
    for i in range(LENGTH // 4):
        c0, c1, c2, c3 = (
            jnp.broadcast_to(columns[4 * i + p : 4 * i + p + 1], (8, LANES)) for p in range(4)
        )
        even, odd = c0 + c1, c2 + c3
        for k, tap in enumerate((c0, c0 + c2, c2, even, even + odd, odd, c1, c1 + c3, c3)):
            taps_ref[k, i] = tap


def lane_half():
    return lax.broadcasted_iota(jnp.int32, (1, 8, LANES), 2) // ATOMS


def sublane():
    return lax.broadcasted_iota(jnp.int32, (1, 8, LANES), 1)


def later_segment(rows):
    up = pltpu.roll(rows, 7, 1)
    return jnp.where(sublane() == 7, pltpu.roll(up, ATOMS, 2), up)


def earlier_segment(rows):
    down = pltpu.roll(rows, 1, 1)
    return jnp.where(sublane() == 0, pltpu.roll(down, ATOMS, 2), down)


def spread_later(rows, spread_ref):
    for first in range(0, 4 * REACH, SEGMENT):
        count = min(SEGMENT, 4 * REACH - first)
        spread_ref[first // 4 : (first + count) // 4] = rows[:count].reshape(count // 4, 4, 8, LANES)
        if count == SEGMENT:
            rows = later_segment(rows)


def spread_earlier(rows, spread_ref, outside=None):
    start = LENGTH
    while True:
        skip = max(0, -start)
        kept = rows[skip:]
        first, count = start + skip, SEGMENT - skip
        spread_ref[first // 4 : (first + count) // 4] = kept.reshape(count // 4, 4, 8, LANES)
        if start <= 0:
            return
        rows = earlier_segment(rows)
        start -= SEGMENT
        if outside is not None:
            rim = outside(start)
            rows = jnp.where((sublane() == 0) & (lane_half() == 0), rim, rows)


def short_inputs(spread_ref, inputs_ref, offset):
    count = REACH - 1

    def x(p):
        p = p + offset
        return spread_ref[p // 4 : p // 4 + count, p % 4]

    x0, x1, x2, x3, x4, x5 = (x(p) for p in range(6))
    inputs_ref[0, :count] = (x0 - x1) - (x2 - x3)
    inputs_ref[1, :count] = x2 - x3
    inputs_ref[2, :count] = (x4 - x5) - (x2 - x3)
    inputs_ref[3, :count] = x1 - x3
    inputs_ref[4, :count] = x3
    inputs_ref[5, :count] = x5 - x3
    inputs_ref[6, :count] = (x2 - x1) - (x4 - x3)
    inputs_ref[7, :count] = x4 - x3
    last = min(count, REACH - (6 + offset) // 4)
    x6 = spread_ref[(6 + offset) // 4 : (6 + offset) // 4 + last, (6 + offset) % 4]
    inputs_ref[8, :last] = (x6 - x5[:last]) - (x4[:last] - x3[:last])


def filter_rows(inputs_ref, taps_ref, sums_ref, reverse):
    taps = LENGTH // 4

    @pl.loop(0, 9)
    def _(k):
        sums = [None] * PHASE
        held = {}
        for j in range(PHASE + taps - 1):
            if j < taps:
                held[j] = taps_ref[8 - k, taps - 1 - j] if reverse else taps_ref[k, j]
            value = inputs_ref[k, j]
            for m in range(max(0, j - PHASE + 1), min(taps, j + 1)):
                term = value * held[m]
                sums[j - m] = term if sums[j - m] is None else sums[j - m] + term
        for i in range(PHASE):
            sums_ref[k, i] = sums[i]

    a, b, c = sums_ref[0] + sums_ref[1], sums_ref[3] + sums_ref[4], sums_ref[6] + sums_ref[7]
    d, e, f = sums_ref[1] + sums_ref[2], sums_ref[4] + sums_ref[5], sums_ref[7] + sums_ref[8]
    rows = jnp.stack([a + b, b + c, d + e, e + f], axis=1)
    return rows.reshape(SEGMENT, 8, LANES)


FILTER_SCRATCH = [
    pltpu.VMEM((9, LENGTH // 4, 8, LANES), F32),
    pltpu.VMEM((REACH, 4, 8, LANES), F32),
    pltpu.VMEM((9, REACH, 8, LANES), F32),
    pltpu.VMEM((9, PHASE, 8, LANES), F32),
    pltpu.VMEM((LANES, 512), F32),
]


def rebuild_body(
    place_ref, temporal_ref, before_ref, first_ref, second_ref, after_ref, edge_ref,
    rebuilt_ref, point_ref, taps_ref, spread_ref, inputs_ref, sums_ref, wide_ref, rim_ref,
):
    place = place_ref[0]
    spread_taps(temporal_ref, taps_ref)
    edge = edge_ref[...]
    before = jnp.where(place == 0, edge, before_ref[...])
    after = jnp.where(place == CHUNKS - 1, edge, after_ref[...])
    second = second_ref[...]
    wide_ref[:ATOMS] = jnp.concatenate([before[:, 128:], first_ref[...], second[:, :128]], axis=1)
    wide_ref[ATOMS:] = jnp.concatenate([second[:, 64:], after, after[:, :64]], axis=1)
    to_segments(wide_ref, point_ref)
    rim = before[:, :128]
    rim_ref[...] = jnp.concatenate([rim, rim], axis=0).T

    def outside(start):
        count = min(SEGMENT, SEGMENT + start)
        rows = rim_ref[max(start, 0) : max(start, 0) + count].reshape(count, 1, LANES)
        rows = jnp.broadcast_to(rows, (count, 8, LANES))
        if count < SEGMENT:
            rows = jnp.concatenate([jnp.zeros((SEGMENT - count, 8, LANES), F32), rows], axis=0)
        return rows

    rows = point_ref[...].reshape(SEGMENT, 8, LANES)
    spread_earlier(rows, spread_ref, outside)
    short_inputs(spread_ref, inputs_ref, 1)
    rebuilt_ref[...] = filter_rows(inputs_ref, taps_ref, sums_ref, True).reshape(SIDE, LANES)


def rebuild(place, temporal, activations, edge):
    atoms, width = activations.shape
    half = CHUNK // 2
    last = width // half - 1
    block = (atoms, half)
    return pl.pallas_call(
        rebuild_body,
        grid_spec=pltpu.PrefetchScalarGridSpec(
            num_scalar_prefetch=1,
            grid=(1,),
            in_specs=[
                pl.BlockSpec((ATOMS, LENGTH), lambda i, place: (0, 0)),
                pl.BlockSpec(block, lambda i, place: (0, jnp.maximum(2 * place[0] - 1, 0))),
                pl.BlockSpec(block, lambda i, place: (0, 2 * place[0])),
                pl.BlockSpec(block, lambda i, place: (0, 2 * place[0] + 1)),
                pl.BlockSpec(block, lambda i, place: (0, jnp.minimum(2 * place[0] + 2, last))),
                pl.BlockSpec(block, lambda i, place: (0, 0)),
            ],
            out_specs=[pl.BlockSpec((SIDE, LANES), lambda i, place: (0, 0))] * 2,
            scratch_shapes=FILTER_SCRATCH + [pltpu.VMEM((LENGTH, LANES), F32)],
        ),
        out_shape=[jax.ShapeDtypeStruct((SIDE, LANES), F32)] * 2,
        compiler_params=params(12),
        cost_estimate=cost(2 * SIDE * LANES * LENGTH, 2**20),
    )(place, temporal, activations, activations, activations, activations, edge)


def steps_body(
    total, begin_ref, step_ref, mine_ref, left_ref, right_ref, rebuilt_ref, point_ref,
    temporal_ref, threshold_ref, out_ref, taps_ref, spread_ref, inputs_ref, sums_ref, wide_ref,
    cross_ref, mix_ref,
):
    begin = begin_ref[0]
    rate = step_ref[0]
    spread_taps(temporal_ref, taps_ref)
    gram_rows = mine_ref[ATOMS:]
    gram = jnp.concatenate([gram_rows[:, ATOMS * i : ATOMS * (i + 1)] for i in range(8)], axis=0)
    mix_ref[...] = jnp.zeros_like(mix_ref)
    mix_ref[:ATOMS, :ATOMS] = gram
    mix_ref[ATOMS:, ATOMS:] = gram
    mine = mine_ref[:ATOMS]
    right = right_ref[...]
    wide_ref[:ATOMS] = jnp.concatenate([left_ref[...], mine[:, :384]], axis=1)
    wide_ref[ATOMS:] = jnp.concatenate([mine[:, 320:], right, right[:, :64]], axis=1)
    to_segments(wide_ref, cross_ref)

    shape = (SEGMENT, 8, LANES)
    sample = lax.broadcasted_iota(jnp.int32, shape, 0) + (
        (lane_half() * 8 + sublane()) * SEGMENT + (begin - LENGTH)
    )
    shrink = threshold_ref[...]
    shrink = jnp.concatenate([shrink, shrink], axis=1).reshape(1, 1, LANES)

    def projected(rebuilt):
        mixed = jnp.dot(rebuilt, mix_ref[...], precision=HIGHEST, preferred_element_type=F32)
        rows = (mixed - cross_ref[...]).reshape(shape)
        return jnp.where(sample < total, rows, 0.0)

    def stepped(point, rows):
        spread_later(rows, spread_ref)
        short_inputs(spread_ref, inputs_ref, 0)
        gradient = filter_rows(inputs_ref, taps_ref, sums_ref, False)
        return jnp.maximum(point - rate * (gradient + shrink), 0.0)

    inertia = 1.0
    inertia_next = (1.0 + (1.0 + 4.0 * inertia * inertia) ** 0.5) / 2.0
    momentum = (inertia - 1.0) / inertia_next
    previous = point_ref[...].reshape(shape)
    update = stepped(previous, projected(rebuilt_ref[...]))
    point = update + momentum * (update - previous)
    point = jnp.where(sample >= 0, point, 0.0)

    spread_earlier(point, spread_ref)
    short_inputs(spread_ref, inputs_ref, 1)
    rebuilt = filter_rows(inputs_ref, taps_ref, sums_ref, True)
    update = stepped(point, projected(rebuilt.reshape(SIDE, LANES)))

    cross_ref[...] = update.reshape(SIDE, LANES)
    rows = [cross_ref[pl.ds(s, SEGMENT, stride=8)] for s in range(8)]
    rows.append(jnp.zeros((512 - SIDE, LANES), F32))
    columns = jnp.concatenate(rows, axis=0).T
    out_ref[...] = jnp.concatenate([columns[:ATOMS, 128:SIDE], columns[ATOMS:, :192]], axis=1)


def steps(total, begin, step_size, mine, left, right, rebuilt, point, temporal, threshold):
    def body(*refs):
        steps_body(total, *refs)

    return pl.pallas_call(
        body,
        in_specs=[SMEM, SMEM] + [VMEM] * 7,
        out_specs=VMEM,
        out_shape=jax.ShapeDtypeStruct((ATOMS, CHUNK), F32),
        scratch_shapes=FILTER_SCRATCH
        + [pltpu.VMEM((SIDE, LANES), F32), pltpu.VMEM((LANES, LANES), F32)],
        compiler_params=params(12),
        cost_estimate=cost(6 * SIDE * LANES * LENGTH, 2**20),
    )(begin, step_size, mine, left, right, rebuilt, point, temporal, threshold)


def place_copies(half, chunks_ref, out_ref, sems):
    copies = []
    for i in range(QUARTER):
        column = pl.multiple_of((half * QUARTER + i) * CHUNK, CHUNK)
        copies.append(
            pltpu.make_async_copy(chunks_ref.at[i], out_ref.at[:, pl.ds(column, CHUNK)], sems.at[i])
        )
    for copy in copies:
        copy.start()
    for copy in copies:
        copy.wait()


def place_mine_body(half_ref, chunks_ref, out_ref, sems):
    place_copies(half_ref[0], chunks_ref, out_ref, sems)


def place_other_body(half_ref, chunks_ref, begun_ref, out_ref, sems):
    place_copies(1 - half_ref[0], chunks_ref, out_ref, sems)


def place_half(half, chunks, begun=None):
    out_shape = jax.ShapeDtypeStruct((ATOMS, CHUNKS * CHUNK), F32)
    first = begun is None
    return pl.pallas_call(
        place_mine_body if first else place_other_body,
        in_specs=[SMEM, ANY] + ([] if first else [ANY]),
        out_specs=ANY,
        out_shape=out_shape,
        scratch_shapes=[pltpu.SemaphoreType.DMA((QUARTER,))],
        input_output_aliases={} if first else {2: 0},
        compiler_params=params(4),
        cost_estimate=cost(0, 2**20),
    )(half, chunks, *([] if first else [begun]))


def solution(mesh):
    blocks = mesh.shape["tm"]
    split = Mesh(mesh.devices.reshape(2, 4, 2, blocks), ("zh", "y", "c", "tm"))
    swap = [(0, 1), (1, 0)]
    line = ("y", "c", "tm")

    def device(y, c, tm):
        return (y * 2 + c) * blocks + tm

    order = [device(q % 4, q // 4, tm) for tm in range(blocks) for q in range(CHUNKS)]
    to_next = list(zip(order[:-1], order[1:]))
    to_previous = list(zip(order[1:], order[:-1]))
    rims = []
    for tm in range(blocks - 1):
        last, first = device(3, 1, tm), device(0, 0, tm + 1)
        rims += [(last, first), (first, last)]

    def per_device(signal, spatial, temporal, activations, threshold, step_size):
        half = lax.axis_index("c").astype(jnp.int32)
        place = half * 4 + lax.axis_index("y").astype(jnp.int32)
        time_block = lax.axis_index("tm").astype(jnp.int32)
        width = activations.shape[1]
        spatial = spatial.T

        away = project_half((1 - half)[None], spatial, signal)
        arrived = lax.ppermute(away, "c", swap)
        kept = project_half(half[None], spatial, signal)
        summed = kept + arrived
        rim = CHUNK // 2
        edge = jnp.where(place == 0, activations[:, :rim], activations[:, width - rim :])
        edge, summed = lax.optimization_barrier((edge, summed))
        pieces = lax.all_to_all(summed, "y", 0, 0, tiled=True)
        edge = lax.ppermute(edge, line, rims)
        rebuilt, point = rebuild(place[None], temporal, activations, edge)
        group_sum = jnp.sum(pieces, axis=0)
        group_sum, rebuilt, point = lax.optimization_barrier((group_sum, rebuilt, point))
        mine = group_sum + lax.ppermute(group_sum, "zh", swap)

        right = lax.ppermute(mine[:ATOMS, :256], line, to_previous)
        left = lax.ppermute(mine[:ATOMS, CHUNK - 128 :], line, to_next)
        begin = time_block * width + place * CHUNK
        update = steps(
            blocks * width, begin[None], step_size, mine, left, right, rebuilt, point, temporal,
            threshold[None, :],
        )

        gathered = lax.all_gather(update, "y", axis=0)
        other = lax.ppermute(gathered, "c", swap)
        return place_half(half[None], other, place_half(half[None], gathered))

    chan = ("zh", "y", "c")
    in_specs = (P(chan, "tm"), P(chan, None), P(), P(None, "tm"), P(), P())
    return jax.shard_map(
        per_device, mesh=split, in_specs=in_specs, out_specs=P(None, "tm"), check_vma=False
    )
```

```python
import jax
import jax.numpy as jnp
from jax import lax
from jax.experimental import pallas as pl
from jax.experimental.pallas import tpu as pltpu
from jax.sharding import Mesh, PartitionSpec as P

ATOMS = 64
LENGTH = 128
CHUNK = 512
CHUNKS = 8
QUARTER = 4
LANES = 2 * ATOMS
ROWS = ATOMS + 8
SEGMENT = 56
SIDE = 8 * SEGMENT
WINDOW = 2 * SIDE
PHASE = SEGMENT // 4
REACH = 46
HIGHEST = lax.Precision.HIGHEST
F32 = jnp.float32
VMEM = pl.BlockSpec(memory_space=pltpu.VMEM)
SMEM = pl.BlockSpec(memory_space=pltpu.SMEM)
ANY = pl.BlockSpec(memory_space=pl.ANY)
HBM = pl.BlockSpec(memory_space=pltpu.HBM)
RUN = 8


def cost(flops, bytes_accessed):
    return pl.CostEstimate(flops=flops, bytes_accessed=bytes_accessed, transcendentals=0)


def params(mebibytes):
    return pltpu.CompilerParams(vmem_limit_bytes=mebibytes * 2**20)


def project_body(half_ref, spatial_ref, signal_ref, out_ref, block_ref, sems):
    def fetch(i):
        column = pl.multiple_of((2 * i + half_ref[0]) * CHUNK, CHUNK)
        return pltpu.make_async_copy(
            signal_ref.at[:, pl.ds(column, CHUNK)], block_ref.at[i], sems.at[i]
        )

    for i in range(QUARTER):
        fetch(i).start()
    spatial = spatial_ref[...]
    high = spatial.astype(jnp.bfloat16)
    low = (spatial - high.astype(F32)).astype(jnp.bfloat16)
    parts = jnp.concatenate([high, low], axis=0)
    gram = lax.dot_general(
        spatial, spatial, (((1,), (1,)), ((), ())), precision=HIGHEST, preferred_element_type=F32
    )
    gram = jnp.concatenate([gram[8 * i : 8 * i + 8] for i in range(8)], axis=1)
    for i in range(QUARTER):
        out_ref[i, ATOMS:] = gram
    for i in range(QUARTER):
        fetch(i).wait()
        product = jnp.dot(parts, block_ref[i], preferred_element_type=F32)
        out_ref[i, :ATOMS] = product[:ATOMS] + product[ATOMS:]


def project_half(half, spatial, signal):
    channels, width = signal.shape
    return pl.pallas_call(
        project_body,
        in_specs=[SMEM, VMEM, HBM],
        out_specs=VMEM,
        out_shape=jax.ShapeDtypeStruct((QUARTER, ROWS, CHUNK), F32),
        scratch_shapes=[
            pltpu.VMEM((QUARTER, channels, CHUNK), jnp.bfloat16),
            pltpu.SemaphoreType.DMA((QUARTER,)),
        ],
        compiler_params=params(8),
        cost_estimate=cost(2 * channels * LANES * width // 2, channels * width),
    )(half, spatial, signal)


def to_segments(wide_ref, out_ref):
    columns = wide_ref[...].T
    for s in range(8):
        out_ref[pl.ds(s, SEGMENT, stride=8)] = columns[s * SEGMENT : (s + 1) * SEGMENT]


def spread_taps(temporal_ref, taps_ref):
    temporal = temporal_ref[...]
    columns = jnp.concatenate([temporal, temporal], axis=0).T
    for i in range(LENGTH // 4):
        c0, c1, c2, c3 = (
            jnp.broadcast_to(columns[4 * i + p : 4 * i + p + 1], (8, LANES)) for p in range(4)
        )
        even, odd = c0 + c1, c2 + c3
        for k, tap in enumerate((c0, c0 + c2, c2, even, even + odd, odd, c1, c1 + c3, c3)):
            taps_ref[k, i] = tap


def lane_half():
    return lax.broadcasted_iota(jnp.int32, (1, 8, LANES), 2) // ATOMS


def sublane():
    return lax.broadcasted_iota(jnp.int32, (1, 8, LANES), 1)


def later_segment(rows):
    up = pltpu.roll(rows, 7, 1)
    return jnp.where(sublane() == 7, pltpu.roll(up, ATOMS, 2), up)


def earlier_segment(rows):
    down = pltpu.roll(rows, 1, 1)
    return jnp.where(sublane() == 0, pltpu.roll(down, ATOMS, 2), down)


def spread_later(rows, spread_ref):
    for first in range(0, 4 * REACH, SEGMENT):
        count = min(SEGMENT, 4 * REACH - first)
        spread_ref[first // 4 : (first + count) // 4] = rows[:count].reshape(count // 4, 4, 8, LANES)
        if count == SEGMENT:
            rows = later_segment(rows)


def spread_earlier(rows, spread_ref, outside=None):
    start = LENGTH
    while True:
        skip = max(0, -start)
        kept = rows[skip:]
        first, count = start + skip, SEGMENT - skip
        spread_ref[first // 4 : (first + count) // 4] = kept.reshape(count // 4, 4, 8, LANES)
        if start <= 0:
            return
        rows = earlier_segment(rows)
        start -= SEGMENT
        if outside is not None:
            rim = outside(start)
            rows = jnp.where((sublane() == 0) & (lane_half() == 0), rim, rows)


def short_inputs(spread_ref, inputs_ref, offset):
    count = REACH - 1

    def x(p):
        p = p + offset
        return spread_ref[p // 4 : p // 4 + count, p % 4]

    x0, x1, x2, x3, x4, x5 = (x(p) for p in range(6))
    inputs_ref[0, :count] = (x0 - x1) - (x2 - x3)
    inputs_ref[1, :count] = x2 - x3
    inputs_ref[2, :count] = (x4 - x5) - (x2 - x3)
    inputs_ref[3, :count] = x1 - x3
    inputs_ref[4, :count] = x3
    inputs_ref[5, :count] = x5 - x3
    inputs_ref[6, :count] = (x2 - x1) - (x4 - x3)
    inputs_ref[7, :count] = x4 - x3
    last = min(count, REACH - (6 + offset) // 4)
    x6 = spread_ref[(6 + offset) // 4 : (6 + offset) // 4 + last, (6 + offset) % 4]
    inputs_ref[8, :last] = (x6 - x5[:last]) - (x4[:last] - x3[:last])


def filter_rows(inputs_ref, taps_ref, sums_ref, reverse):
    taps = LENGTH // 4

    @pl.loop(0, 9)
    def _(k):
        sums = [None] * PHASE
        held = {}
        for j in range(PHASE + taps - 1):
            if j < taps:
                held[j] = taps_ref[8 - k, taps - 1 - j] if reverse else taps_ref[k, j]
            value = inputs_ref[k, j]
            for m in range(max(0, j - PHASE + 1), min(taps, j + 1)):
                term = value * held[m]
                sums[j - m] = term if sums[j - m] is None else sums[j - m] + term
        for i in range(PHASE):
            sums_ref[k, i] = sums[i]

    a, b, c = sums_ref[0] + sums_ref[1], sums_ref[3] + sums_ref[4], sums_ref[6] + sums_ref[7]
    d, e, f = sums_ref[1] + sums_ref[2], sums_ref[4] + sums_ref[5], sums_ref[7] + sums_ref[8]
    rows = jnp.stack([a + b, b + c, d + e, e + f], axis=1)
    return rows.reshape(SEGMENT, 8, LANES)


FILTER_SCRATCH = [
    pltpu.VMEM((9, LENGTH // 4, 8, LANES), F32),
    pltpu.VMEM((REACH, 4, 8, LANES), F32),
    pltpu.VMEM((9, REACH, 8, LANES), F32),
    pltpu.VMEM((9, PHASE, 8, LANES), F32),
    pltpu.VMEM((LANES, 512), F32),
]


def rebuild_body(
    place_ref, temporal_ref, before_ref, first_ref, second_ref, after_ref, edge_ref,
    rebuilt_ref, point_ref, taps_ref, spread_ref, inputs_ref, sums_ref, wide_ref, rim_ref,
):
    place = place_ref[0]
    spread_taps(temporal_ref, taps_ref)
    edge = edge_ref[...]
    before = jnp.where(place == 0, edge, before_ref[...])
    after = jnp.where(place == CHUNKS - 1, edge, after_ref[...])
    second = second_ref[...]
    wide_ref[:ATOMS] = jnp.concatenate([before[:, 128:], first_ref[...], second[:, :128]], axis=1)
    wide_ref[ATOMS:] = jnp.concatenate([second[:, 64:], after, after[:, :64]], axis=1)
    to_segments(wide_ref, point_ref)
    rim = before[:, :128]
    rim_ref[...] = jnp.concatenate([rim, rim], axis=0).T

    def outside(start):
        count = min(SEGMENT, SEGMENT + start)
        rows = rim_ref[max(start, 0) : max(start, 0) + count].reshape(count, 1, LANES)
        rows = jnp.broadcast_to(rows, (count, 8, LANES))
        if count < SEGMENT:
            rows = jnp.concatenate([jnp.zeros((SEGMENT - count, 8, LANES), F32), rows], axis=0)
        return rows

    rows = point_ref[...].reshape(SEGMENT, 8, LANES)
    spread_earlier(rows, spread_ref, outside)
    short_inputs(spread_ref, inputs_ref, 1)
    rebuilt_ref[...] = filter_rows(inputs_ref, taps_ref, sums_ref, True).reshape(SIDE, LANES)


def rebuild(place, temporal, activations, edge):
    atoms, width = activations.shape
    half = CHUNK // 2
    last = width // half - 1
    block = (atoms, half)
    return pl.pallas_call(
        rebuild_body,
        grid_spec=pltpu.PrefetchScalarGridSpec(
            num_scalar_prefetch=1,
            grid=(1,),
            in_specs=[
                pl.BlockSpec((ATOMS, LENGTH), lambda i, place: (0, 0)),
                pl.BlockSpec(block, lambda i, place: (0, jnp.maximum(2 * place[0] - 1, 0))),
                pl.BlockSpec(block, lambda i, place: (0, 2 * place[0])),
                pl.BlockSpec(block, lambda i, place: (0, 2 * place[0] + 1)),
                pl.BlockSpec(block, lambda i, place: (0, jnp.minimum(2 * place[0] + 2, last))),
                pl.BlockSpec(block, lambda i, place: (0, 0)),
            ],
            out_specs=[pl.BlockSpec((SIDE, LANES), lambda i, place: (0, 0))] * 2,
            scratch_shapes=FILTER_SCRATCH + [pltpu.VMEM((LENGTH, LANES), F32)],
        ),
        out_shape=[jax.ShapeDtypeStruct((SIDE, LANES), F32)] * 2,
        compiler_params=params(12),
        cost_estimate=cost(2 * SIDE * LANES * LENGTH, 2**20),
    )(place, temporal, activations, activations, activations, activations, edge)


def steps_body(
    total, begin_ref, half_ref, step_ref, mine_ref, inner_ref, outer_ref, rebuilt_ref, point_ref,
    temporal_ref, threshold_ref, out_ref, taps_ref, spread_ref, inputs_ref, sums_ref, wide_ref,
    cross_ref, mix_ref,
):
    begin = begin_ref[0]
    rate = step_ref[0]
    spread_taps(temporal_ref, taps_ref)
    gram_rows = mine_ref[ATOMS:]
    gram = jnp.concatenate([gram_rows[:, ATOMS * i : ATOMS * (i + 1)] for i in range(8)], axis=0)
    mix_ref[...] = jnp.zeros_like(mix_ref)
    mix_ref[:ATOMS, :ATOMS] = gram
    mix_ref[ATOMS:, ATOMS:] = gram
    mine = mine_ref[:ATOMS]
    first = half_ref[0] == 0
    left = jnp.where(first, outer_ref[:, 128:], inner_ref[:, 128:])
    right = jnp.where(first, inner_ref[...], outer_ref[...])
    wide_ref[:ATOMS] = jnp.concatenate([left, mine[:, :384]], axis=1)
    wide_ref[ATOMS:] = jnp.concatenate([mine[:, 320:], right, right[:, :64]], axis=1)
    to_segments(wide_ref, cross_ref)

    shape = (SEGMENT, 8, LANES)
    sample = lax.broadcasted_iota(jnp.int32, shape, 0) + (
        (lane_half() * 8 + sublane()) * SEGMENT + (begin - LENGTH)
    )
    shrink = threshold_ref[...]
    shrink = jnp.concatenate([shrink, shrink], axis=1).reshape(1, 1, LANES)

    def projected(rebuilt):
        mixed = jnp.dot(rebuilt, mix_ref[...], precision=HIGHEST, preferred_element_type=F32)
        rows = (mixed - cross_ref[...]).reshape(shape)
        return jnp.where(sample < total, rows, 0.0)

    def stepped(point, rows):
        spread_later(rows, spread_ref)
        short_inputs(spread_ref, inputs_ref, 0)
        gradient = filter_rows(inputs_ref, taps_ref, sums_ref, False)
        return jnp.maximum(point - rate * (gradient + shrink), 0.0)

    inertia = 1.0
    inertia_next = (1.0 + (1.0 + 4.0 * inertia * inertia) ** 0.5) / 2.0
    momentum = (inertia - 1.0) / inertia_next
    previous = point_ref[...].reshape(shape)
    update = stepped(previous, projected(rebuilt_ref[...]))
    point = update + momentum * (update - previous)
    point = jnp.where(sample >= 0, point, 0.0)

    spread_earlier(point, spread_ref)
    short_inputs(spread_ref, inputs_ref, 1)
    rebuilt = filter_rows(inputs_ref, taps_ref, sums_ref, True)
    update = stepped(point, projected(rebuilt.reshape(SIDE, LANES)))

    cross_ref[...] = update.reshape(SIDE, LANES)
    rows = [cross_ref[pl.ds(s, SEGMENT, stride=8)] for s in range(8)]
    rows.append(jnp.zeros((512 - SIDE, LANES), F32))
    columns = jnp.concatenate(rows, axis=0).T
    out_ref[...] = jnp.concatenate([columns[:ATOMS, 128:SIDE], columns[ATOMS:, :192]], axis=1)


def steps(total, begin, half, step_size, mine, inner, outer, rebuilt, point, temporal, threshold):
    def body(*refs):
        steps_body(total, *refs)

    return pl.pallas_call(
        body,
        in_specs=[SMEM] * 3 + [VMEM] * 7,
        out_specs=VMEM,
        out_shape=jax.ShapeDtypeStruct((ATOMS, CHUNK), F32),
        scratch_shapes=FILTER_SCRATCH
        + [pltpu.VMEM((SIDE, LANES), F32), pltpu.VMEM((LANES, LANES), F32)],
        compiler_params=params(12),
        cost_estimate=cost(6 * SIDE * LANES * LENGTH, 2**20),
    )(begin, half, step_size, mine, inner, outer, rebuilt, point, temporal, threshold)


def place_copies(half, chunks_ref, out_ref, sems):
    copies = []
    for i in range(QUARTER):
        column = pl.multiple_of((2 * i + half) * CHUNK, CHUNK)
        copies.append(
            pltpu.make_async_copy(chunks_ref.at[i], out_ref.at[:, pl.ds(column, CHUNK)], sems.at[i])
        )
    for copy in copies:
        copy.start()
    for copy in copies:
        copy.wait()


def place_mine_body(half_ref, chunks_ref, out_ref, sems):
    place_copies(half_ref[0], chunks_ref, out_ref, sems)


def place_other_body(half_ref, chunks_ref, begun_ref, out_ref, sems):
    place_copies(1 - half_ref[0], chunks_ref, out_ref, sems)


def place_half(half, chunks, begun=None):
    out_shape = jax.ShapeDtypeStruct((ATOMS, CHUNKS * CHUNK), F32)
    first = begun is None
    return pl.pallas_call(
        place_mine_body if first else place_other_body,
        in_specs=[SMEM, ANY] + ([] if first else [ANY]),
        out_specs=ANY,
        out_shape=out_shape,
        scratch_shapes=[pltpu.SemaphoreType.DMA((QUARTER,))],
        input_output_aliases={} if first else {2: 0},
        compiler_params=params(4),
        cost_estimate=cost(0, 2**20),
    )(half, chunks, *([] if first else [begun]))


def solution(mesh):
    blocks = mesh.shape["tm"]
    split = Mesh(mesh.devices.reshape(2, 4, 2, blocks), ("zh", "y", "c", "tm"))
    swap = [(0, 1), (1, 0)]
    line = ("zh", "y", "c", "tm")

    def device(zh, q, tm):
        return (zh * CHUNKS + q) * blocks + tm

    inside, rims = [], []
    for zh in range(2):
        for tm in range(blocks):
            for q in range(1, CHUNKS - 1, 2):
                inside.append((device(zh, q, tm), device(zh, q + 1, tm)))
            if tm + 1 < blocks:
                near = 1 - zh if (tm + 1) % RUN == 0 else zh
                rims.append((device(zh, CHUNKS - 1, tm), device(near, 0, tm + 1)))
    rims = rims + [(b, a) for a, b in rims]
    outside = rims + inside + [(b, a) for a, b in inside]

    def per_device(signal, spatial, temporal, activations, threshold, step_size):
        half = lax.axis_index("c").astype(jnp.int32)
        place = lax.axis_index("y").astype(jnp.int32) * 2 + half
        time_block = lax.axis_index("tm").astype(jnp.int32)
        width = activations.shape[1]
        spatial = spatial.T

        away = project_half((1 - half)[None], spatial, signal)
        arrived = lax.ppermute(away, "c", swap)
        kept = project_half(half[None], spatial, signal)
        summed = kept + arrived
        rim = CHUNK // 2
        edge = jnp.where(place == 0, activations[:, :rim], activations[:, width - rim :])
        edge, summed = lax.optimization_barrier((edge, summed))
        pieces = lax.all_to_all(summed, "y", 0, 0, tiled=True)
        edge = lax.ppermute(edge, line, rims)
        rebuilt, point = rebuild(place[None], temporal, activations, edge)
        group_sum = jnp.sum(pieces, axis=0)
        group_sum, rebuilt, point = lax.optimization_barrier((group_sum, rebuilt, point))
        mine = group_sum + lax.ppermute(group_sum, "zh", swap)

        start, end = mine[:ATOMS, :rim], mine[:ATOMS, CHUNK - rim :]
        first = half == 0
        outer = lax.ppermute(jnp.where(first, start, end), line, outside)
        inner = lax.ppermute(jnp.where(first, end, start), "c", swap)
        begin = time_block * width + place * CHUNK
        update = steps(
            blocks * width, begin[None], half[None], step_size, mine, inner, outer, rebuilt, point,
            temporal, threshold[None, :],
        )

        gathered = lax.all_gather(update, "y", axis=0)
        other = lax.ppermute(gathered, "c", swap)
        return place_half(half[None], other, place_half(half[None], gathered))

    chan = ("zh", "y", "c")
    in_specs = (P(chan, "tm"), P(chan, None), P(), P(None, "tm"), P(), P())
    return jax.shard_map(
        per_device, mesh=split, in_specs=in_specs, out_specs=P(None, "tm"), check_vma=False
    )
```

```python
import jax
import jax.numpy as jnp
from jax import lax
from jax.experimental import pallas as pl
from jax.experimental.pallas import tpu as pltpu
from jax.sharding import Mesh, PartitionSpec as P

ATOMS = 64
LENGTH = 128
CHUNK = 512
CHUNKS = 8
QUARTER = 4
LANES = 2 * ATOMS
ROWS = ATOMS + 8
SEGMENT = 56
SIDE = 8 * SEGMENT
WINDOW = 2 * SIDE
PHASE = SEGMENT // 4
REACH = 46
HIGHEST = lax.Precision.HIGHEST
F32 = jnp.float32
VMEM = pl.BlockSpec(memory_space=pltpu.VMEM)
SMEM = pl.BlockSpec(memory_space=pltpu.SMEM)
ANY = pl.BlockSpec(memory_space=pl.ANY)
HBM = pl.BlockSpec(memory_space=pltpu.HBM)
RUN = 8


def cost(flops, bytes_accessed):
    return pl.CostEstimate(flops=flops, bytes_accessed=bytes_accessed, transcendentals=0)


def params(mebibytes):
    return pltpu.CompilerParams(vmem_limit_bytes=mebibytes * 2**20)


def project_body(half_ref, spatial_ref, signal_ref, out_ref, block_ref, sems):
    def fetch(i):
        column = pl.multiple_of((2 * i + half_ref[0]) * CHUNK, CHUNK)
        return pltpu.make_async_copy(
            signal_ref.at[:, pl.ds(column, CHUNK)], block_ref.at[i], sems.at[i]
        )

    for i in range(QUARTER):
        fetch(i).start()
    spatial = spatial_ref[...]
    high = spatial.astype(jnp.bfloat16)
    low = (spatial - high.astype(F32)).astype(jnp.bfloat16)
    parts = jnp.concatenate([high, low], axis=0)
    gram = lax.dot_general(
        spatial, spatial, (((1,), (1,)), ((), ())), precision=HIGHEST, preferred_element_type=F32
    )
    gram = jnp.concatenate([gram[8 * i : 8 * i + 8] for i in range(8)], axis=1)
    for i in range(QUARTER):
        out_ref[i, ATOMS:] = gram
    for i in range(QUARTER):
        fetch(i).wait()
        product = jnp.dot(parts, block_ref[i], preferred_element_type=F32)
        out_ref[i, :ATOMS] = product[:ATOMS] + product[ATOMS:]


def project_half(half, spatial, signal):
    channels, width = signal.shape
    return pl.pallas_call(
        project_body,
        in_specs=[SMEM, VMEM, HBM],
        out_specs=VMEM,
        out_shape=jax.ShapeDtypeStruct((QUARTER, ROWS, CHUNK), F32),
        scratch_shapes=[
            pltpu.VMEM((QUARTER, channels, CHUNK), jnp.bfloat16),
            pltpu.SemaphoreType.DMA((QUARTER,)),
        ],
        compiler_params=params(60),
        cost_estimate=cost(2 * channels * LANES * width // 2, channels * width),
    )(half, spatial, signal)


def to_segments(wide_ref, out_ref):
    columns = wide_ref[...].T
    for s in range(8):
        out_ref[pl.ds(s, SEGMENT, stride=8)] = columns[s * SEGMENT : (s + 1) * SEGMENT]


def spread_taps(temporal_ref, taps_ref):
    temporal = temporal_ref[...]
    columns = jnp.concatenate([temporal, temporal], axis=0).T
    for i in range(LENGTH // 4):
        c0, c1, c2, c3 = (
            jnp.broadcast_to(columns[4 * i + p : 4 * i + p + 1], (8, LANES)) for p in range(4)
        )
        even, odd = c0 + c1, c2 + c3
        for k, tap in enumerate((c0, c0 + c2, c2, even, even + odd, odd, c1, c1 + c3, c3)):
            taps_ref[k, i] = tap


def lane_half():
    return lax.broadcasted_iota(jnp.int32, (1, 8, LANES), 2) // ATOMS


def sublane():
    return lax.broadcasted_iota(jnp.int32, (1, 8, LANES), 1)


def later_segment(rows):
    up = pltpu.roll(rows, 7, 1)
    return jnp.where(sublane() == 7, pltpu.roll(up, ATOMS, 2), up)


def earlier_segment(rows):
    down = pltpu.roll(rows, 1, 1)
    return jnp.where(sublane() == 0, pltpu.roll(down, ATOMS, 2), down)


def spread_later(rows, spread_ref):
    for first in range(0, 4 * REACH, SEGMENT):
        count = min(SEGMENT, 4 * REACH - first)
        spread_ref[first // 4 : (first + count) // 4] = rows[:count].reshape(count // 4, 4, 8, LANES)
        if count == SEGMENT:
            rows = later_segment(rows)


def spread_earlier(rows, spread_ref, outside=None):
    start = LENGTH
    while True:
        skip = max(0, -start)
        kept = rows[skip:]
        first, count = start + skip, SEGMENT - skip
        spread_ref[first // 4 : (first + count) // 4] = kept.reshape(count // 4, 4, 8, LANES)
        if start <= 0:
            return
        rows = earlier_segment(rows)
        start -= SEGMENT
        if outside is not None:
            rim = outside(start)
            rows = jnp.where((sublane() == 0) & (lane_half() == 0), rim, rows)


def short_inputs(spread_ref, inputs_ref, offset):
    count = REACH - 1

    def x(p):
        p = p + offset
        return spread_ref[p // 4 : p // 4 + count, p % 4]

    x0, x1, x2, x3, x4, x5 = (x(p) for p in range(6))
    inputs_ref[0, :count] = (x0 - x1) - (x2 - x3)
    inputs_ref[1, :count] = x2 - x3
    inputs_ref[2, :count] = (x4 - x5) - (x2 - x3)
    inputs_ref[3, :count] = x1 - x3
    inputs_ref[4, :count] = x3
    inputs_ref[5, :count] = x5 - x3
    inputs_ref[6, :count] = (x2 - x1) - (x4 - x3)
    inputs_ref[7, :count] = x4 - x3
    last = min(count, REACH - (6 + offset) // 4)
    x6 = spread_ref[(6 + offset) // 4 : (6 + offset) // 4 + last, (6 + offset) % 4]
    inputs_ref[8, :last] = (x6 - x5[:last]) - (x4[:last] - x3[:last])


def filter_rows(inputs_ref, taps_ref, sums_ref, reverse):
    taps = LENGTH // 4

    @pl.loop(0, 9)
    def _(k):
        sums = [None] * PHASE
        held = {}
        for j in range(PHASE + taps - 1):
            if j < taps:
                held[j] = taps_ref[8 - k, taps - 1 - j] if reverse else taps_ref[k, j]
            value = inputs_ref[k, j]
            for m in range(max(0, j - PHASE + 1), min(taps, j + 1)):
                term = value * held[m]
                sums[j - m] = term if sums[j - m] is None else sums[j - m] + term
        for i in range(PHASE):
            sums_ref[k, i] = sums[i]

    a, b, c = sums_ref[0] + sums_ref[1], sums_ref[3] + sums_ref[4], sums_ref[6] + sums_ref[7]
    d, e, f = sums_ref[1] + sums_ref[2], sums_ref[4] + sums_ref[5], sums_ref[7] + sums_ref[8]
    rows = jnp.stack([a + b, b + c, d + e, e + f], axis=1)
    return rows.reshape(SEGMENT, 8, LANES)


FILTER_SCRATCH = [
    pltpu.VMEM((9, LENGTH // 4, 8, LANES), F32),
    pltpu.VMEM((REACH, 4, 8, LANES), F32),
    pltpu.VMEM((9, REACH, 8, LANES), F32),
    pltpu.VMEM((9, PHASE, 8, LANES), F32),
    pltpu.VMEM((LANES, 512), F32),
]


def steps_body(
    total, place_ref, begin_ref, step_ref, mine_ref, inner_ref, outer_ref, before_ref, first_ref,
    second_ref, after_ref, temporal_ref, threshold_ref, out_ref, taps_ref, spread_ref, inputs_ref,
    sums_ref, wide_ref, rim_ref, point_ref, cross_ref, mix_ref,
):
    place, begin = place_ref[0], begin_ref[0]
    rate = step_ref[0]
    half = CHUNK // 2
    spread_taps(temporal_ref, taps_ref)

    edge = outer_ref[:, half:]
    before = jnp.where(place == 0, edge, before_ref[...])
    after = jnp.where(place == CHUNKS - 1, edge, after_ref[...])
    second = second_ref[...]
    wide_ref[:ATOMS] = jnp.concatenate([before[:, 128:], first_ref[...], second[:, :128]], axis=1)
    wide_ref[ATOMS:] = jnp.concatenate([second[:, 64:], after, after[:, :64]], axis=1)
    to_segments(wide_ref, point_ref)
    rim = before[:, :128]
    rim_ref[...] = jnp.concatenate([rim, rim], axis=0).T

    def outside(start):
        count = min(SEGMENT, SEGMENT + start)
        rows = rim_ref[max(start, 0) : max(start, 0) + count].reshape(count, 1, LANES)
        rows = jnp.broadcast_to(rows, (count, 8, LANES))
        if count < SEGMENT:
            rows = jnp.concatenate([jnp.zeros((SEGMENT - count, 8, LANES), F32), rows], axis=0)
        return rows

    mine = mine_ref[:ATOMS]
    first = place % 2 == 0
    left = jnp.where(first, outer_ref[:, 128:half], inner_ref[:, 128:])
    right = jnp.where(first, inner_ref[...], outer_ref[:, :half])
    wide_ref[:ATOMS] = jnp.concatenate([left, mine[:, :384]], axis=1)
    wide_ref[ATOMS:] = jnp.concatenate([mine[:, 320:], right, right[:, :64]], axis=1)
    to_segments(wide_ref, cross_ref)

    gram_rows = mine_ref[ATOMS:]
    gram = jnp.concatenate([gram_rows[:, ATOMS * i : ATOMS * (i + 1)] for i in range(8)], axis=0)
    mix_ref[...] = jnp.zeros_like(mix_ref)
    mix_ref[:ATOMS, :ATOMS] = gram
    mix_ref[ATOMS:, ATOMS:] = gram

    shape = (SEGMENT, 8, LANES)
    sample = lax.broadcasted_iota(jnp.int32, shape, 0) + (
        (lane_half() * 8 + sublane()) * SEGMENT + (begin - LENGTH)
    )
    shrink = threshold_ref[...]
    shrink = jnp.concatenate([shrink, shrink], axis=1).reshape(1, 1, LANES)

    def projected(point, samples_before=None):
        spread_earlier(point, spread_ref, samples_before)
        short_inputs(spread_ref, inputs_ref, 1)
        rebuilt = filter_rows(inputs_ref, taps_ref, sums_ref, True).reshape(SIDE, LANES)
        mixed = jnp.dot(rebuilt, mix_ref[...], precision=HIGHEST, preferred_element_type=F32)
        rows = (mixed - cross_ref[...]).reshape(shape)
        return jnp.where(sample < total, rows, 0.0)

    def stepped(point, rows):
        spread_later(rows, spread_ref)
        short_inputs(spread_ref, inputs_ref, 0)
        gradient = filter_rows(inputs_ref, taps_ref, sums_ref, False)
        return jnp.maximum(point - rate * (gradient + shrink), 0.0)

    inertia = 1.0
    inertia_next = (1.0 + (1.0 + 4.0 * inertia * inertia) ** 0.5) / 2.0
    momentum = (inertia - 1.0) / inertia_next
    previous = point_ref[...].reshape(shape)
    update = stepped(previous, projected(previous, outside))
    point = update + momentum * (update - previous)
    point = jnp.where(sample >= 0, point, 0.0)
    update = stepped(point, projected(point))

    cross_ref[...] = update.reshape(SIDE, LANES)
    rows = [cross_ref[pl.ds(s, SEGMENT, stride=8)] for s in range(8)]
    rows.append(jnp.zeros((512 - SIDE, LANES), F32))
    columns = jnp.concatenate(rows, axis=0).T
    out_ref[...] = jnp.concatenate([columns[:ATOMS, 128:SIDE], columns[ATOMS:, :192]], axis=1)


def steps(total, place, begin, step_size, mine, inner, outer, activations, temporal, threshold):
    width = activations.shape[1]
    half = CHUNK // 2
    last = width // half - 1

    def body(*refs):
        steps_body(total, *refs)

    def whole(array):
        return pl.BlockSpec(array.shape, lambda i, place: (0, 0))

    def piece(index):
        return pl.BlockSpec((ATOMS, half), lambda i, place: (0, index(2 * place[0])))

    return pl.pallas_call(
        body,
        grid_spec=pltpu.PrefetchScalarGridSpec(
            num_scalar_prefetch=1,
            grid=(1,),
            in_specs=[SMEM, SMEM, whole(mine), whole(inner), whole(outer)]
            + [
                piece(lambda k: jnp.maximum(k - 1, 0)),
                piece(lambda k: k),
                piece(lambda k: k + 1),
                piece(lambda k: jnp.minimum(k + 2, last)),
            ]
            + [whole(temporal), whole(threshold)],
            out_specs=pl.BlockSpec((ATOMS, CHUNK), lambda i, place: (0, 0)),
            scratch_shapes=FILTER_SCRATCH
            + [
                pltpu.VMEM((LENGTH, LANES), F32),
                pltpu.VMEM((SIDE, LANES), F32),
                pltpu.VMEM((SIDE, LANES), F32),
                pltpu.VMEM((LANES, LANES), F32),
            ],
        ),
        out_shape=jax.ShapeDtypeStruct((ATOMS, CHUNK), F32),
        compiler_params=params(12),
        cost_estimate=cost(8 * SIDE * LANES * LENGTH, 2**20),
    )(
        place, begin, step_size, mine, inner, outer, activations, activations, activations,
        activations, temporal, threshold,
    )


def place_copies(half, chunks_ref, out_ref, sems):
    copies = []
    for i in range(QUARTER):
        column = pl.multiple_of((2 * i + half) * CHUNK, CHUNK)
        copies.append(
            pltpu.make_async_copy(chunks_ref.at[i], out_ref.at[:, pl.ds(column, CHUNK)], sems.at[i])
        )
    for copy in copies:
        copy.start()
    for copy in copies:
        copy.wait()


def place_mine_body(half_ref, chunks_ref, out_ref, sems):
    place_copies(half_ref[0], chunks_ref, out_ref, sems)


def place_other_body(half_ref, chunks_ref, begun_ref, out_ref, sems):
    place_copies(1 - half_ref[0], chunks_ref, out_ref, sems)


def place_half(half, chunks, begun=None):
    out_shape = jax.ShapeDtypeStruct((ATOMS, CHUNKS * CHUNK), F32)
    first = begun is None
    return pl.pallas_call(
        place_mine_body if first else place_other_body,
        in_specs=[SMEM, ANY] + ([] if first else [ANY]),
        out_specs=ANY,
        out_shape=out_shape,
        scratch_shapes=[pltpu.SemaphoreType.DMA((QUARTER,))],
        input_output_aliases={} if first else {2: 0},
        compiler_params=params(4),
        cost_estimate=cost(0, 2**20),
    )(half, chunks, *([] if first else [begun]))


def solution(mesh):
    blocks = mesh.shape["tm"]
    split = Mesh(mesh.devices.reshape(2, 4, 2, blocks), ("zh", "y", "c", "tm"))
    swap = [(0, 1), (1, 0)]
    line = ("zh", "y", "c", "tm")

    def device(zh, q, tm):
        return (zh * CHUNKS + q) * blocks + tm

    inside, rims = [], []
    for zh in range(2):
        for tm in range(blocks):
            for q in range(1, CHUNKS - 1, 2):
                inside.append((device(zh, q, tm), device(zh, q + 1, tm)))
            if tm + 1 < blocks:
                near = 1 - zh if (tm + 1) % RUN == 0 else zh
                rims.append((device(zh, CHUNKS - 1, tm), device(near, 0, tm + 1)))
    rims = rims + [(b, a) for a, b in rims]
    outside = rims + inside + [(b, a) for a, b in inside]

    def per_device(signal, spatial, temporal, activations, threshold, step_size):
        half = lax.axis_index("c").astype(jnp.int32)
        place = lax.axis_index("y").astype(jnp.int32) * 2 + half
        time_block = lax.axis_index("tm").astype(jnp.int32)
        width = activations.shape[1]
        spatial = spatial.T

        away = project_half((1 - half)[None], spatial, signal)
        arrived = lax.ppermute(away, "c", swap)
        kept = project_half(half[None], spatial, signal)
        summed = kept + arrived
        pieces = lax.all_to_all(summed, "y", 0, 0, tiled=True)
        group_sum = jnp.sum(pieces, axis=0)
        mine = group_sum + lax.ppermute(group_sum, "zh", swap)

        rim = CHUNK // 2
        first = half == 0
        edge = jnp.where(first, activations[:, :rim], activations[:, width - rim :])
        start, end = mine[:ATOMS, :rim], mine[:ATOMS, CHUNK - rim :]
        outer = jnp.concatenate([jnp.where(first, start, end), edge], axis=1)
        outer = lax.ppermute(outer, line, outside)
        inner = lax.ppermute(jnp.where(first, end, start), "c", swap)
        begin = time_block * width + place * CHUNK
        update = steps(
            blocks * width, place[None], begin[None], step_size, mine, inner, outer, activations,
            temporal, threshold[None, :],
        )

        gathered = lax.all_gather(update, "y", axis=0)
        other = lax.ppermute(gathered, "c", swap)
        return place_half(half[None], other, place_half(half[None], gathered))

    chan = ("zh", "y", "c")
    in_specs = (P(chan, "tm"), P(chan, None), P(), P(None, "tm"), P(), P())
    return jax.shard_map(
        per_device, mesh=split, in_specs=in_specs, out_specs=P(None, "tm"), check_vma=False
    )
```

```python
import jax
import jax.numpy as jnp
from jax import lax
from jax.experimental import pallas as pl
from jax.experimental.pallas import tpu as pltpu
from jax.sharding import Mesh, PartitionSpec as P

ATOMS = 64
LENGTH = 128
CHUNK = 512
CHUNKS = 8
QUARTER = 4
LANES = 2 * ATOMS
ROWS = ATOMS + 8
SEGMENT = 56
SIDE = 8 * SEGMENT
WINDOW = 2 * SIDE
PHASE = SEGMENT // 4
REACH = 46
HIGHEST = lax.Precision.HIGHEST
F32 = jnp.float32
VMEM = pl.BlockSpec(memory_space=pltpu.VMEM)
SMEM = pl.BlockSpec(memory_space=pltpu.SMEM)
ANY = pl.BlockSpec(memory_space=pl.ANY)
HBM = pl.BlockSpec(memory_space=pltpu.HBM)
RUN = 8


def cost(flops, bytes_accessed):
    return pl.CostEstimate(flops=flops, bytes_accessed=bytes_accessed, transcendentals=0)


def params(mebibytes):
    return pltpu.CompilerParams(vmem_limit_bytes=mebibytes * 2**20)


def project_chunk(parts, signal):
    product = jnp.dot(parts, signal, preferred_element_type=F32)
    return product[:ATOMS] + product[ATOMS:]


def gram_rows(parts):
    gram = lax.dot_general(parts, parts, (((1,), (1,)), ((), ())), preferred_element_type=F32)
    gram = gram[:ATOMS] + gram[ATOMS:]
    gram = gram[:, :ATOMS] + gram[:, ATOMS:]
    return jnp.concatenate([gram[8 * i : 8 * i + 8] for i in range(8)], axis=1)


def project_away_body(half_ref, parts_ref, signal_ref, out_ref, kept_ref, block_ref, sems):
    def fetch(i, half, target, sem):
        column = pl.multiple_of((2 * i + half) * CHUNK, CHUNK)
        return pltpu.make_async_copy(signal_ref.at[:, pl.ds(column, CHUNK)], target.at[i], sem)

    half = half_ref[0]
    away = [fetch(i, 1 - half, block_ref, sems.at[i]) for i in range(QUARTER)]
    kept = [fetch(i, half, kept_ref, sems.at[QUARTER + i]) for i in range(QUARTER)]
    for copy in away + kept:
        copy.start()
    parts = parts_ref[...]
    rows = gram_rows(parts)
    for i in range(QUARTER):
        out_ref[i, ATOMS:] = rows
    for i in range(QUARTER):
        away[i].wait()
        out_ref[i, :ATOMS] = project_chunk(parts, block_ref[i])
    for copy in kept:
        copy.wait()


def project_away(half, parts, signal):
    channels, width = signal.shape
    blocks = (QUARTER, channels, CHUNK)
    return pl.pallas_call(
        project_away_body,
        in_specs=[SMEM, VMEM, HBM],
        out_specs=[VMEM, VMEM],
        out_shape=[
            jax.ShapeDtypeStruct((QUARTER, ROWS, CHUNK), F32),
            jax.ShapeDtypeStruct(blocks, jnp.bfloat16),
        ],
        scratch_shapes=[
            pltpu.VMEM(blocks, jnp.bfloat16),
            pltpu.SemaphoreType.DMA((2 * QUARTER,)),
        ],
        compiler_params=params(8),
        cost_estimate=cost(channels * LANES * width, 2 * channels * width),
    )(half, parts, signal)


def project_kept_body(parts_ref, signal_ref, out_ref):
    parts = parts_ref[...]
    rows = gram_rows(parts)
    for i in range(QUARTER):
        out_ref[i, ATOMS:] = rows
        out_ref[i, :ATOMS] = project_chunk(parts, signal_ref[i])


def project_kept(parts, signal):
    count, channels, width = signal.shape
    return pl.pallas_call(
        project_kept_body,
        in_specs=[VMEM, VMEM],
        out_specs=VMEM,
        out_shape=jax.ShapeDtypeStruct((QUARTER, ROWS, CHUNK), F32),
        compiler_params=params(8),
        cost_estimate=cost(2 * channels * LANES * count * width, channels * count * width),
    )(parts, signal)


def to_segments(wide_ref, out_ref):
    columns = wide_ref[...].T
    for s in range(8):
        out_ref[pl.ds(s, SEGMENT, stride=8)] = columns[s * SEGMENT : (s + 1) * SEGMENT]


def spread_taps(temporal_ref, taps_ref):
    temporal = temporal_ref[...]
    columns = jnp.concatenate([temporal, temporal], axis=0).T
    for i in range(LENGTH // 4):
        c0, c1, c2, c3 = (
            jnp.broadcast_to(columns[4 * i + p : 4 * i + p + 1], (8, LANES)) for p in range(4)
        )
        even, odd = c0 + c1, c2 + c3
        for k, tap in enumerate((c0, c0 + c2, c2, even, even + odd, odd, c1, c1 + c3, c3)):
            taps_ref[k, i] = tap


def lane_half():
    return lax.broadcasted_iota(jnp.int32, (1, 8, LANES), 2) // ATOMS


def sublane():
    return lax.broadcasted_iota(jnp.int32, (1, 8, LANES), 1)


def later_segment(rows):
    up = pltpu.roll(rows, 7, 1)
    return jnp.where(sublane() == 7, pltpu.roll(up, ATOMS, 2), up)


def earlier_segment(rows):
    down = pltpu.roll(rows, 1, 1)
    return jnp.where(sublane() == 0, pltpu.roll(down, ATOMS, 2), down)


def spread_later(rows, spread_ref):
    for first in range(0, 4 * REACH, SEGMENT):
        count = min(SEGMENT, 4 * REACH - first)
        spread_ref[first // 4 : (first + count) // 4] = rows[:count].reshape(count // 4, 4, 8, LANES)
        if count == SEGMENT:
            rows = later_segment(rows)


def spread_earlier(rows, spread_ref, outside=None):
    start = LENGTH
    while True:
        skip = max(0, -start)
        kept = rows[skip:]
        first, count = start + skip, SEGMENT - skip
        spread_ref[first // 4 : (first + count) // 4] = kept.reshape(count // 4, 4, 8, LANES)
        if start <= 0:
            return
        rows = earlier_segment(rows)
        start -= SEGMENT
        if outside is not None:
            rim = outside(start)
            rows = jnp.where((sublane() == 0) & (lane_half() == 0), rim, rows)


def short_inputs(spread_ref, inputs_ref, offset):
    count = REACH - 1

    def x(p):
        p = p + offset
        return spread_ref[p // 4 : p // 4 + count, p % 4]

    x0, x1, x2, x3, x4, x5 = (x(p) for p in range(6))
    inputs_ref[0, :count] = (x0 - x1) - (x2 - x3)
    inputs_ref[1, :count] = x2 - x3
    inputs_ref[2, :count] = (x4 - x5) - (x2 - x3)
    inputs_ref[3, :count] = x1 - x3
    inputs_ref[4, :count] = x3
    inputs_ref[5, :count] = x5 - x3
    inputs_ref[6, :count] = (x2 - x1) - (x4 - x3)
    inputs_ref[7, :count] = x4 - x3
    last = min(count, REACH - (6 + offset) // 4)
    x6 = spread_ref[(6 + offset) // 4 : (6 + offset) // 4 + last, (6 + offset) % 4]
    inputs_ref[8, :last] = (x6 - x5[:last]) - (x4[:last] - x3[:last])


def filter_rows(inputs_ref, taps_ref, sums_ref, reverse):
    taps = LENGTH // 4

    @pl.loop(0, 9)
    def _(k):
        sums = [None] * PHASE
        held = {}
        for j in range(PHASE + taps - 1):
            if j < taps:
                held[j] = taps_ref[8 - k, taps - 1 - j] if reverse else taps_ref[k, j]
            value = inputs_ref[k, j]
            for m in range(max(0, j - PHASE + 1), min(taps, j + 1)):
                term = value * held[m]
                sums[j - m] = term if sums[j - m] is None else sums[j - m] + term
        for i in range(PHASE):
            sums_ref[k, i] = sums[i]

    a, b, c = sums_ref[0] + sums_ref[1], sums_ref[3] + sums_ref[4], sums_ref[6] + sums_ref[7]
    d, e, f = sums_ref[1] + sums_ref[2], sums_ref[4] + sums_ref[5], sums_ref[7] + sums_ref[8]
    rows = jnp.stack([a + b, b + c, d + e, e + f], axis=1)
    return rows.reshape(SEGMENT, 8, LANES)


FILTER_SCRATCH = [
    pltpu.VMEM((9, LENGTH // 4, 8, LANES), F32),
    pltpu.VMEM((REACH, 4, 8, LANES), F32),
    pltpu.VMEM((9, REACH, 8, LANES), F32),
    pltpu.VMEM((9, PHASE, 8, LANES), F32),
    pltpu.VMEM((LANES, 512), F32),
]


def rebuild_body(
    place_ref, temporal_ref, before_ref, first_ref, second_ref, after_ref, edge_ref,
    rebuilt_ref, point_ref, taps_ref, spread_ref, inputs_ref, sums_ref, wide_ref, rim_ref,
):
    place = place_ref[0]
    spread_taps(temporal_ref, taps_ref)
    edge = edge_ref[...]
    before = jnp.where(place == 0, edge, before_ref[...])
    after = jnp.where(place == CHUNKS - 1, edge, after_ref[...])
    second = second_ref[...]
    wide_ref[:ATOMS] = jnp.concatenate([before[:, 128:], first_ref[...], second[:, :128]], axis=1)
    wide_ref[ATOMS:] = jnp.concatenate([second[:, 64:], after, after[:, :64]], axis=1)
    to_segments(wide_ref, point_ref)
    rim = before[:, :128]
    rim_ref[...] = jnp.concatenate([rim, rim], axis=0).T

    def outside(start):
        count = min(SEGMENT, SEGMENT + start)
        rows = rim_ref[max(start, 0) : max(start, 0) + count].reshape(count, 1, LANES)
        rows = jnp.broadcast_to(rows, (count, 8, LANES))
        if count < SEGMENT:
            rows = jnp.concatenate([jnp.zeros((SEGMENT - count, 8, LANES), F32), rows], axis=0)
        return rows

    rows = point_ref[...].reshape(SEGMENT, 8, LANES)
    spread_earlier(rows, spread_ref, outside)
    short_inputs(spread_ref, inputs_ref, 1)
    rebuilt_ref[...] = filter_rows(inputs_ref, taps_ref, sums_ref, True).reshape(SIDE, LANES)


def rebuild(place, temporal, activations, edge):
    atoms, width = activations.shape
    half = CHUNK // 2
    last = width // half - 1
    block = (atoms, half)
    return pl.pallas_call(
        rebuild_body,
        grid_spec=pltpu.PrefetchScalarGridSpec(
            num_scalar_prefetch=1,
            grid=(1,),
            in_specs=[
                pl.BlockSpec((ATOMS, LENGTH), lambda i, place: (0, 0)),
                pl.BlockSpec(block, lambda i, place: (0, jnp.maximum(2 * place[0] - 1, 0))),
                pl.BlockSpec(block, lambda i, place: (0, 2 * place[0])),
                pl.BlockSpec(block, lambda i, place: (0, 2 * place[0] + 1)),
                pl.BlockSpec(block, lambda i, place: (0, jnp.minimum(2 * place[0] + 2, last))),
                pl.BlockSpec(block, lambda i, place: (0, 0)),
            ],
            out_specs=[pl.BlockSpec((SIDE, LANES), lambda i, place: (0, 0))] * 2,
            scratch_shapes=FILTER_SCRATCH + [pltpu.VMEM((LENGTH, LANES), F32)],
        ),
        out_shape=[jax.ShapeDtypeStruct((SIDE, LANES), F32)] * 2,
        compiler_params=params(12),
        cost_estimate=cost(2 * SIDE * LANES * LENGTH, 2**20),
    )(place, temporal, activations, activations, activations, activations, edge)


def steps_body(
    total, begin_ref, half_ref, step_ref, mine_ref, inner_ref, outer_ref, rebuilt_ref, point_ref,
    temporal_ref, threshold_ref, out_ref, taps_ref, spread_ref, inputs_ref, sums_ref, wide_ref,
    cross_ref, mix_ref,
):
    begin = begin_ref[0]
    rate = step_ref[0]
    spread_taps(temporal_ref, taps_ref)
    gram_rows = mine_ref[ATOMS:]
    gram = jnp.concatenate([gram_rows[:, ATOMS * i : ATOMS * (i + 1)] for i in range(8)], axis=0)
    mix_ref[...] = jnp.zeros_like(mix_ref)
    mix_ref[:ATOMS, :ATOMS] = gram
    mix_ref[ATOMS:, ATOMS:] = gram
    mine = mine_ref[:ATOMS]
    first = half_ref[0] == 0
    left = jnp.where(first, outer_ref[:, 128:], inner_ref[:, 128:])
    right = jnp.where(first, inner_ref[...], outer_ref[...])
    wide_ref[:ATOMS] = jnp.concatenate([left, mine[:, :384]], axis=1)
    wide_ref[ATOMS:] = jnp.concatenate([mine[:, 320:], right, right[:, :64]], axis=1)
    to_segments(wide_ref, cross_ref)

    shape = (SEGMENT, 8, LANES)
    sample = lax.broadcasted_iota(jnp.int32, shape, 0) + (
        (lane_half() * 8 + sublane()) * SEGMENT + (begin - LENGTH)
    )
    shrink = threshold_ref[...]
    shrink = jnp.concatenate([shrink, shrink], axis=1).reshape(1, 1, LANES)

    def projected(rebuilt):
        mixed = jnp.dot(rebuilt, mix_ref[...], precision=HIGHEST, preferred_element_type=F32)
        rows = (mixed - cross_ref[...]).reshape(shape)
        return jnp.where(sample < total, rows, 0.0)

    def stepped(point, rows):
        spread_later(rows, spread_ref)
        short_inputs(spread_ref, inputs_ref, 0)
        gradient = filter_rows(inputs_ref, taps_ref, sums_ref, False)
        return jnp.maximum(point - rate * (gradient + shrink), 0.0)

    inertia = 1.0
    inertia_next = (1.0 + (1.0 + 4.0 * inertia * inertia) ** 0.5) / 2.0
    momentum = (inertia - 1.0) / inertia_next
    previous = point_ref[...].reshape(shape)
    update = stepped(previous, projected(rebuilt_ref[...]))
    point = update + momentum * (update - previous)
    point = jnp.where(sample >= 0, point, 0.0)

    spread_earlier(point, spread_ref)
    short_inputs(spread_ref, inputs_ref, 1)
    rebuilt = filter_rows(inputs_ref, taps_ref, sums_ref, True)
    update = stepped(point, projected(rebuilt.reshape(SIDE, LANES)))

    cross_ref[...] = update.reshape(SIDE, LANES)
    rows = [cross_ref[pl.ds(s, SEGMENT, stride=8)] for s in range(8)]
    rows.append(jnp.zeros((512 - SIDE, LANES), F32))
    columns = jnp.concatenate(rows, axis=0).T
    out_ref[...] = jnp.concatenate([columns[:ATOMS, 128:SIDE], columns[ATOMS:, :192]], axis=1)


def steps(total, begin, half, step_size, mine, inner, outer, rebuilt, point, temporal, threshold):
    def body(*refs):
        steps_body(total, *refs)

    return pl.pallas_call(
        body,
        in_specs=[SMEM] * 3 + [VMEM] * 7,
        out_specs=VMEM,
        out_shape=jax.ShapeDtypeStruct((ATOMS, CHUNK), F32),
        scratch_shapes=FILTER_SCRATCH
        + [pltpu.VMEM((SIDE, LANES), F32), pltpu.VMEM((LANES, LANES), F32)],
        compiler_params=params(12),
        cost_estimate=cost(6 * SIDE * LANES * LENGTH, 2**20),
    )(begin, half, step_size, mine, inner, outer, rebuilt, point, temporal, threshold)


def place_copies(half, chunks_ref, out_ref, sems):
    copies = []
    for i in range(QUARTER):
        column = pl.multiple_of((2 * i + half) * CHUNK, CHUNK)
        copies.append(
            pltpu.make_async_copy(chunks_ref.at[i], out_ref.at[:, pl.ds(column, CHUNK)], sems.at[i])
        )
    for copy in copies:
        copy.start()
    for copy in copies:
        copy.wait()


def place_mine_body(half_ref, chunks_ref, out_ref, sems):
    place_copies(half_ref[0], chunks_ref, out_ref, sems)


def place_other_body(half_ref, chunks_ref, begun_ref, out_ref, sems):
    place_copies(1 - half_ref[0], chunks_ref, out_ref, sems)


def place_half(half, chunks, begun=None):
    out_shape = jax.ShapeDtypeStruct((ATOMS, CHUNKS * CHUNK), F32)
    first = begun is None
    return pl.pallas_call(
        place_mine_body if first else place_other_body,
        in_specs=[SMEM, ANY] + ([] if first else [ANY]),
        out_specs=ANY,
        out_shape=out_shape,
        scratch_shapes=[pltpu.SemaphoreType.DMA((QUARTER,))],
        input_output_aliases={} if first else {2: 0},
        compiler_params=params(4),
        cost_estimate=cost(0, 2**20),
    )(half, chunks, *([] if first else [begun]))


def solution(mesh):
    blocks = mesh.shape["tm"]
    split = Mesh(mesh.devices.reshape(2, 4, 2, blocks), ("zh", "y", "c", "tm"))
    swap = [(0, 1), (1, 0)]
    line = ("zh", "y", "c", "tm")

    def device(zh, q, tm):
        return (zh * CHUNKS + q) * blocks + tm

    inside, rims = [], []
    for zh in range(2):
        for tm in range(blocks):
            for q in range(1, CHUNKS - 1, 2):
                inside.append((device(zh, q, tm), device(zh, q + 1, tm)))
            if tm + 1 < blocks:
                near = 1 - zh if (tm + 1) % RUN == 0 else zh
                rims.append((device(zh, CHUNKS - 1, tm), device(near, 0, tm + 1)))
    rims = rims + [(b, a) for a, b in rims]
    outside = rims + inside + [(b, a) for a, b in inside]

    def per_device(signal, spatial, temporal, activations, threshold, step_size):
        half = lax.axis_index("c").astype(jnp.int32)
        place = lax.axis_index("y").astype(jnp.int32) * 2 + half
        time_block = lax.axis_index("tm").astype(jnp.int32)
        width = activations.shape[1]
        spatial = spatial.T
        high = lax.reduce_precision(spatial, 8, 7)
        parts = jnp.concatenate([high, spatial - high], axis=0).astype(jnp.bfloat16)

        away, kept_signal = project_away(half[None], parts, signal)
        arrived = lax.ppermute(away, "c", swap)
        kept = project_kept(parts, kept_signal)
        pieces = lax.all_to_all(kept + arrived, "y", 0, 0, tiled=True)
        group_sum = jnp.sum(pieces, axis=0)

        rim = CHUNK // 2
        first = half == 0
        activations, group_sum = lax.optimization_barrier((activations, group_sum))
        edge = jnp.where(first, activations[:, :rim], activations[:, width - rim :])
        other_sum = lax.ppermute(group_sum, "zh", swap)
        edge = lax.ppermute(edge, line, rims)
        rebuilt, point = rebuild(place[None], temporal, activations, edge)
        rebuilt, point, other_sum = lax.optimization_barrier((rebuilt, point, other_sum))
        mine = group_sum + other_sum

        start, end = mine[:ATOMS, :rim], mine[:ATOMS, CHUNK - rim :]
        outer = lax.ppermute(jnp.where(first, start, end), line, outside)
        inner = lax.ppermute(jnp.where(first, end, start), "c", swap)
        begin = time_block * width + place * CHUNK
        update = steps(
            blocks * width, begin[None], half[None], step_size, mine, inner, outer, rebuilt, point,
            temporal, threshold[None, :],
        )

        gathered = lax.all_gather(update, "y", axis=0)
        other = lax.ppermute(gathered, "c", swap)
        return place_half(half[None], other, place_half(half[None], gathered))

    chan = ("zh", "y", "c")
    in_specs = (P(chan, "tm"), P(chan, None), P(), P(None, "tm"), P(), P())
    return jax.shard_map(
        per_device, mesh=split, in_specs=in_specs, out_specs=P(None, "tm"), check_vma=False
    )
```

```python
import jax
import jax.numpy as jnp
from jax import lax
from jax.experimental import pallas as pl
from jax.experimental.pallas import tpu as pltpu
from jax.sharding import Mesh, PartitionSpec as P

ATOMS = 64
LENGTH = 128
CHUNK = 512
CHUNKS = 8
QUARTER = 4
LANES = 2 * ATOMS
ROWS = ATOMS + 8
SEGMENT = 56
SIDE = 8 * SEGMENT
WINDOW = 2 * SIDE
PHASE = SEGMENT // 4
REACH = 46
HIGHEST = lax.Precision.HIGHEST
F32 = jnp.float32
VMEM = pl.BlockSpec(memory_space=pltpu.VMEM)
SMEM = pl.BlockSpec(memory_space=pltpu.SMEM)
ANY = pl.BlockSpec(memory_space=pl.ANY)
RUN = 8


def cost(flops, bytes_accessed):
    return pl.CostEstimate(flops=flops, bytes_accessed=bytes_accessed, transcendentals=0)


def params(mebibytes):
    return pltpu.CompilerParams(vmem_limit_bytes=mebibytes * 2**20)


def project_chunk(parts, signal):
    product = jnp.dot(parts, signal, preferred_element_type=F32)
    return product[:ATOMS] + product[ATOMS:]


def gram_rows(parts):
    gram = lax.dot_general(parts, parts, (((1,), (1,)), ((), ())), preferred_element_type=F32)
    gram = gram[:ATOMS] + gram[ATOMS:]
    gram = gram[:, :ATOMS] + gram[:, ATOMS:]
    return jnp.concatenate([gram[8 * i : 8 * i + 8] for i in range(8)], axis=1)


def project_body(half_ref, parts_ref, signal_ref, away_ref, kept_ref):
    half = half_ref[0]
    parts = parts_ref[...]
    rows = gram_rows(parts)
    for out_ref, which in ((away_ref, 1 - half), (kept_ref, half)):
        for i in range(QUARTER):
            column = pl.multiple_of((2 * i + which) * CHUNK, CHUNK)
            out_ref[i, :ATOMS] = project_chunk(parts, signal_ref[:, pl.ds(column, CHUNK)])
            out_ref[i, ATOMS:] = rows


def project(half, parts, signal):
    channels, width = signal.shape
    return pl.pallas_call(
        project_body,
        in_specs=[SMEM, VMEM, VMEM],
        out_specs=[VMEM, VMEM],
        out_shape=[jax.ShapeDtypeStruct((QUARTER, ROWS, CHUNK), F32)] * 2,
        compiler_params=params(8),
        cost_estimate=cost(2 * channels * LANES * width, 2 * channels * width),
    )(half, parts, signal)


def to_segments(wide_ref, out_ref):
    columns = wide_ref[...].T
    for s in range(8):
        out_ref[pl.ds(s, SEGMENT, stride=8)] = columns[s * SEGMENT : (s + 1) * SEGMENT]


def spread_taps(temporal_ref, taps_ref):
    temporal = temporal_ref[...]
    columns = jnp.concatenate([temporal, temporal], axis=0).T
    for i in range(LENGTH // 4):
        c0, c1, c2, c3 = (
            jnp.broadcast_to(columns[4 * i + p : 4 * i + p + 1], (8, LANES)) for p in range(4)
        )
        even, odd = c0 + c1, c2 + c3
        for k, tap in enumerate((c0, c0 + c2, c2, even, even + odd, odd, c1, c1 + c3, c3)):
            taps_ref[k, i] = tap


def lane_half():
    return lax.broadcasted_iota(jnp.int32, (1, 8, LANES), 2) // ATOMS


def sublane():
    return lax.broadcasted_iota(jnp.int32, (1, 8, LANES), 1)


def later_segment(rows):
    up = pltpu.roll(rows, 7, 1)
    return jnp.where(sublane() == 7, pltpu.roll(up, ATOMS, 2), up)


def earlier_segment(rows):
    down = pltpu.roll(rows, 1, 1)
    return jnp.where(sublane() == 0, pltpu.roll(down, ATOMS, 2), down)


def spread_later(rows, spread_ref):
    for first in range(0, 4 * REACH, SEGMENT):
        count = min(SEGMENT, 4 * REACH - first)
        spread_ref[first // 4 : (first + count) // 4] = rows[:count].reshape(count // 4, 4, 8, LANES)
        if count == SEGMENT:
            rows = later_segment(rows)


def spread_earlier(rows, spread_ref, outside=None):
    start = LENGTH
    while True:
        skip = max(0, -start)
        kept = rows[skip:]
        first, count = start + skip, SEGMENT - skip
        spread_ref[first // 4 : (first + count) // 4] = kept.reshape(count // 4, 4, 8, LANES)
        if start <= 0:
            return
        rows = earlier_segment(rows)
        start -= SEGMENT
        if outside is not None:
            rim = outside(start)
            rows = jnp.where((sublane() == 0) & (lane_half() == 0), rim, rows)


def short_inputs(spread_ref, inputs_ref, offset):
    count = REACH - 1

    def x(p):
        p = p + offset
        return spread_ref[p // 4 : p // 4 + count, p % 4]

    x0, x1, x2, x3, x4, x5 = (x(p) for p in range(6))
    inputs_ref[0, :count] = (x0 - x1) - (x2 - x3)
    inputs_ref[1, :count] = x2 - x3
    inputs_ref[2, :count] = (x4 - x5) - (x2 - x3)
    inputs_ref[3, :count] = x1 - x3
    inputs_ref[4, :count] = x3
    inputs_ref[5, :count] = x5 - x3
    inputs_ref[6, :count] = (x2 - x1) - (x4 - x3)
    inputs_ref[7, :count] = x4 - x3
    last = min(count, REACH - (6 + offset) // 4)
    x6 = spread_ref[(6 + offset) // 4 : (6 + offset) // 4 + last, (6 + offset) % 4]
    inputs_ref[8, :last] = (x6 - x5[:last]) - (x4[:last] - x3[:last])


def filter_rows(inputs_ref, taps_ref, sums_ref, reverse):
    taps = LENGTH // 4

    @pl.loop(0, 9)
    def _(k):
        sums = [None] * PHASE
        held = {}
        for j in range(PHASE + taps - 1):
            if j < taps:
                held[j] = taps_ref[8 - k, taps - 1 - j] if reverse else taps_ref[k, j]
            value = inputs_ref[k, j]
            for m in range(max(0, j - PHASE + 1), min(taps, j + 1)):
                term = value * held[m]
                sums[j - m] = term if sums[j - m] is None else sums[j - m] + term
        for i in range(PHASE):
            sums_ref[k, i] = sums[i]

    a, b, c = sums_ref[0] + sums_ref[1], sums_ref[3] + sums_ref[4], sums_ref[6] + sums_ref[7]
    d, e, f = sums_ref[1] + sums_ref[2], sums_ref[4] + sums_ref[5], sums_ref[7] + sums_ref[8]
    rows = jnp.stack([a + b, b + c, d + e, e + f], axis=1)
    return rows.reshape(SEGMENT, 8, LANES)


FILTER_SCRATCH = [
    pltpu.VMEM((9, LENGTH // 4, 8, LANES), F32),
    pltpu.VMEM((REACH, 4, 8, LANES), F32),
    pltpu.VMEM((9, REACH, 8, LANES), F32),
    pltpu.VMEM((9, PHASE, 8, LANES), F32),
    pltpu.VMEM((LANES, 512), F32),
]


def rebuild_body(
    place_ref, temporal_ref, before_ref, first_ref, second_ref, after_ref, edge_ref,
    rebuilt_ref, point_ref, taps_ref, spread_ref, inputs_ref, sums_ref, wide_ref, rim_ref,
):
    place = place_ref[0]
    spread_taps(temporal_ref, taps_ref)
    edge = edge_ref[...]
    before = jnp.where(place == 0, edge, before_ref[...])
    after = jnp.where(place == CHUNKS - 1, edge, after_ref[...])
    second = second_ref[...]
    wide_ref[:ATOMS] = jnp.concatenate([before[:, 128:], first_ref[...], second[:, :128]], axis=1)
    wide_ref[ATOMS:] = jnp.concatenate([second[:, 64:], after, after[:, :64]], axis=1)
    to_segments(wide_ref, point_ref)
    rim = before[:, :128]
    rim_ref[...] = jnp.concatenate([rim, rim], axis=0).T

    def outside(start):
        count = min(SEGMENT, SEGMENT + start)
        rows = rim_ref[max(start, 0) : max(start, 0) + count].reshape(count, 1, LANES)
        rows = jnp.broadcast_to(rows, (count, 8, LANES))
        if count < SEGMENT:
            rows = jnp.concatenate([jnp.zeros((SEGMENT - count, 8, LANES), F32), rows], axis=0)
        return rows

    rows = point_ref[...].reshape(SEGMENT, 8, LANES)
    spread_earlier(rows, spread_ref, outside)
    short_inputs(spread_ref, inputs_ref, 1)
    rebuilt_ref[...] = filter_rows(inputs_ref, taps_ref, sums_ref, True).reshape(SIDE, LANES)


def rebuild(place, temporal, activations, edge):
    atoms, width = activations.shape
    half = CHUNK // 2
    last = width // half - 1
    block = (atoms, half)
    return pl.pallas_call(
        rebuild_body,
        grid_spec=pltpu.PrefetchScalarGridSpec(
            num_scalar_prefetch=1,
            grid=(1,),
            in_specs=[
                pl.BlockSpec((ATOMS, LENGTH), lambda i, place: (0, 0)),
                pl.BlockSpec(block, lambda i, place: (0, jnp.maximum(2 * place[0] - 1, 0))),
                pl.BlockSpec(block, lambda i, place: (0, 2 * place[0])),
                pl.BlockSpec(block, lambda i, place: (0, 2 * place[0] + 1)),
                pl.BlockSpec(block, lambda i, place: (0, jnp.minimum(2 * place[0] + 2, last))),
                pl.BlockSpec(block, lambda i, place: (0, 0)),
            ],
            out_specs=[pl.BlockSpec((SIDE, LANES), lambda i, place: (0, 0))] * 2,
            scratch_shapes=FILTER_SCRATCH + [pltpu.VMEM((LENGTH, LANES), F32)],
        ),
        out_shape=[jax.ShapeDtypeStruct((SIDE, LANES), F32)] * 2,
        compiler_params=params(12),
        cost_estimate=cost(2 * SIDE * LANES * LENGTH, 2**20),
    )(place, temporal, activations, activations, activations, activations, edge)


def steps_body(
    total, begin_ref, half_ref, step_ref, mine_ref, inner_ref, outer_ref, rebuilt_ref, point_ref,
    temporal_ref, threshold_ref, out_ref, taps_ref, spread_ref, inputs_ref, sums_ref, wide_ref,
    cross_ref, mix_ref,
):
    begin = begin_ref[0]
    rate = step_ref[0]
    spread_taps(temporal_ref, taps_ref)
    gram_rows = mine_ref[ATOMS:]
    gram = jnp.concatenate([gram_rows[:, ATOMS * i : ATOMS * (i + 1)] for i in range(8)], axis=0)
    mix_ref[...] = jnp.zeros_like(mix_ref)
    mix_ref[:ATOMS, :ATOMS] = gram
    mix_ref[ATOMS:, ATOMS:] = gram
    mine = mine_ref[:ATOMS]
    first = half_ref[0] == 0
    left = jnp.where(first, outer_ref[:, 128:], inner_ref[:, 128:])
    right = jnp.where(first, inner_ref[...], outer_ref[...])
    wide_ref[:ATOMS] = jnp.concatenate([left, mine[:, :384]], axis=1)
    wide_ref[ATOMS:] = jnp.concatenate([mine[:, 320:], right, right[:, :64]], axis=1)
    to_segments(wide_ref, cross_ref)

    shape = (SEGMENT, 8, LANES)
    sample = lax.broadcasted_iota(jnp.int32, shape, 0) + (
        (lane_half() * 8 + sublane()) * SEGMENT + (begin - LENGTH)
    )
    shrink = threshold_ref[...]
    shrink = jnp.concatenate([shrink, shrink], axis=1).reshape(1, 1, LANES)

    def projected(rebuilt):
        mixed = jnp.dot(rebuilt, mix_ref[...], precision=HIGHEST, preferred_element_type=F32)
        rows = (mixed - cross_ref[...]).reshape(shape)
        return jnp.where(sample < total, rows, 0.0)

    def stepped(point, rows):
        spread_later(rows, spread_ref)
        short_inputs(spread_ref, inputs_ref, 0)
        gradient = filter_rows(inputs_ref, taps_ref, sums_ref, False)
        return jnp.maximum(point - rate * (gradient + shrink), 0.0)

    inertia = 1.0
    inertia_next = (1.0 + (1.0 + 4.0 * inertia * inertia) ** 0.5) / 2.0
    momentum = (inertia - 1.0) / inertia_next
    previous = point_ref[...].reshape(shape)
    update = stepped(previous, projected(rebuilt_ref[...]))
    point = update + momentum * (update - previous)
    point = jnp.where(sample >= 0, point, 0.0)

    spread_earlier(point, spread_ref)
    short_inputs(spread_ref, inputs_ref, 1)
    rebuilt = filter_rows(inputs_ref, taps_ref, sums_ref, True)
    update = stepped(point, projected(rebuilt.reshape(SIDE, LANES)))

    cross_ref[...] = update.reshape(SIDE, LANES)
    rows = [cross_ref[pl.ds(s, SEGMENT, stride=8)] for s in range(8)]
    rows.append(jnp.zeros((512 - SIDE, LANES), F32))
    columns = jnp.concatenate(rows, axis=0).T
    out_ref[...] = jnp.concatenate([columns[:ATOMS, 128:SIDE], columns[ATOMS:, :192]], axis=1)


def steps(total, begin, half, step_size, mine, inner, outer, rebuilt, point, temporal, threshold):
    def body(*refs):
        steps_body(total, *refs)

    return pl.pallas_call(
        body,
        in_specs=[SMEM] * 3 + [VMEM] * 7,
        out_specs=VMEM,
        out_shape=jax.ShapeDtypeStruct((ATOMS, CHUNK), F32),
        scratch_shapes=FILTER_SCRATCH
        + [pltpu.VMEM((SIDE, LANES), F32), pltpu.VMEM((LANES, LANES), F32)],
        compiler_params=params(12),
        cost_estimate=cost(6 * SIDE * LANES * LENGTH, 2**20),
    )(begin, half, step_size, mine, inner, outer, rebuilt, point, temporal, threshold)


def place_copies(half, chunks_ref, out_ref, sems):
    copies = []
    for i in range(QUARTER):
        column = pl.multiple_of((2 * i + half) * CHUNK, CHUNK)
        copies.append(
            pltpu.make_async_copy(chunks_ref.at[i], out_ref.at[:, pl.ds(column, CHUNK)], sems.at[i])
        )
    for copy in copies:
        copy.start()
    for copy in copies:
        copy.wait()


def place_mine_body(half_ref, chunks_ref, out_ref, sems):
    place_copies(half_ref[0], chunks_ref, out_ref, sems)


def place_other_body(half_ref, chunks_ref, begun_ref, out_ref, sems):
    place_copies(1 - half_ref[0], chunks_ref, out_ref, sems)


def place_half(half, chunks, begun=None):
    out_shape = jax.ShapeDtypeStruct((ATOMS, CHUNKS * CHUNK), F32)
    first = begun is None
    return pl.pallas_call(
        place_mine_body if first else place_other_body,
        in_specs=[SMEM, ANY] + ([] if first else [ANY]),
        out_specs=ANY,
        out_shape=out_shape,
        scratch_shapes=[pltpu.SemaphoreType.DMA((QUARTER,))],
        input_output_aliases={} if first else {2: 0},
        compiler_params=params(4),
        cost_estimate=cost(0, 2**20),
    )(half, chunks, *([] if first else [begun]))


def solution(mesh):
    blocks = mesh.shape["tm"]
    split = Mesh(mesh.devices.reshape(2, 4, 2, blocks), ("zh", "y", "c", "tm"))
    swap = [(0, 1), (1, 0)]
    line = ("zh", "y", "c", "tm")

    def device(zh, q, tm):
        return (zh * CHUNKS + q) * blocks + tm

    inside, rims = [], []
    for zh in range(2):
        for tm in range(blocks):
            for q in range(1, CHUNKS - 1, 2):
                inside.append((device(zh, q, tm), device(zh, q + 1, tm)))
            if tm + 1 < blocks:
                near = 1 - zh if (tm + 1) % RUN == 0 else zh
                rims.append((device(zh, CHUNKS - 1, tm), device(near, 0, tm + 1)))
    rims = rims + [(b, a) for a, b in rims]
    outside = rims + inside + [(b, a) for a, b in inside]

    def per_device(signal, spatial, temporal, activations, threshold, step_size):
        half = lax.axis_index("c").astype(jnp.int32)
        place = lax.axis_index("y").astype(jnp.int32) * 2 + half
        time_block = lax.axis_index("tm").astype(jnp.int32)
        width = activations.shape[1]
        spatial = spatial.T
        high = lax.reduce_precision(spatial, 8, 7)
        parts = jnp.concatenate([high, spatial - high], axis=0).astype(jnp.bfloat16)

        away, kept = project(half[None], parts, signal)
        summed = kept + lax.ppermute(away, "c", swap)

        rim = CHUNK // 2
        first = half == 0
        activations, summed = lax.optimization_barrier((activations, summed))
        edge = jnp.where(first, activations[:, :rim], activations[:, width - rim :])
        pieces = lax.all_to_all(summed, "y", 0, 0, tiled=True)
        edge = lax.ppermute(edge, line, rims)
        rebuilt, point = rebuild(place[None], temporal, activations, edge)
        group_sum = jnp.sum(pieces, axis=0)
        group_sum, rebuilt, point = lax.optimization_barrier((group_sum, rebuilt, point))
        mine = jnp.sum(lax.all_gather(group_sum, "zh", axis=0), axis=0)

        start, end = mine[:ATOMS, :rim], mine[:ATOMS, CHUNK - rim :]
        outer = lax.ppermute(jnp.where(first, start, end), line, outside)
        inner = lax.ppermute(jnp.where(first, end, start), "c", swap)
        begin = time_block * width + place * CHUNK
        update = steps(
            blocks * width, begin[None], half[None], step_size, mine, inner, outer, rebuilt, point,
            temporal, threshold[None, :],
        )

        gathered = lax.all_gather(update, "y", axis=0)
        other = lax.ppermute(gathered, "c", swap)
        return place_half(half[None], other, place_half(half[None], gathered))

    chan = ("zh", "y", "c")
    in_specs = (P(chan, "tm"), P(chan, None), P(), P(None, "tm"), P(), P())
    return jax.shard_map(
        per_device, mesh=split, in_specs=in_specs, out_specs=P(None, "tm"), check_vma=False
    )
```

```python
import jax
import jax.numpy as jnp
from jax import lax
from jax.experimental import pallas as pl
from jax.experimental.pallas import tpu as pltpu
from jax.sharding import Mesh, PartitionSpec as P

ATOMS = 64
LENGTH = 128
CHUNK = 512
CHUNKS = 8
QUARTER = 4
LANES = 2 * ATOMS
TILES = CHUNK // LANES
BODY = TILES * ATOMS
ROWS = BODY + 16
HALO = BODY // 2 + 16
RIM = LANES + ATOMS
NARROW, WIDE = 48, 56
RUN = 8
HIGHEST = lax.Precision.HIGHEST
F32 = jnp.float32
VMEM = pl.BlockSpec(memory_space=pltpu.VMEM)
SMEM = pl.BlockSpec(memory_space=pltpu.SMEM)
ANY = pl.BlockSpec(memory_space=pl.ANY)


def cost(flops, bytes_accessed):
    return pl.CostEstimate(flops=flops, bytes_accessed=bytes_accessed, transcendentals=0)


def params(mebibytes):
    return pltpu.CompilerParams(vmem_limit_bytes=mebibytes * 2**20)


def project_body(half_ref, parts_ref, signal_ref, away_ref, kept_ref):
    first = half_ref[0] == 0
    parts = parts_ref[...]
    gram = lax.dot_general(parts, parts, (((1,), (1,)), ((), ())), preferred_element_type=F32)
    gram = gram[:ATOMS] + gram[ATOMS:]
    gram = gram[:, :ATOMS] + gram[:, ATOMS:]
    upper = jnp.concatenate([gram[:16], gram[16:32]], axis=1)
    lower = jnp.concatenate([gram[32:48], gram[48:]], axis=1)
    away_gram, kept_gram = jnp.where(first, lower, upper), jnp.where(first, upper, lower)
    for i in range(QUARTER):
        away_ref[i, BODY:] = away_gram
        kept_ref[i, BODY:] = kept_gram
    for out_ref, which in ((away_ref, 1 - half_ref[0]), (kept_ref, half_ref[0])):
        for i in range(QUARTER):
            column = pl.multiple_of((2 * i + which) * CHUNK, CHUNK)
            product = jnp.dot(
                parts, signal_ref[:, pl.ds(column, CHUNK)], preferred_element_type=F32
            )
            product = product[:ATOMS] + product[ATOMS:]
            for t in range(TILES):
                out_ref[i, t * ATOMS : (t + 1) * ATOMS] = product[:, t * LANES : (t + 1) * LANES]


def project(half, parts, signal):
    channels, width = signal.shape
    return pl.pallas_call(
        project_body,
        in_specs=[SMEM, VMEM, VMEM],
        out_specs=[VMEM, VMEM],
        out_shape=[jax.ShapeDtypeStruct((QUARTER, ROWS, LANES), F32)] * 2,
        compiler_params=params(8),
        cost_estimate=cost(2 * channels * LANES * width, 2 * channels * width),
    )(half, parts, signal)


def to_segments(rows, segment, out_ref):
    for s in range(8):
        out_ref[pl.ds(s, segment, stride=8)] = rows[s * segment : (s + 1) * segment]


def from_segments(ref, segment):
    return jnp.concatenate([ref[pl.ds(s, segment, stride=8)] for s in range(8)], axis=0)


def spread_taps(temporal_ref, taps_ref):
    temporal = temporal_ref[...]
    columns = jnp.concatenate([temporal, temporal], axis=0).T
    for i in range(LENGTH // 4):
        c0, c1, c2, c3 = (
            jnp.broadcast_to(columns[4 * i + p : 4 * i + p + 1], (8, LANES)) for p in range(4)
        )
        even, odd = c0 + c1, c2 + c3
        for k, tap in enumerate((c0, c0 + c2, c2, even, even + odd, odd, c1, c1 + c3, c3)):
            taps_ref[k, i] = tap


def lane_half():
    return lax.broadcasted_iota(jnp.int32, (1, 8, LANES), 2) // ATOMS


def sublane():
    return lax.broadcasted_iota(jnp.int32, (1, 8, LANES), 1)


def later_segment(rows):
    up = pltpu.roll(rows, 7, 1)
    return jnp.where(sublane() == 7, pltpu.roll(up, ATOMS, 2), up)


def earlier_segment(rows):
    down = pltpu.roll(rows, 1, 1)
    return jnp.where(sublane() == 0, pltpu.roll(down, ATOMS, 2), down)


def over_sublanes(rows):
    count = rows.shape[0]
    return jnp.broadcast_to(rows.reshape(count, 1, LANES), (count, 8, LANES))


def spread_later(rows, spread_ref, beyond=None):
    segment = rows.shape[0]
    reach = segment + LENGTH
    for first in range(0, reach, segment):
        count = min(segment, reach - first)
        rows = rows[:count]
        if first > 0:
            rows = later_segment(rows)
            if beyond is not None:
                last = (sublane() == 7) & (lane_half() == 1)
                start = first - segment
                rows = jnp.where(last, over_sublanes(beyond[start : start + count]), rows)
        spread_ref[first // 4 : (first + count) // 4] = rows.reshape(count // 4, 4, 8, LANES)


def spread_earlier(rows, spread_ref, before=None):
    segment = rows.shape[0]
    start = LENGTH
    while True:
        skip = max(0, -start)
        first, count = start + skip, segment - skip
        kept = rows[skip:]
        spread_ref[first // 4 : (first + count) // 4] = kept.reshape(count // 4, 4, 8, LANES)
        if start <= 0:
            return
        rows = earlier_segment(rows)
        start -= segment
        if before is not None:
            skip = max(0, -start)
            rim = over_sublanes(before[start + skip : start + segment])
            if skip:
                rim = jnp.concatenate([jnp.zeros((skip, 8, LANES), F32), rim], axis=0)
            rows = jnp.where((sublane() == 0) & (lane_half() == 0), rim, rows)


def short_inputs(segment, spread_ref, inputs_ref, offset):
    count = (segment + LENGTH) // 4 - 1

    def x(p):
        p = p + offset
        return spread_ref[p // 4 : p // 4 + count, p % 4]

    x0, x1, x2, x3, x4, x5, x6 = (x(p) for p in range(7))
    inputs_ref[0, :count] = (x0 - x1) - (x2 - x3)
    inputs_ref[1, :count] = x2 - x3
    inputs_ref[2, :count] = (x4 - x5) - (x2 - x3)
    inputs_ref[3, :count] = x1 - x3
    inputs_ref[4, :count] = x3
    inputs_ref[5, :count] = x5 - x3
    inputs_ref[6, :count] = (x2 - x1) - (x4 - x3)
    inputs_ref[7, :count] = x4 - x3
    inputs_ref[8, :count] = (x6 - x5) - (x4 - x3)


def filter_rows(segment, inputs_ref, taps_ref, sums_ref, reverse):
    taps = LENGTH // 4
    phase = segment // 4

    @pl.loop(0, 9, unroll=3)
    def _(k):
        sums = [None] * phase
        held = {}
        for j in range(phase + taps - 1):
            if j < taps:
                held[j] = taps_ref[8 - k, taps - 1 - j] if reverse else taps_ref[k, j]
            value = inputs_ref[k, j]
            for m in range(max(0, j - phase + 1), min(taps, j + 1)):
                term = value * held[m]
                sums[j - m] = term if sums[j - m] is None else sums[j - m] + term
        for i in range(phase):
            sums_ref[k, i] = sums[i]

    def total(i, k):
        return sums_ref[i, :phase] + sums_ref[k, :phase]

    a, b, c = total(0, 1), total(3, 4), total(6, 7)
    d, e, f = total(1, 2), total(4, 5), total(7, 8)
    rows = jnp.stack([a + b, b + c, d + e, e + f], axis=1)
    return rows.reshape(segment, 8, LANES)


def filter_scratch(segment):
    reach = (segment + LENGTH) // 4
    return [
        pltpu.VMEM((9, LENGTH // 4, 8, LANES), F32),
        pltpu.VMEM((reach, 4, 8, LANES), F32),
        pltpu.VMEM((9, reach, 8, LANES), F32),
        pltpu.VMEM((9, segment // 4, 8, LANES), F32),
    ]


def rebuild_body(
    place_ref, temporal_ref, before_ref, first_ref, second_ref, after_ref,
    rebuilt_ref, beyond_ref, point_ref, rim_ref, taps_ref, spread_ref, inputs_ref, sums_ref, wide_ref,
):
    place = place_ref[0]
    spread_taps(temporal_ref, taps_ref)
    before = jnp.where(place == 0, 0.0, before_ref[...])
    after = jnp.where(place == CHUNKS - 1, 0.0, after_ref[...])
    first, second = first_ref[...], second_ref[...]
    upper = jnp.concatenate([before[:, 128:], first], axis=1)
    lower = jnp.concatenate([second, after[:, :128]], axis=1)
    to_segments(jnp.concatenate([upper, lower], axis=0).T, NARROW, point_ref)

    upper = jnp.concatenate([upper, second[:, :128]], axis=1)
    lower = jnp.concatenate([second[:, 64:], after, after[:, :64]], axis=1)
    to_segments(jnp.concatenate([upper, lower], axis=0).T, WIDE, wide_ref)
    ahead = before[:, :128]
    ahead = jnp.concatenate([ahead, ahead], axis=0).T
    spread_earlier(wide_ref[...].reshape(WIDE, 8, LANES), spread_ref, ahead)
    short_inputs(WIDE, spread_ref, inputs_ref, 1)
    rebuilt = filter_rows(WIDE, inputs_ref, taps_ref, sums_ref, True)

    wide_ref[...] = rebuilt.reshape(8 * WIDE, LANES)
    rows = from_segments(wide_ref, WIDE)
    swapped = pltpu.roll(rows, ATOMS, 1)
    left = lax.broadcasted_iota(jnp.int32, (1, LANES), 1) < ATOMS
    lower = jnp.concatenate([swapped[384:], rows[:320]], axis=0)
    to_segments(jnp.where(left, rows[:384], lower), NARROW, rebuilt_ref)
    beyond_ref[...] = jnp.where(left, swapped[320:], rows[320:])

    starting = place % 2 == 0
    start = jnp.where(left, rows[128:256], swapped[256:384])
    end = jnp.where(left, swapped[64:192], rows[192:320])
    rim_ref[:LANES] = jnp.where(starting, start, end)
    rim_ref[LANES:] = jnp.where(starting, first[:, :128], second[:, 128:])


def rebuild(place, temporal, activations):
    atoms, width = activations.shape
    half = CHUNK // 2
    last = width // half - 1
    block = (atoms, half)
    shapes = [(8 * NARROW, LANES), (LENGTH, LANES), (8 * NARROW, LANES), (RIM, LANES)]
    return pl.pallas_call(
        rebuild_body,
        grid_spec=pltpu.PrefetchScalarGridSpec(
            num_scalar_prefetch=1,
            grid=(1,),
            in_specs=[
                pl.BlockSpec((ATOMS, LENGTH), lambda i, place: (0, 0)),
                pl.BlockSpec(block, lambda i, place: (0, jnp.maximum(2 * place[0] - 1, 0))),
                pl.BlockSpec(block, lambda i, place: (0, 2 * place[0])),
                pl.BlockSpec(block, lambda i, place: (0, 2 * place[0] + 1)),
                pl.BlockSpec(block, lambda i, place: (0, jnp.minimum(2 * place[0] + 2, last))),
            ],
            out_specs=[pl.BlockSpec(shape, lambda i, place: (0, 0)) for shape in shapes],
            scratch_shapes=filter_scratch(WIDE) + [pltpu.VMEM((8 * WIDE, LANES), F32)],
        ),
        out_shape=[jax.ShapeDtypeStruct(shape, F32) for shape in shapes],
        compiler_params=params(12),
        cost_estimate=cost(2 * 8 * WIDE * LANES * LENGTH, 2**20),
    )(place, temporal, activations, activations, activations, activations)


def steps_body(
    total, begin_ref, place_ref, step_ref, mine_ref, inner_ref, outer_ref, rebuilt_ref, beyond_ref,
    point_ref, temporal_ref, threshold_ref, out_ref, taps_ref, spread_ref, inputs_ref, sums_ref,
    cross_ref, side_ref, mix_ref,
):
    begin, place = begin_ref[0], place_ref[0]
    first = place % 2 == 0
    rate = step_ref[0]
    spread_taps(temporal_ref, taps_ref)

    own, other = mine_ref[BODY:], inner_ref[BODY // 2 :]
    upper, lower = jnp.where(first, own, other), jnp.where(first, other, own)
    gram = jnp.concatenate(
        [upper[:, :ATOMS], upper[:, ATOMS:], lower[:, :ATOMS], lower[:, ATOMS:]], axis=0
    )
    mix_ref[...] = jnp.zeros_like(mix_ref)
    mix_ref[:ATOMS, :ATOMS] = gram
    mix_ref[ATOMS:, ATOMS:] = gram

    near, far = slice(0, ATOMS), slice(ATOMS, 2 * ATOMS)
    left = jnp.where(first, outer_ref[far], inner_ref[far])
    right = jnp.where(first, inner_ref[near], outer_ref[near])
    beyond = jnp.where(first, inner_ref[far], outer_ref[far])
    tiles = [mine_ref[t * ATOMS : (t + 1) * ATOMS] for t in range(TILES)]
    upper = jnp.concatenate([left, tiles[0], tiles[1]], axis=1)
    lower = jnp.concatenate([tiles[2], tiles[3], right], axis=1)
    to_segments(jnp.concatenate([upper, lower], axis=0).T, NARROW, cross_ref)
    beyond = jnp.concatenate([beyond, beyond], axis=0).T

    left_half = lax.broadcasted_iota(jnp.int32, (1, LANES), 1) < ATOMS
    at_start = left_half & (place == 0)
    at_end = jnp.logical_not(left_half) & (place == CHUNKS - 1)
    added = outer_ref[HALO : HALO + LANES]
    swapped = pltpu.roll(added, ATOMS, 1)
    to_segments(
        jnp.concatenate(
            [
                jnp.where(at_start, added, 0.0),
                jnp.where(at_start, swapped, 0.0),
                jnp.where(at_end, swapped, 0.0),
            ],
            axis=0,
        ),
        NARROW,
        side_ref,
    )
    rebuilt = rebuilt_ref[...] + side_ref[...]
    added_beyond = jnp.where(left_half, swapped, added)
    rebuilt_beyond = beyond_ref[...] + jnp.where(place == CHUNKS - 1, added_beyond, 0.0)
    rim = outer_ref[HALO + LANES :]
    rim = jnp.concatenate([rim, rim], axis=0).T
    to_segments(
        jnp.concatenate(
            [jnp.where(at_start, rim, 0.0), jnp.zeros_like(rim), jnp.where(at_end, rim, 0.0)],
            axis=0,
        ),
        NARROW,
        side_ref,
    )

    shape = (NARROW, 8, LANES)
    sample = lax.broadcasted_iota(jnp.int32, shape, 0) + (
        (lane_half() * 8 + sublane()) * NARROW + (begin - LENGTH)
    )
    sample_beyond = lax.broadcasted_iota(jnp.int32, (LENGTH, LANES), 0) + (begin + CHUNK + LENGTH)
    shrink = threshold_ref[...]
    shrink = jnp.concatenate([shrink, shrink], axis=1).reshape(1, 1, LANES)

    def mixed(rebuilt):
        return jnp.dot(rebuilt, mix_ref[...], precision=HIGHEST, preferred_element_type=F32)

    def projected(rebuilt):
        rows = (mixed(rebuilt) - cross_ref[...]).reshape(shape)
        return jnp.where(sample < total, rows, 0.0)

    def stepped(point, rows, rows_beyond=None):
        spread_later(rows, spread_ref, rows_beyond)
        short_inputs(NARROW, spread_ref, inputs_ref, 0)
        gradient = filter_rows(NARROW, inputs_ref, taps_ref, sums_ref, False)
        return jnp.maximum(point - rate * (gradient + shrink), 0.0)

    inertia = 1.0
    inertia_next = (1.0 + (1.0 + 4.0 * inertia * inertia) ** 0.5) / 2.0
    momentum = (inertia - 1.0) / inertia_next
    previous = (point_ref[...] + side_ref[...]).reshape(shape)
    beyond = jnp.where(sample_beyond < total, mixed(rebuilt_beyond) - beyond, 0.0)
    update = stepped(previous, projected(rebuilt), beyond)
    point = update + momentum * (update - previous)
    point = jnp.where(sample >= 0, point, 0.0)

    spread_earlier(point, spread_ref)
    short_inputs(NARROW, spread_ref, inputs_ref, 1)
    rebuilt = filter_rows(NARROW, inputs_ref, taps_ref, sums_ref, True)
    update = stepped(point, projected(rebuilt.reshape(8 * NARROW, LANES)))

    cross_ref[...] = update.reshape(8 * NARROW, LANES)
    columns = from_segments(cross_ref, NARROW).T
    out_ref[...] = jnp.concatenate([columns[:ATOMS, 128:], columns[ATOMS:, :256]], axis=1)


def steps(total, begin, place, step_size, mine, inner, outer, before_steps, temporal, threshold):
    def body(*refs):
        steps_body(total, *refs)

    return pl.pallas_call(
        body,
        in_specs=[SMEM] * 3 + [VMEM] * 8,
        out_specs=VMEM,
        out_shape=jax.ShapeDtypeStruct((ATOMS, CHUNK), F32),
        scratch_shapes=filter_scratch(NARROW)
        + [pltpu.VMEM((8 * NARROW, LANES), F32)] * 2
        + [pltpu.VMEM((LANES, LANES), F32)],
        compiler_params=params(12),
        cost_estimate=cost(6 * 8 * NARROW * LANES * LENGTH, 2**20),
    )(begin, place, step_size, mine, inner, outer, *before_steps, temporal, threshold)


def place_copies(half, chunks_ref, out_ref, sems):
    copies = []
    for i in range(QUARTER):
        column = pl.multiple_of((2 * i + half) * CHUNK, CHUNK)
        copies.append(
            pltpu.make_async_copy(chunks_ref.at[i], out_ref.at[:, pl.ds(column, CHUNK)], sems.at[i])
        )
    for copy in copies:
        copy.start()
    for copy in copies:
        copy.wait()


def place_mine_body(half_ref, chunks_ref, out_ref, sems):
    place_copies(half_ref[0], chunks_ref, out_ref, sems)


def place_other_body(half_ref, chunks_ref, begun_ref, out_ref, sems):
    place_copies(1 - half_ref[0], chunks_ref, out_ref, sems)


def place_half(half, chunks, begun=None):
    out_shape = jax.ShapeDtypeStruct((ATOMS, CHUNKS * CHUNK), F32)
    first = begun is None
    return pl.pallas_call(
        place_mine_body if first else place_other_body,
        in_specs=[SMEM, ANY] + ([] if first else [ANY]),
        out_specs=ANY,
        out_shape=out_shape,
        scratch_shapes=[pltpu.SemaphoreType.DMA((QUARTER,))],
        input_output_aliases={} if first else {2: 0},
        compiler_params=params(4),
        cost_estimate=cost(0, 2**20),
    )(half, chunks, *([] if first else [begun]))


def solution(mesh):
    blocks = mesh.shape["tm"]
    split = Mesh(mesh.devices.reshape(2, 4, 2, blocks), ("zh", "y", "c", "tm"))
    swap = [(0, 1), (1, 0)]
    line = ("zh", "y", "c", "tm")

    def device(zh, q, tm):
        return (zh * CHUNKS + q) * blocks + tm

    inside, rims = [], []
    for zh in range(2):
        for tm in range(blocks):
            for q in range(1, CHUNKS - 1, 2):
                inside.append((device(zh, q, tm), device(zh, q + 1, tm)))
            if tm + 1 < blocks:
                near = 1 - zh if (tm + 1) % RUN == 0 else zh
                rims.append((device(zh, CHUNKS - 1, tm), device(near, 0, tm + 1)))
    rims = rims + [(b, a) for a, b in rims]
    outside = rims + inside + [(b, a) for a, b in inside]

    def per_device(signal, spatial, temporal, activations, threshold, step_size):
        half = lax.axis_index("c").astype(jnp.int32)
        place = lax.axis_index("y").astype(jnp.int32) * 2 + half
        time_block = lax.axis_index("tm").astype(jnp.int32)
        width = activations.shape[1]
        spatial = spatial.T
        high = lax.reduce_precision(spatial, 8, 7)
        parts = jnp.concatenate([high, spatial - high], axis=0).astype(jnp.bfloat16)
        away, kept = project(half[None], parts, signal)
        summed = kept + lax.ppermute(away, "c", swap)

        activations, summed = lax.optimization_barrier((activations, summed))
        pieces = lax.all_to_all(summed, "y", 0, 0, tiled=True)
        *before_steps, rim = rebuild(place[None], temporal, activations)
        group_sum = jnp.sum(pieces, axis=0)
        group_sum, before_steps, rim = lax.optimization_barrier((group_sum, before_steps, rim))
        mine = jnp.sum(lax.all_gather(group_sum, "zh", axis=0), axis=0)

        first = half == 0
        start, end, gram = mine[: BODY // 2], mine[BODY // 2 : BODY], mine[BODY:]
        outer = jnp.concatenate([jnp.where(first, start, end), gram, rim], axis=0)
        outer = lax.ppermute(outer, line, outside)
        inner = jnp.concatenate([jnp.where(first, end, start), gram], axis=0)
        inner = lax.ppermute(inner, "c", swap)
        begin = time_block * width + place * CHUNK
        update = steps(
            blocks * width, begin[None], place[None], step_size, mine, inner, outer, before_steps,
            temporal, threshold[None, :],
        )

        copies = jnp.broadcast_to(update[None], (QUARTER, ATOMS, CHUNK))
        gathered = lax.all_to_all(copies, "y", 0, 0, tiled=True)
        other = lax.ppermute(gathered, "c", swap)
        return place_half(half[None], other, place_half(half[None], gathered))

    chan = ("zh", "y", "c")
    in_specs = (P(chan, "tm"), P(chan, None), P(), P(None, "tm"), P(), P())
    return jax.shard_map(
        per_device, mesh=split, in_specs=in_specs, out_specs=P(None, "tm"), check_vma=False
    )
```

```python
import jax
import jax.numpy as jnp
from jax import lax
from jax.experimental import pallas as pl
from jax.experimental.pallas import tpu as pltpu
from jax.sharding import Mesh, PartitionSpec as P

ATOMS = 64
LENGTH = 128
CHUNK = 512
CHUNKS = 8
QUARTER = 4
LANES = 2 * ATOMS
TILES = CHUNK // LANES
BODY = TILES * ATOMS
ROWS = BODY + 16
RIM = LANES + ATOMS
NARROW, WIDE = 48, 56
RUN = 8
HIGHEST = lax.Precision.HIGHEST
F32 = jnp.float32
VMEM = pl.BlockSpec(memory_space=pltpu.VMEM)
SMEM = pl.BlockSpec(memory_space=pltpu.SMEM)
ANY = pl.BlockSpec(memory_space=pl.ANY)


def cost(flops, bytes_accessed):
    return pl.CostEstimate(flops=flops, bytes_accessed=bytes_accessed, transcendentals=0)


def params(mebibytes):
    return pltpu.CompilerParams(vmem_limit_bytes=mebibytes * 2**20)


def project_body(half_ref, parts_ref, signal_ref, away_ref, kept_ref):
    first = half_ref[0] == 0
    parts = parts_ref[...]
    gram = lax.dot_general(parts, parts, (((1,), (1,)), ((), ())), preferred_element_type=F32)
    gram = gram[:ATOMS] + gram[ATOMS:]
    gram = gram[:, :ATOMS] + gram[:, ATOMS:]
    upper = jnp.concatenate([gram[:16], gram[16:32]], axis=1)
    lower = jnp.concatenate([gram[32:48], gram[48:]], axis=1)
    away_gram, kept_gram = jnp.where(first, lower, upper), jnp.where(first, upper, lower)
    for i in range(QUARTER):
        away_ref[i, BODY:] = away_gram
        kept_ref[i, BODY:] = kept_gram
    for out_ref, which in ((away_ref, 1 - half_ref[0]), (kept_ref, half_ref[0])):
        for i in range(QUARTER):
            column = pl.multiple_of((2 * i + which) * CHUNK, CHUNK)
            product = jnp.dot(
                parts, signal_ref[:, pl.ds(column, CHUNK)], preferred_element_type=F32
            )
            product = product[:ATOMS] + product[ATOMS:]
            for t in range(TILES):
                out_ref[i, t * ATOMS : (t + 1) * ATOMS] = product[:, t * LANES : (t + 1) * LANES]


def project(half, parts, signal):
    channels, width = signal.shape
    return pl.pallas_call(
        project_body,
        in_specs=[SMEM, VMEM, VMEM],
        out_specs=[VMEM, VMEM],
        out_shape=[jax.ShapeDtypeStruct((QUARTER, ROWS, LANES), F32)] * 2,
        compiler_params=params(8),
        cost_estimate=cost(2 * channels * LANES * width, 2 * channels * width),
    )(half, parts, signal)


def to_segments(rows, segment, out_ref):
    for s in range(8):
        out_ref[pl.ds(s, segment, stride=8)] = rows[s * segment : (s + 1) * segment]


def from_segments(ref, segment):
    return jnp.concatenate([ref[pl.ds(s, segment, stride=8)] for s in range(8)], axis=0)


def spread_taps(temporal_ref, taps_ref):
    temporal = temporal_ref[...]
    columns = jnp.concatenate([temporal, temporal], axis=0).T
    for i in range(LENGTH // 4):
        c0, c1, c2, c3 = (
            jnp.broadcast_to(columns[4 * i + p : 4 * i + p + 1], (8, LANES)) for p in range(4)
        )
        even, odd = c0 + c1, c2 + c3
        for k, tap in enumerate((c0, c0 + c2, c2, even, even + odd, odd, c1, c1 + c3, c3)):
            taps_ref[k, i] = tap


def lane_half():
    return lax.broadcasted_iota(jnp.int32, (1, 8, LANES), 2) // ATOMS


def sublane():
    return lax.broadcasted_iota(jnp.int32, (1, 8, LANES), 1)


def later_segment(rows):
    up = pltpu.roll(rows, 7, 1)
    return jnp.where(sublane() == 7, pltpu.roll(up, ATOMS, 2), up)


def earlier_segment(rows):
    down = pltpu.roll(rows, 1, 1)
    return jnp.where(sublane() == 0, pltpu.roll(down, ATOMS, 2), down)


def over_sublanes(rows):
    count = rows.shape[0]
    return jnp.broadcast_to(rows.reshape(count, 1, LANES), (count, 8, LANES))


def spread_later(rows, spread_ref, beyond=None):
    segment = rows.shape[0]
    reach = segment + LENGTH
    for first in range(0, reach, segment):
        count = min(segment, reach - first)
        rows = rows[:count]
        if first > 0:
            rows = later_segment(rows)
            if beyond is not None:
                last = (sublane() == 7) & (lane_half() == 1)
                start = first - segment
                rows = jnp.where(last, over_sublanes(beyond[start : start + count]), rows)
        spread_ref[first // 4 : (first + count) // 4] = rows.reshape(count // 4, 4, 8, LANES)


def spread_earlier(rows, spread_ref, before=None):
    segment = rows.shape[0]
    start = LENGTH
    while True:
        skip = max(0, -start)
        first, count = start + skip, segment - skip
        kept = rows[skip:]
        spread_ref[first // 4 : (first + count) // 4] = kept.reshape(count // 4, 4, 8, LANES)
        if start <= 0:
            return
        rows = earlier_segment(rows)
        start -= segment
        if before is not None:
            skip = max(0, -start)
            rim = over_sublanes(before[start + skip : start + segment])
            if skip:
                rim = jnp.concatenate([jnp.zeros((skip, 8, LANES), F32), rim], axis=0)
            rows = jnp.where((sublane() == 0) & (lane_half() == 0), rim, rows)


def short_inputs(segment, spread_ref, inputs_ref, offset):
    count = (segment + LENGTH) // 4 - 1

    def x(p):
        p = p + offset
        return spread_ref[p // 4 : p // 4 + count, p % 4]

    x0, x1, x2, x3, x4, x5, x6 = (x(p) for p in range(7))
    inputs_ref[0, :count] = (x0 - x1) - (x2 - x3)
    inputs_ref[1, :count] = x2 - x3
    inputs_ref[2, :count] = (x4 - x5) - (x2 - x3)
    inputs_ref[3, :count] = x1 - x3
    inputs_ref[4, :count] = x3
    inputs_ref[5, :count] = x5 - x3
    inputs_ref[6, :count] = (x2 - x1) - (x4 - x3)
    inputs_ref[7, :count] = x4 - x3
    inputs_ref[8, :count] = (x6 - x5) - (x4 - x3)


def filter_rows(segment, inputs_ref, taps_ref, sums_ref, reverse):
    taps = LENGTH // 4
    phase = segment // 4

    @pl.loop(0, 9, unroll=3)
    def _(k):
        sums = [None] * phase
        held = {}
        for j in range(phase + taps - 1):
            if j < taps:
                held[j] = taps_ref[8 - k, taps - 1 - j] if reverse else taps_ref[k, j]
            value = inputs_ref[k, j]
            for m in range(max(0, j - phase + 1), min(taps, j + 1)):
                term = value * held[m]
                sums[j - m] = term if sums[j - m] is None else sums[j - m] + term
        for i in range(phase):
            sums_ref[k, i] = sums[i]

    def total(i, k):
        return sums_ref[i, :phase] + sums_ref[k, :phase]

    a, b, c = total(0, 1), total(3, 4), total(6, 7)
    d, e, f = total(1, 2), total(4, 5), total(7, 8)
    rows = jnp.stack([a + b, b + c, d + e, e + f], axis=1)
    return rows.reshape(segment, 8, LANES)


def filter_scratch(segment):
    reach = (segment + LENGTH) // 4
    return [
        pltpu.VMEM((9, LENGTH // 4, 8, LANES), F32),
        pltpu.VMEM((reach, 4, 8, LANES), F32),
        pltpu.VMEM((9, reach, 8, LANES), F32),
        pltpu.VMEM((9, segment // 4, 8, LANES), F32),
    ]


def rebuild_body(
    place_ref, temporal_ref, before_ref, first_ref, second_ref, after_ref,
    rebuilt_ref, beyond_ref, point_ref, rim_ref, taps_ref, spread_ref, inputs_ref, sums_ref, wide_ref,
):
    place = place_ref[0]
    spread_taps(temporal_ref, taps_ref)
    before = jnp.where(place == 0, 0.0, before_ref[...])
    after = jnp.where(place == CHUNKS - 1, 0.0, after_ref[...])
    first, second = first_ref[...], second_ref[...]
    upper = jnp.concatenate([before[:, 128:], first], axis=1)
    lower = jnp.concatenate([second, after[:, :128]], axis=1)
    to_segments(jnp.concatenate([upper, lower], axis=0).T, NARROW, point_ref)

    upper = jnp.concatenate([upper, second[:, :128]], axis=1)
    lower = jnp.concatenate([second[:, 64:], after, after[:, :64]], axis=1)
    to_segments(jnp.concatenate([upper, lower], axis=0).T, WIDE, wide_ref)
    ahead = before[:, :128]
    ahead = jnp.concatenate([ahead, ahead], axis=0).T
    spread_earlier(wide_ref[...].reshape(WIDE, 8, LANES), spread_ref, ahead)
    short_inputs(WIDE, spread_ref, inputs_ref, 1)
    rebuilt = filter_rows(WIDE, inputs_ref, taps_ref, sums_ref, True)

    wide_ref[...] = rebuilt.reshape(8 * WIDE, LANES)
    rows = from_segments(wide_ref, WIDE)
    swapped = pltpu.roll(rows, ATOMS, 1)
    left = lax.broadcasted_iota(jnp.int32, (1, LANES), 1) < ATOMS
    lower = jnp.concatenate([swapped[384:], rows[:320]], axis=0)
    to_segments(jnp.where(left, rows[:384], lower), NARROW, rebuilt_ref)
    beyond_ref[...] = jnp.where(left, swapped[320:], rows[320:])

    starting = place % 2 == 0
    start = jnp.where(left, rows[128:256], swapped[256:384])
    end = jnp.where(left, swapped[64:192], rows[192:320])
    rim_ref[:LANES] = jnp.where(starting, start, end)
    rim_ref[LANES:] = jnp.where(starting, first[:, :128], second[:, 128:])


def rebuild(place, temporal, activations):
    atoms, width = activations.shape
    half = CHUNK // 2
    last = width // half - 1
    block = (atoms, half)
    shapes = [(8 * NARROW, LANES), (LENGTH, LANES), (8 * NARROW, LANES), (RIM, LANES)]
    return pl.pallas_call(
        rebuild_body,
        grid_spec=pltpu.PrefetchScalarGridSpec(
            num_scalar_prefetch=1,
            grid=(1,),
            in_specs=[
                pl.BlockSpec((ATOMS, LENGTH), lambda i, place: (0, 0)),
                pl.BlockSpec(block, lambda i, place: (0, jnp.maximum(2 * place[0] - 1, 0))),
                pl.BlockSpec(block, lambda i, place: (0, 2 * place[0])),
                pl.BlockSpec(block, lambda i, place: (0, 2 * place[0] + 1)),
                pl.BlockSpec(block, lambda i, place: (0, jnp.minimum(2 * place[0] + 2, last))),
            ],
            out_specs=[pl.BlockSpec(shape, lambda i, place: (0, 0)) for shape in shapes],
            scratch_shapes=filter_scratch(WIDE) + [pltpu.VMEM((8 * WIDE, LANES), F32)],
        ),
        out_shape=[jax.ShapeDtypeStruct(shape, F32) for shape in shapes],
        compiler_params=params(12),
        cost_estimate=cost(2 * 8 * WIDE * LANES * LENGTH, 2**20),
    )(place, temporal, activations, activations, activations, activations)


def steps_body(
    total, begin_ref, place_ref, step_ref, mine_ref, inner_ref, outer_ref, rim_ref, rebuilt_ref,
    beyond_ref, point_ref, temporal_ref, threshold_ref, out_ref, taps_ref, spread_ref, inputs_ref,
    sums_ref, cross_ref, side_ref, mix_ref,
):
    begin, place = begin_ref[0], place_ref[0]
    first = place % 2 == 0
    rate = step_ref[0]
    spread_taps(temporal_ref, taps_ref)

    own, other = mine_ref[BODY:], inner_ref[BODY // 2 :]
    upper, lower = jnp.where(first, own, other), jnp.where(first, other, own)
    gram = jnp.concatenate(
        [upper[:, :ATOMS], upper[:, ATOMS:], lower[:, :ATOMS], lower[:, ATOMS:]], axis=0
    )
    mix_ref[...] = jnp.zeros_like(mix_ref)
    mix_ref[:ATOMS, :ATOMS] = gram
    mix_ref[ATOMS:, ATOMS:] = gram

    near, far = slice(0, ATOMS), slice(ATOMS, 2 * ATOMS)
    left = jnp.where(first, outer_ref[far], inner_ref[far])
    right = jnp.where(first, inner_ref[near], outer_ref[near])
    beyond = jnp.where(first, inner_ref[far], outer_ref[far])
    tiles = [mine_ref[t * ATOMS : (t + 1) * ATOMS] for t in range(TILES)]
    upper = jnp.concatenate([left, tiles[0], tiles[1]], axis=1)
    lower = jnp.concatenate([tiles[2], tiles[3], right], axis=1)
    to_segments(jnp.concatenate([upper, lower], axis=0).T, NARROW, cross_ref)
    beyond = jnp.concatenate([beyond, beyond], axis=0).T

    left_half = lax.broadcasted_iota(jnp.int32, (1, LANES), 1) < ATOMS
    at_start = left_half & (place == 0)
    at_end = jnp.logical_not(left_half) & (place == CHUNKS - 1)
    added = rim_ref[:LANES]
    swapped = pltpu.roll(added, ATOMS, 1)
    to_segments(
        jnp.concatenate(
            [
                jnp.where(at_start, added, 0.0),
                jnp.where(at_start, swapped, 0.0),
                jnp.where(at_end, swapped, 0.0),
            ],
            axis=0,
        ),
        NARROW,
        side_ref,
    )
    rebuilt = rebuilt_ref[...] + side_ref[...]
    added_beyond = jnp.where(left_half, swapped, added)
    rebuilt_beyond = beyond_ref[...] + jnp.where(place == CHUNKS - 1, added_beyond, 0.0)
    rim = rim_ref[LANES:]
    rim = jnp.concatenate([rim, rim], axis=0).T
    to_segments(
        jnp.concatenate(
            [jnp.where(at_start, rim, 0.0), jnp.zeros_like(rim), jnp.where(at_end, rim, 0.0)],
            axis=0,
        ),
        NARROW,
        side_ref,
    )

    shape = (NARROW, 8, LANES)
    sample = lax.broadcasted_iota(jnp.int32, shape, 0) + (
        (lane_half() * 8 + sublane()) * NARROW + (begin - LENGTH)
    )
    sample_beyond = lax.broadcasted_iota(jnp.int32, (LENGTH, LANES), 0) + (begin + CHUNK + LENGTH)
    shrink = threshold_ref[...]
    shrink = jnp.concatenate([shrink, shrink], axis=1).reshape(1, 1, LANES)

    def mixed(rebuilt):
        return jnp.dot(rebuilt, mix_ref[...], precision=HIGHEST, preferred_element_type=F32)

    def projected(rebuilt):
        rows = (mixed(rebuilt) - cross_ref[...]).reshape(shape)
        return jnp.where(sample < total, rows, 0.0)

    def stepped(point, rows, rows_beyond=None):
        spread_later(rows, spread_ref, rows_beyond)
        short_inputs(NARROW, spread_ref, inputs_ref, 0)
        gradient = filter_rows(NARROW, inputs_ref, taps_ref, sums_ref, False)
        return jnp.maximum(point - rate * (gradient + shrink), 0.0)

    inertia = 1.0
    inertia_next = (1.0 + (1.0 + 4.0 * inertia * inertia) ** 0.5) / 2.0
    momentum = (inertia - 1.0) / inertia_next
    previous = (point_ref[...] + side_ref[...]).reshape(shape)
    beyond = jnp.where(sample_beyond < total, mixed(rebuilt_beyond) - beyond, 0.0)
    update = stepped(previous, projected(rebuilt), beyond)
    point = update + momentum * (update - previous)
    point = jnp.where(sample >= 0, point, 0.0)

    spread_earlier(point, spread_ref)
    short_inputs(NARROW, spread_ref, inputs_ref, 1)
    rebuilt = filter_rows(NARROW, inputs_ref, taps_ref, sums_ref, True)
    update = stepped(point, projected(rebuilt.reshape(8 * NARROW, LANES)))

    cross_ref[...] = update.reshape(8 * NARROW, LANES)
    columns = from_segments(cross_ref, NARROW).T
    for i in range(QUARTER):
        out_ref[i] = jnp.concatenate([columns[:ATOMS, 128:], columns[ATOMS:, :256]], axis=1)


def steps(
    total, begin, place, step_size, mine, inner, outer, rim, before_steps, temporal, threshold
):
    def body(*refs):
        steps_body(total, *refs)

    return pl.pallas_call(
        body,
        in_specs=[SMEM] * 3 + [VMEM] * 9,
        out_specs=VMEM,
        out_shape=jax.ShapeDtypeStruct((QUARTER, ATOMS, CHUNK), F32),
        scratch_shapes=filter_scratch(NARROW)
        + [pltpu.VMEM((8 * NARROW, LANES), F32)] * 2
        + [pltpu.VMEM((LANES, LANES), F32)],
        compiler_params=params(12),
        cost_estimate=cost(6 * 8 * NARROW * LANES * LENGTH, 2**20),
    )(begin, place, step_size, mine, inner, outer, rim, *before_steps, temporal, threshold)


def place_copies(half, chunks_ref, out_ref, sems):
    copies = []
    for i in range(QUARTER):
        column = pl.multiple_of((2 * i + half) * CHUNK, CHUNK)
        copies.append(
            pltpu.make_async_copy(chunks_ref.at[i], out_ref.at[:, pl.ds(column, CHUNK)], sems.at[i])
        )
    for copy in copies:
        copy.start()
    for copy in copies:
        copy.wait()


def place_mine_body(half_ref, chunks_ref, out_ref, sems):
    place_copies(half_ref[0], chunks_ref, out_ref, sems)


def place_other_body(half_ref, chunks_ref, begun_ref, out_ref, sems):
    place_copies(1 - half_ref[0], chunks_ref, out_ref, sems)


def place_half(half, chunks, begun=None):
    out_shape = jax.ShapeDtypeStruct((ATOMS, CHUNKS * CHUNK), F32)
    first = begun is None
    return pl.pallas_call(
        place_mine_body if first else place_other_body,
        in_specs=[SMEM, ANY] + ([] if first else [ANY]),
        out_specs=ANY,
        out_shape=out_shape,
        scratch_shapes=[pltpu.SemaphoreType.DMA((QUARTER,))],
        input_output_aliases={} if first else {2: 0},
        compiler_params=params(4),
        cost_estimate=cost(0, 2**20),
    )(half, chunks, *([] if first else [begun]))


def solution(mesh):
    blocks = mesh.shape["tm"]
    split = Mesh(mesh.devices.reshape(2, 4, 2, blocks), ("zh", "y", "c", "tm"))
    swap = [(0, 1), (1, 0)]
    line = ("zh", "y", "c", "tm")

    def device(zh, q, tm):
        return (zh * CHUNKS + q) * blocks + tm

    outside, rims = [], []
    for zh in range(2):
        for tm in range(blocks):
            for q in range(1, CHUNKS - 1, 2):
                outside.append((device(zh, q, tm), device(zh, q + 1, tm)))
            if tm + 1 < blocks:
                last = device(zh, CHUNKS - 1, tm)
                near = 1 - zh if (tm + 1) % RUN == 0 else zh
                outside.append((last, device(zh, 0, tm + 1)))
                rims.append((last, device(near, 0, tm + 1)))
    outside = outside + [(b, a) for a, b in outside]
    rims = rims + [(b, a) for a, b in rims]

    def per_device(signal, spatial, temporal, activations, threshold, step_size):
        half = lax.axis_index("c").astype(jnp.int32)
        place = lax.axis_index("y").astype(jnp.int32) * 2 + half
        time_block = lax.axis_index("tm").astype(jnp.int32)
        width = activations.shape[1]
        spatial = spatial.T
        high = lax.reduce_precision(spatial, 8, 7)
        parts = jnp.concatenate([high, spatial - high], axis=0).astype(jnp.bfloat16)
        away, kept = project(half[None], parts, signal)
        summed = kept + lax.ppermute(away, "c", swap)

        activations, summed = lax.optimization_barrier((activations, summed))
        pieces = lax.all_to_all(summed, "y", 0, 0, tiled=True)
        *before_steps, rim = rebuild(place[None], temporal, activations)
        rim = lax.ppermute(rim, line, rims)
        group_sum = jnp.sum(pieces, axis=0)
        group_sum, before_steps = lax.optimization_barrier((group_sum, before_steps))
        mine = jnp.sum(lax.all_gather(group_sum, "zh", axis=0), axis=0)

        first = half == 0
        start, end, gram = mine[: BODY // 2], mine[BODY // 2 : BODY], mine[BODY:]
        outer = jnp.concatenate([jnp.where(first, start, end), gram], axis=0)
        outer = lax.ppermute(outer, line, outside)
        inner = jnp.concatenate([jnp.where(first, end, start), gram], axis=0)
        inner = lax.ppermute(inner, "c", swap)
        begin = time_block * width + place * CHUNK
        update = steps(
            blocks * width, begin[None], place[None], step_size, mine, inner, outer, rim,
            before_steps, temporal, threshold[None, :],
        )

        gathered = lax.all_to_all(update, "y", 0, 0, tiled=True)
        other = lax.ppermute(gathered, "c", swap)
        return place_half(half[None], other, place_half(half[None], gathered))

    chan = ("zh", "y", "c")
    in_specs = (P(chan, "tm"), P(chan, None), P(), P(None, "tm"), P(), P())
    return jax.shard_map(
        per_device, mesh=split, in_specs=in_specs, out_specs=P(None, "tm"), check_vma=False
    )
```

```python
import jax
import jax.numpy as jnp
from jax import lax
from jax.experimental import pallas as pl
from jax.experimental.pallas import tpu as pltpu
from jax.sharding import Mesh, PartitionSpec as P

ATOMS = 64
LENGTH = 128
CHUNK = 512
CHUNKS = 8
QUARTER = 4
LANES = 2 * ATOMS
TILES = CHUNK // LANES
BODY = TILES * ATOMS
ROWS = BODY + 16
RIM = LANES + ATOMS
NARROW, WIDE = 48, 56
RUN = 8
HIGHEST = lax.Precision.HIGHEST
F32 = jnp.float32
VMEM = pl.BlockSpec(memory_space=pltpu.VMEM)
SMEM = pl.BlockSpec(memory_space=pltpu.SMEM)
ANY = pl.BlockSpec(memory_space=pl.ANY)


def cost(flops, bytes_accessed):
    return pl.CostEstimate(flops=flops, bytes_accessed=bytes_accessed, transcendentals=0)


def params(mebibytes):
    return pltpu.CompilerParams(vmem_limit_bytes=mebibytes * 2**20)


def split_body(spatial_ref, parts_ref):
    spatial = spatial_ref[...]
    high = spatial.astype(jnp.bfloat16)
    parts_ref[:ATOMS] = high
    parts_ref[ATOMS:] = (spatial - high.astype(F32)).astype(jnp.bfloat16)


def two_parts(spatial):
    rows, channels = spatial.shape
    return pl.pallas_call(
        split_body,
        in_specs=[VMEM],
        out_specs=VMEM,
        out_shape=jax.ShapeDtypeStruct((2 * rows, channels), jnp.bfloat16),
        compiler_params=params(8),
        cost_estimate=cost(2**30, 2**17),
    )(spatial)


def project_body(half_ref, parts_ref, signal_ref, away_ref, kept_ref):
    first = half_ref[0] == 0
    parts = parts_ref[...]
    gram = lax.dot_general(parts, parts, (((1,), (1,)), ((), ())), preferred_element_type=F32)
    gram = gram[:ATOMS] + gram[ATOMS:]
    gram = gram[:, :ATOMS] + gram[:, ATOMS:]
    upper = jnp.concatenate([gram[:16], gram[16:32]], axis=1)
    lower = jnp.concatenate([gram[32:48], gram[48:]], axis=1)
    away_gram, kept_gram = jnp.where(first, lower, upper), jnp.where(first, upper, lower)
    for i in range(QUARTER):
        away_ref[i, BODY:] = away_gram
        kept_ref[i, BODY:] = kept_gram
    for out_ref, which in ((away_ref, 1 - half_ref[0]), (kept_ref, half_ref[0])):
        for i in range(QUARTER):
            column = pl.multiple_of((2 * i + which) * CHUNK, CHUNK)
            product = jnp.dot(
                parts, signal_ref[:, pl.ds(column, CHUNK)], preferred_element_type=F32
            )
            product = product[:ATOMS] + product[ATOMS:]
            for t in range(TILES):
                out_ref[i, t * ATOMS : (t + 1) * ATOMS] = product[:, t * LANES : (t + 1) * LANES]


def project(half, parts, signal):
    channels, width = signal.shape
    return pl.pallas_call(
        project_body,
        in_specs=[SMEM, VMEM, VMEM],
        out_specs=[VMEM, VMEM],
        out_shape=[jax.ShapeDtypeStruct((QUARTER, ROWS, LANES), F32)] * 2,
        compiler_params=params(8),
        cost_estimate=cost(2 * channels * LANES * width, 2 * channels * width),
    )(half, parts, signal)


def to_segments(rows, segment, out_ref):
    for s in range(8):
        out_ref[pl.ds(s, segment, stride=8)] = rows[s * segment : (s + 1) * segment]


def from_segments(ref, segment):
    return jnp.concatenate([ref[pl.ds(s, segment, stride=8)] for s in range(8)], axis=0)


def spread_taps(temporal_ref, taps_ref):
    temporal = temporal_ref[...]
    columns = jnp.concatenate([temporal, temporal], axis=0).T
    for i in range(LENGTH // 4):
        c0, c1, c2, c3 = (
            jnp.broadcast_to(columns[4 * i + p : 4 * i + p + 1], (8, LANES)) for p in range(4)
        )
        even, odd = c0 + c1, c2 + c3
        for k, tap in enumerate((c0, c0 + c2, c2, even, even + odd, odd, c1, c1 + c3, c3)):
            taps_ref[k, i] = tap


def lane_half():
    return lax.broadcasted_iota(jnp.int32, (1, 8, LANES), 2) // ATOMS


def sublane():
    return lax.broadcasted_iota(jnp.int32, (1, 8, LANES), 1)


def later_segment(rows):
    up = pltpu.roll(rows, 7, 1)
    return jnp.where(sublane() == 7, pltpu.roll(up, ATOMS, 2), up)


def earlier_segment(rows):
    down = pltpu.roll(rows, 1, 1)
    return jnp.where(sublane() == 0, pltpu.roll(down, ATOMS, 2), down)


def over_sublanes(rows):
    count = rows.shape[0]
    return jnp.broadcast_to(rows.reshape(count, 1, LANES), (count, 8, LANES))


def spread_later(rows, spread_ref, beyond=None):
    segment = rows.shape[0]
    reach = segment + LENGTH
    for first in range(0, reach, segment):
        count = min(segment, reach - first)
        rows = rows[:count]
        if first > 0:
            rows = later_segment(rows)
            if beyond is not None:
                last = (sublane() == 7) & (lane_half() == 1)
                start = first - segment
                rows = jnp.where(last, over_sublanes(beyond[start : start + count]), rows)
        spread_ref[first // 4 : (first + count) // 4] = rows.reshape(count // 4, 4, 8, LANES)


def spread_earlier(rows, spread_ref, before=None):
    segment = rows.shape[0]
    start = LENGTH
    while True:
        skip = max(0, -start)
        first, count = start + skip, segment - skip
        kept = rows[skip:]
        spread_ref[first // 4 : (first + count) // 4] = kept.reshape(count // 4, 4, 8, LANES)
        if start <= 0:
            return
        rows = earlier_segment(rows)
        start -= segment
        if before is not None:
            skip = max(0, -start)
            rim = over_sublanes(before[start + skip : start + segment])
            if skip:
                rim = jnp.concatenate([jnp.zeros((skip, 8, LANES), F32), rim], axis=0)
            rows = jnp.where((sublane() == 0) & (lane_half() == 0), rim, rows)


def short_inputs(segment, spread_ref, inputs_ref, offset):
    count = (segment + LENGTH) // 4 - 1

    def x(p):
        p = p + offset
        return spread_ref[p // 4 : p // 4 + count, p % 4]

    x0, x1, x2, x3, x4, x5, x6 = (x(p) for p in range(7))
    inputs_ref[0, :count] = (x0 - x1) - (x2 - x3)
    inputs_ref[1, :count] = x2 - x3
    inputs_ref[2, :count] = (x4 - x5) - (x2 - x3)
    inputs_ref[3, :count] = x1 - x3
    inputs_ref[4, :count] = x3
    inputs_ref[5, :count] = x5 - x3
    inputs_ref[6, :count] = (x2 - x1) - (x4 - x3)
    inputs_ref[7, :count] = x4 - x3
    inputs_ref[8, :count] = (x6 - x5) - (x4 - x3)


def filter_rows(segment, inputs_ref, taps_ref, sums_ref, reverse):
    taps = LENGTH // 4
    phase = segment // 4

    @pl.loop(0, 9, unroll=3)
    def _(k):
        sums = [None] * phase
        held = {}
        for j in range(phase + taps - 1):
            if j < taps:
                held[j] = taps_ref[8 - k, taps - 1 - j] if reverse else taps_ref[k, j]
            value = inputs_ref[k, j]
            for m in range(max(0, j - phase + 1), min(taps, j + 1)):
                term = value * held[m]
                sums[j - m] = term if sums[j - m] is None else sums[j - m] + term
        for i in range(phase):
            sums_ref[k, i] = sums[i]

    def total(i, k):
        return sums_ref[i, :phase] + sums_ref[k, :phase]

    a, b, c = total(0, 1), total(3, 4), total(6, 7)
    d, e, f = total(1, 2), total(4, 5), total(7, 8)
    rows = jnp.stack([a + b, b + c, d + e, e + f], axis=1)
    return rows.reshape(segment, 8, LANES)


def filter_scratch(segment):
    reach = (segment + LENGTH) // 4
    return [
        pltpu.VMEM((9, LENGTH // 4, 8, LANES), F32),
        pltpu.VMEM((reach, 4, 8, LANES), F32),
        pltpu.VMEM((9, reach, 8, LANES), F32),
        pltpu.VMEM((9, segment // 4, 8, LANES), F32),
    ]


def rebuild_body(
    place_ref, temporal_ref, before_ref, first_ref, second_ref, after_ref,
    rebuilt_ref, beyond_ref, point_ref, rim_ref, taps_ref, spread_ref, inputs_ref, sums_ref, wide_ref,
):
    place = place_ref[0]
    spread_taps(temporal_ref, taps_ref)
    before = jnp.where(place == 0, 0.0, before_ref[...])
    after = jnp.where(place == CHUNKS - 1, 0.0, after_ref[...])
    first, second = first_ref[...], second_ref[...]
    upper = jnp.concatenate([before[:, 128:], first], axis=1)
    lower = jnp.concatenate([second, after[:, :128]], axis=1)
    to_segments(jnp.concatenate([upper, lower], axis=0).T, NARROW, point_ref)

    upper = jnp.concatenate([upper, second[:, :128]], axis=1)
    lower = jnp.concatenate([second[:, 64:], after, after[:, :64]], axis=1)
    to_segments(jnp.concatenate([upper, lower], axis=0).T, WIDE, wide_ref)
    ahead = before[:, :128]
    ahead = jnp.concatenate([ahead, ahead], axis=0).T
    spread_earlier(wide_ref[...].reshape(WIDE, 8, LANES), spread_ref, ahead)
    short_inputs(WIDE, spread_ref, inputs_ref, 1)
    rebuilt = filter_rows(WIDE, inputs_ref, taps_ref, sums_ref, True)

    wide_ref[...] = rebuilt.reshape(8 * WIDE, LANES)
    rows = from_segments(wide_ref, WIDE)
    swapped = pltpu.roll(rows, ATOMS, 1)
    left = lax.broadcasted_iota(jnp.int32, (1, LANES), 1) < ATOMS
    lower = jnp.concatenate([swapped[384:], rows[:320]], axis=0)
    to_segments(jnp.where(left, rows[:384], lower), NARROW, rebuilt_ref)
    beyond_ref[...] = jnp.where(left, swapped[320:], rows[320:])

    starting = place % 2 == 0
    start = jnp.where(left, rows[128:256], swapped[256:384])
    end = jnp.where(left, swapped[64:192], rows[192:320])
    rim_ref[:LANES] = jnp.where(starting, start, end)
    rim_ref[LANES:] = jnp.where(starting, first[:, :128], second[:, 128:])


def rebuild(place, temporal, activations):
    atoms, width = activations.shape
    half = CHUNK // 2
    last = width // half - 1
    block = (atoms, half)
    shapes = [(8 * NARROW, LANES), (LENGTH, LANES), (8 * NARROW, LANES), (RIM, LANES)]
    return pl.pallas_call(
        rebuild_body,
        grid_spec=pltpu.PrefetchScalarGridSpec(
            num_scalar_prefetch=1,
            grid=(1,),
            in_specs=[
                pl.BlockSpec((ATOMS, LENGTH), lambda i, place: (0, 0)),
                pl.BlockSpec(block, lambda i, place: (0, jnp.maximum(2 * place[0] - 1, 0))),
                pl.BlockSpec(block, lambda i, place: (0, 2 * place[0])),
                pl.BlockSpec(block, lambda i, place: (0, 2 * place[0] + 1)),
                pl.BlockSpec(block, lambda i, place: (0, jnp.minimum(2 * place[0] + 2, last))),
            ],
            out_specs=[pl.BlockSpec(shape, lambda i, place: (0, 0)) for shape in shapes],
            scratch_shapes=filter_scratch(WIDE) + [pltpu.VMEM((8 * WIDE, LANES), F32)],
        ),
        out_shape=[jax.ShapeDtypeStruct(shape, F32) for shape in shapes],
        compiler_params=params(12),
        cost_estimate=cost(2 * 8 * WIDE * LANES * LENGTH, 2**20),
    )(place, temporal, activations, activations, activations, activations)


def steps_body(
    total, begin_ref, place_ref, step_ref, mine_ref, inner_ref, outer_ref, rim_ref, rebuilt_ref,
    beyond_ref, point_ref, temporal_ref, threshold_ref, out_ref, taps_ref, spread_ref, inputs_ref,
    sums_ref, cross_ref, side_ref, mix_ref,
):
    begin, place = begin_ref[0], place_ref[0]
    first = place % 2 == 0
    rate = step_ref[0]
    spread_taps(temporal_ref, taps_ref)

    own, other = mine_ref[BODY:], inner_ref[BODY // 2 :]
    upper, lower = jnp.where(first, own, other), jnp.where(first, other, own)
    gram = jnp.concatenate(
        [upper[:, :ATOMS], upper[:, ATOMS:], lower[:, :ATOMS], lower[:, ATOMS:]], axis=0
    )
    mix_ref[...] = jnp.zeros_like(mix_ref)
    mix_ref[:ATOMS, :ATOMS] = gram
    mix_ref[ATOMS:, ATOMS:] = gram

    near, far = slice(0, ATOMS), slice(ATOMS, 2 * ATOMS)
    left = jnp.where(first, outer_ref[far], inner_ref[far])
    right = jnp.where(first, inner_ref[near], outer_ref[near])
    beyond = jnp.where(first, inner_ref[far], outer_ref[far])
    tiles = [mine_ref[t * ATOMS : (t + 1) * ATOMS] for t in range(TILES)]
    upper = jnp.concatenate([left, tiles[0], tiles[1]], axis=1)
    lower = jnp.concatenate([tiles[2], tiles[3], right], axis=1)
    to_segments(jnp.concatenate([upper, lower], axis=0).T, NARROW, cross_ref)
    beyond = jnp.concatenate([beyond, beyond], axis=0).T

    left_half = lax.broadcasted_iota(jnp.int32, (1, LANES), 1) < ATOMS
    at_start = left_half & (place == 0)
    at_end = jnp.logical_not(left_half) & (place == CHUNKS - 1)
    added = rim_ref[:LANES]
    swapped = pltpu.roll(added, ATOMS, 1)
    to_segments(
        jnp.concatenate(
            [
                jnp.where(at_start, added, 0.0),
                jnp.where(at_start, swapped, 0.0),
                jnp.where(at_end, swapped, 0.0),
            ],
            axis=0,
        ),
        NARROW,
        side_ref,
    )
    rebuilt = rebuilt_ref[...] + side_ref[...]
    added_beyond = jnp.where(left_half, swapped, added)
    rebuilt_beyond = beyond_ref[...] + jnp.where(place == CHUNKS - 1, added_beyond, 0.0)
    rim = rim_ref[LANES:]
    rim = jnp.concatenate([rim, rim], axis=0).T
    to_segments(
        jnp.concatenate(
            [jnp.where(at_start, rim, 0.0), jnp.zeros_like(rim), jnp.where(at_end, rim, 0.0)],
            axis=0,
        ),
        NARROW,
        side_ref,
    )

    shape = (NARROW, 8, LANES)
    sample = lax.broadcasted_iota(jnp.int32, shape, 0) + (
        (lane_half() * 8 + sublane()) * NARROW + (begin - LENGTH)
    )
    sample_beyond = lax.broadcasted_iota(jnp.int32, (LENGTH, LANES), 0) + (begin + CHUNK + LENGTH)
    shrink = threshold_ref[...]
    shrink = jnp.concatenate([shrink, shrink], axis=1).reshape(1, 1, LANES)

    def mixed(rebuilt):
        return jnp.dot(rebuilt, mix_ref[...], precision=HIGHEST, preferred_element_type=F32)

    def projected(rebuilt):
        rows = (mixed(rebuilt) - cross_ref[...]).reshape(shape)
        return jnp.where(sample < total, rows, 0.0)

    def stepped(point, rows, rows_beyond=None):
        spread_later(rows, spread_ref, rows_beyond)
        short_inputs(NARROW, spread_ref, inputs_ref, 0)
        gradient = filter_rows(NARROW, inputs_ref, taps_ref, sums_ref, False)
        return jnp.maximum(point - rate * (gradient + shrink), 0.0)

    inertia = 1.0
    inertia_next = (1.0 + (1.0 + 4.0 * inertia * inertia) ** 0.5) / 2.0
    momentum = (inertia - 1.0) / inertia_next
    previous = (point_ref[...] + side_ref[...]).reshape(shape)
    beyond = jnp.where(sample_beyond < total, mixed(rebuilt_beyond) - beyond, 0.0)
    update = stepped(previous, projected(rebuilt), beyond)
    point = update + momentum * (update - previous)
    point = jnp.where(sample >= 0, point, 0.0)

    spread_earlier(point, spread_ref)
    short_inputs(NARROW, spread_ref, inputs_ref, 1)
    rebuilt = filter_rows(NARROW, inputs_ref, taps_ref, sums_ref, True)
    update = stepped(point, projected(rebuilt.reshape(8 * NARROW, LANES)))

    cross_ref[...] = update.reshape(8 * NARROW, LANES)
    columns = from_segments(cross_ref, NARROW).T
    for i in range(QUARTER):
        out_ref[i] = jnp.concatenate([columns[:ATOMS, 128:], columns[ATOMS:, :256]], axis=1)


def steps(
    total, begin, place, step_size, mine, inner, outer, rim, before_steps, temporal, threshold
):
    def body(*refs):
        steps_body(total, *refs)

    return pl.pallas_call(
        body,
        in_specs=[SMEM] * 3 + [VMEM] * 9,
        out_specs=VMEM,
        out_shape=jax.ShapeDtypeStruct((QUARTER, ATOMS, CHUNK), F32),
        scratch_shapes=filter_scratch(NARROW)
        + [pltpu.VMEM((8 * NARROW, LANES), F32)] * 2
        + [pltpu.VMEM((LANES, LANES), F32)],
        compiler_params=params(12),
        cost_estimate=cost(6 * 8 * NARROW * LANES * LENGTH, 2**20),
    )(begin, place, step_size, mine, inner, outer, rim, *before_steps, temporal, threshold)


def place_copies(half, chunks_ref, out_ref, sems):
    copies = []
    for i in range(QUARTER):
        column = pl.multiple_of((2 * i + half) * CHUNK, CHUNK)
        copies.append(
            pltpu.make_async_copy(chunks_ref.at[i], out_ref.at[:, pl.ds(column, CHUNK)], sems.at[i])
        )
    for copy in copies:
        copy.start()
    for copy in copies:
        copy.wait()


def place_mine_body(half_ref, chunks_ref, out_ref, sems):
    place_copies(half_ref[0], chunks_ref, out_ref, sems)


def place_other_body(half_ref, chunks_ref, begun_ref, out_ref, sems):
    place_copies(1 - half_ref[0], chunks_ref, out_ref, sems)


def place_half(half, chunks, begun=None):
    out_shape = jax.ShapeDtypeStruct((ATOMS, CHUNKS * CHUNK), F32)
    first = begun is None
    return pl.pallas_call(
        place_mine_body if first else place_other_body,
        in_specs=[SMEM, ANY] + ([] if first else [ANY]),
        out_specs=ANY,
        out_shape=out_shape,
        scratch_shapes=[pltpu.SemaphoreType.DMA((QUARTER,))],
        input_output_aliases={} if first else {2: 0},
        compiler_params=params(4),
        cost_estimate=cost(0, 2**20),
    )(half, chunks, *([] if first else [begun]))


def solution(mesh):
    blocks = mesh.shape["tm"]
    split = Mesh(mesh.devices.reshape(2, 4, 2, blocks), ("zh", "y", "c", "tm"))
    swap = [(0, 1), (1, 0)]
    line = ("zh", "y", "c", "tm")

    def device(zh, q, tm):
        return (zh * CHUNKS + q) * blocks + tm

    outside, rims = [], []
    for zh in range(2):
        for tm in range(blocks):
            for q in range(1, CHUNKS - 1, 2):
                outside.append((device(zh, q, tm), device(zh, q + 1, tm)))
            if tm + 1 < blocks:
                last = device(zh, CHUNKS - 1, tm)
                near = 1 - zh if (tm + 1) % RUN == 0 else zh
                outside.append((last, device(zh, 0, tm + 1)))
                rims.append((last, device(near, 0, tm + 1)))
    outside = outside + [(b, a) for a, b in outside]
    rims = rims + [(b, a) for a, b in rims]

    def per_device(signal, spatial, temporal, activations, threshold, step_size):
        half = lax.axis_index("c").astype(jnp.int32)
        place = lax.axis_index("y").astype(jnp.int32) * 2 + half
        time_block = lax.axis_index("tm").astype(jnp.int32)
        width = activations.shape[1]
        parts = two_parts(spatial.T)
        away, kept = project(half[None], parts, signal)
        summed = kept + lax.ppermute(away, "c", swap)

        activations, summed = lax.optimization_barrier((activations, summed))
        pieces = lax.all_to_all(summed, "y", 0, 0, tiled=True)
        *before_steps, rim = rebuild(place[None], temporal, activations)
        rim = lax.ppermute(rim, line, rims)
        group_sum = jnp.sum(pieces, axis=0)
        group_sum, before_steps = lax.optimization_barrier((group_sum, before_steps))
        mine = jnp.sum(lax.all_gather(group_sum, "zh", axis=0), axis=0)

        first = half == 0
        start, end, gram = mine[: BODY // 2], mine[BODY // 2 : BODY], mine[BODY:]
        outer = jnp.concatenate([jnp.where(first, start, end), gram], axis=0)
        outer = lax.ppermute(outer, line, outside)
        inner = jnp.concatenate([jnp.where(first, end, start), gram], axis=0)
        inner = lax.ppermute(inner, "c", swap)
        begin = time_block * width + place * CHUNK
        update = steps(
            blocks * width, begin[None], place[None], step_size, mine, inner, outer, rim,
            before_steps, temporal, threshold[None, :],
        )

        gathered = lax.all_to_all(update, "y", 0, 0, tiled=True)
        other = lax.ppermute(gathered, "c", swap)
        return place_half(half[None], other, place_half(half[None], gathered))

    chan = ("zh", "y", "c")
    in_specs = (P(chan, "tm"), P(chan, None), P(), P(None, "tm"), P(), P())
    return jax.shard_map(
        per_device, mesh=split, in_specs=in_specs, out_specs=P(None, "tm"), check_vma=False
    )
```

```python
import jax
import jax.numpy as jnp
from jax import lax
from jax.experimental import pallas as pl
from jax.experimental.pallas import tpu as pltpu
from jax.sharding import Mesh, PartitionSpec as P

ATOMS = 64
LENGTH = 128
CHUNK = 512
CHUNKS = 8
QUARTER = 4
LANES = 2 * ATOMS
TILES = CHUNK // LANES
BODY = TILES * ATOMS
ROWS = BODY + 16
RIM = LANES + ATOMS
NARROW, WIDE = 48, 56
RUN = 8
HIGHEST = lax.Precision.HIGHEST
F32 = jnp.float32
VMEM = pl.BlockSpec(memory_space=pltpu.VMEM)
SMEM = pl.BlockSpec(memory_space=pltpu.SMEM)
ANY = pl.BlockSpec(memory_space=pl.ANY)


def cost(flops, bytes_accessed):
    return pl.CostEstimate(flops=flops, bytes_accessed=bytes_accessed, transcendentals=0)


def params(mebibytes):
    return pltpu.CompilerParams(vmem_limit_bytes=mebibytes * 2**20)


def split_body(spatial_ref, parts_ref, gram_ref):
    spatial = spatial_ref[...]
    high = spatial.astype(jnp.bfloat16)
    low = (spatial - high.astype(F32)).astype(jnp.bfloat16)
    parts = jnp.concatenate([high, low], axis=0)
    parts_ref[...] = parts
    gram = lax.dot_general(parts, parts, (((1,), (1,)), ((), ())), preferred_element_type=F32)
    gram = gram[:ATOMS] + gram[ATOMS:]
    gram = gram[:, :ATOMS] + gram[:, ATOMS:]
    gram_ref[0] = jnp.concatenate([gram[:16], gram[16:32]], axis=1)
    gram_ref[1] = jnp.concatenate([gram[32:48], gram[48:]], axis=1)


def two_parts(spatial):
    rows, channels = spatial.shape
    return pl.pallas_call(
        split_body,
        in_specs=[VMEM],
        out_specs=[VMEM, VMEM],
        out_shape=[
            jax.ShapeDtypeStruct((2 * rows, channels), jnp.bfloat16),
            jax.ShapeDtypeStruct((2, 16, LANES), F32),
        ],
        compiler_params=params(8),
        cost_estimate=cost(2**30, 2**17),
    )(spatial)


def project_body(half_ref, parts_ref, gram_ref, signal_ref, away_ref, kept_ref):
    first = half_ref[0] == 0
    parts = parts_ref[...]
    upper, lower = gram_ref[0], gram_ref[1]
    away_gram, kept_gram = jnp.where(first, lower, upper), jnp.where(first, upper, lower)
    for i in range(QUARTER):
        away_ref[i, BODY:] = away_gram
        kept_ref[i, BODY:] = kept_gram
    for out_ref, which in ((away_ref, 1 - half_ref[0]), (kept_ref, half_ref[0])):
        for i in range(QUARTER):
            column = pl.multiple_of((2 * i + which) * CHUNK, CHUNK)
            product = jnp.dot(
                parts, signal_ref[:, pl.ds(column, CHUNK)], preferred_element_type=F32
            )
            product = product[:ATOMS] + product[ATOMS:]
            for t in range(TILES):
                out_ref[i, t * ATOMS : (t + 1) * ATOMS] = product[:, t * LANES : (t + 1) * LANES]


def project(half, parts, gram, signal):
    channels, width = signal.shape
    return pl.pallas_call(
        project_body,
        in_specs=[SMEM, VMEM, VMEM, VMEM],
        out_specs=[VMEM, VMEM],
        out_shape=[jax.ShapeDtypeStruct((QUARTER, ROWS, LANES), F32)] * 2,
        compiler_params=params(8),
        cost_estimate=cost(2 * channels * LANES * width, 2 * channels * width),
    )(half, parts, gram, signal)


def to_segments(rows, segment, out_ref):
    for s in range(8):
        out_ref[pl.ds(s, segment, stride=8)] = rows[s * segment : (s + 1) * segment]


def from_segments(ref, segment):
    return jnp.concatenate([ref[pl.ds(s, segment, stride=8)] for s in range(8)], axis=0)


def spread_taps(temporal_ref, taps_ref):
    temporal = temporal_ref[...]
    columns = jnp.concatenate([temporal, temporal], axis=0).T
    for i in range(LENGTH // 4):
        c0, c1, c2, c3 = (
            jnp.broadcast_to(columns[4 * i + p : 4 * i + p + 1], (8, LANES)) for p in range(4)
        )
        even, odd = c0 + c1, c2 + c3
        for k, tap in enumerate((c0, c0 + c2, c2, even, even + odd, odd, c1, c1 + c3, c3)):
            taps_ref[k, i] = tap


def lane_half():
    return lax.broadcasted_iota(jnp.int32, (1, 8, LANES), 2) // ATOMS


def sublane():
    return lax.broadcasted_iota(jnp.int32, (1, 8, LANES), 1)


def later_segment(rows):
    up = pltpu.roll(rows, 7, 1)
    return jnp.where(sublane() == 7, pltpu.roll(up, ATOMS, 2), up)


def earlier_segment(rows):
    down = pltpu.roll(rows, 1, 1)
    return jnp.where(sublane() == 0, pltpu.roll(down, ATOMS, 2), down)


def over_sublanes(rows):
    count = rows.shape[0]
    return jnp.broadcast_to(rows.reshape(count, 1, LANES), (count, 8, LANES))


def spread_later(rows, spread_ref, beyond=None):
    segment = rows.shape[0]
    reach = segment + LENGTH
    for first in range(0, reach, segment):
        count = min(segment, reach - first)
        rows = rows[:count]
        if first > 0:
            rows = later_segment(rows)
            if beyond is not None:
                last = (sublane() == 7) & (lane_half() == 1)
                start = first - segment
                rows = jnp.where(last, over_sublanes(beyond[start : start + count]), rows)
        spread_ref[first // 4 : (first + count) // 4] = rows.reshape(count // 4, 4, 8, LANES)


def spread_earlier(rows, spread_ref, before=None):
    segment = rows.shape[0]
    start = LENGTH
    while True:
        skip = max(0, -start)
        first, count = start + skip, segment - skip
        kept = rows[skip:]
        spread_ref[first // 4 : (first + count) // 4] = kept.reshape(count // 4, 4, 8, LANES)
        if start <= 0:
            return
        rows = earlier_segment(rows)
        start -= segment
        if before is not None:
            skip = max(0, -start)
            rim = over_sublanes(before[start + skip : start + segment])
            if skip:
                rim = jnp.concatenate([jnp.zeros((skip, 8, LANES), F32), rim], axis=0)
            rows = jnp.where((sublane() == 0) & (lane_half() == 0), rim, rows)


def short_inputs(segment, spread_ref, inputs_ref, offset):
    count = (segment + LENGTH) // 4 - 1

    def x(p):
        p = p + offset
        return spread_ref[p // 4 : p // 4 + count, p % 4]

    x0, x1, x2, x3, x4, x5, x6 = (x(p) for p in range(7))
    inputs_ref[0, :count] = (x0 - x1) - (x2 - x3)
    inputs_ref[1, :count] = x2 - x3
    inputs_ref[2, :count] = (x4 - x5) - (x2 - x3)
    inputs_ref[3, :count] = x1 - x3
    inputs_ref[4, :count] = x3
    inputs_ref[5, :count] = x5 - x3
    inputs_ref[6, :count] = (x2 - x1) - (x4 - x3)
    inputs_ref[7, :count] = x4 - x3
    inputs_ref[8, :count] = (x6 - x5) - (x4 - x3)


def filter_rows(segment, inputs_ref, taps_ref, sums_ref, reverse):
    taps = LENGTH // 4
    phase = segment // 4

    @pl.loop(0, 9, unroll=3)
    def _(k):
        sums = [None] * phase
        held = {}
        for j in range(phase + taps - 1):
            if j < taps:
                held[j] = taps_ref[8 - k, taps - 1 - j] if reverse else taps_ref[k, j]
            value = inputs_ref[k, j]
            for m in range(max(0, j - phase + 1), min(taps, j + 1)):
                term = value * held[m]
                sums[j - m] = term if sums[j - m] is None else sums[j - m] + term
        for i in range(phase):
            sums_ref[k, i] = sums[i]

    def total(i, k):
        return sums_ref[i, :phase] + sums_ref[k, :phase]

    a, b, c = total(0, 1), total(3, 4), total(6, 7)
    d, e, f = total(1, 2), total(4, 5), total(7, 8)
    rows = jnp.stack([a + b, b + c, d + e, e + f], axis=1)
    return rows.reshape(segment, 8, LANES)


def filter_scratch(segment):
    reach = (segment + LENGTH) // 4
    return [
        pltpu.VMEM((9, LENGTH // 4, 8, LANES), F32),
        pltpu.VMEM((reach, 4, 8, LANES), F32),
        pltpu.VMEM((9, reach, 8, LANES), F32),
        pltpu.VMEM((9, segment // 4, 8, LANES), F32),
    ]


def rebuild_body(
    place_ref, temporal_ref, before_ref, first_ref, second_ref, after_ref,
    rebuilt_ref, beyond_ref, point_ref, rim_ref, taps_ref, spread_ref, inputs_ref, sums_ref, wide_ref,
):
    place = place_ref[0]
    spread_taps(temporal_ref, taps_ref)
    before = jnp.where(place == 0, 0.0, before_ref[...])
    after = jnp.where(place == CHUNKS - 1, 0.0, after_ref[...])
    first, second = first_ref[...], second_ref[...]
    upper = jnp.concatenate([before[:, 128:], first], axis=1)
    lower = jnp.concatenate([second, after[:, :128]], axis=1)
    to_segments(jnp.concatenate([upper, lower], axis=0).T, NARROW, point_ref)

    upper = jnp.concatenate([upper, second[:, :128]], axis=1)
    lower = jnp.concatenate([second[:, 64:], after, after[:, :64]], axis=1)
    to_segments(jnp.concatenate([upper, lower], axis=0).T, WIDE, wide_ref)
    ahead = before[:, :128]
    ahead = jnp.concatenate([ahead, ahead], axis=0).T
    spread_earlier(wide_ref[...].reshape(WIDE, 8, LANES), spread_ref, ahead)
    short_inputs(WIDE, spread_ref, inputs_ref, 1)
    rebuilt = filter_rows(WIDE, inputs_ref, taps_ref, sums_ref, True)

    wide_ref[...] = rebuilt.reshape(8 * WIDE, LANES)
    rows = from_segments(wide_ref, WIDE)
    swapped = pltpu.roll(rows, ATOMS, 1)
    left = lax.broadcasted_iota(jnp.int32, (1, LANES), 1) < ATOMS
    lower = jnp.concatenate([swapped[384:], rows[:320]], axis=0)
    to_segments(jnp.where(left, rows[:384], lower), NARROW, rebuilt_ref)
    beyond_ref[...] = jnp.where(left, swapped[320:], rows[320:])

    starting = place % 2 == 0
    start = jnp.where(left, rows[128:256], swapped[256:384])
    end = jnp.where(left, swapped[64:192], rows[192:320])
    rim_ref[:LANES] = jnp.where(starting, start, end)
    rim_ref[LANES:] = jnp.where(starting, first[:, :128], second[:, 128:])


def rebuild(place, temporal, activations):
    atoms, width = activations.shape
    half = CHUNK // 2
    last = width // half - 1
    block = (atoms, half)
    shapes = [(8 * NARROW, LANES), (LENGTH, LANES), (8 * NARROW, LANES), (RIM, LANES)]
    return pl.pallas_call(
        rebuild_body,
        grid_spec=pltpu.PrefetchScalarGridSpec(
            num_scalar_prefetch=1,
            grid=(1,),
            in_specs=[
                pl.BlockSpec((ATOMS, LENGTH), lambda i, place: (0, 0)),
                pl.BlockSpec(block, lambda i, place: (0, jnp.maximum(2 * place[0] - 1, 0))),
                pl.BlockSpec(block, lambda i, place: (0, 2 * place[0])),
                pl.BlockSpec(block, lambda i, place: (0, 2 * place[0] + 1)),
                pl.BlockSpec(block, lambda i, place: (0, jnp.minimum(2 * place[0] + 2, last))),
            ],
            out_specs=[pl.BlockSpec(shape, lambda i, place: (0, 0)) for shape in shapes],
            scratch_shapes=filter_scratch(WIDE) + [pltpu.VMEM((8 * WIDE, LANES), F32)],
        ),
        out_shape=[jax.ShapeDtypeStruct(shape, F32) for shape in shapes],
        compiler_params=params(12),
        cost_estimate=cost(2 * 8 * WIDE * LANES * LENGTH, 2**20),
    )(place, temporal, activations, activations, activations, activations)


def steps_body(
    total, begin_ref, place_ref, step_ref, mine_ref, inner_ref, outer_ref, rim_ref, rebuilt_ref,
    beyond_ref, point_ref, temporal_ref, threshold_ref, out_ref, taps_ref, spread_ref, inputs_ref,
    sums_ref, cross_ref, side_ref, mix_ref,
):
    begin, place = begin_ref[0], place_ref[0]
    first = place % 2 == 0
    rate = step_ref[0]
    spread_taps(temporal_ref, taps_ref)

    own, other = mine_ref[BODY:], inner_ref[BODY // 2 :]
    upper, lower = jnp.where(first, own, other), jnp.where(first, other, own)
    gram = jnp.concatenate(
        [upper[:, :ATOMS], upper[:, ATOMS:], lower[:, :ATOMS], lower[:, ATOMS:]], axis=0
    )
    mix_ref[...] = jnp.zeros_like(mix_ref)
    mix_ref[:ATOMS, :ATOMS] = gram
    mix_ref[ATOMS:, ATOMS:] = gram

    near, far = slice(0, ATOMS), slice(ATOMS, 2 * ATOMS)
    left = jnp.where(first, outer_ref[far], inner_ref[far])
    right = jnp.where(first, inner_ref[near], outer_ref[near])
    beyond = jnp.where(first, inner_ref[far], outer_ref[far])
    tiles = [mine_ref[t * ATOMS : (t + 1) * ATOMS] for t in range(TILES)]
    upper = jnp.concatenate([left, tiles[0], tiles[1]], axis=1)
    lower = jnp.concatenate([tiles[2], tiles[3], right], axis=1)
    to_segments(jnp.concatenate([upper, lower], axis=0).T, NARROW, cross_ref)
    beyond = jnp.concatenate([beyond, beyond], axis=0).T

    left_half = lax.broadcasted_iota(jnp.int32, (1, LANES), 1) < ATOMS
    at_start = left_half & (place == 0)
    at_end = jnp.logical_not(left_half) & (place == CHUNKS - 1)
    added = rim_ref[:LANES]
    swapped = pltpu.roll(added, ATOMS, 1)
    to_segments(
        jnp.concatenate(
            [
                jnp.where(at_start, added, 0.0),
                jnp.where(at_start, swapped, 0.0),
                jnp.where(at_end, swapped, 0.0),
            ],
            axis=0,
        ),
        NARROW,
        side_ref,
    )
    rebuilt = rebuilt_ref[...] + side_ref[...]
    added_beyond = jnp.where(left_half, swapped, added)
    rebuilt_beyond = beyond_ref[...] + jnp.where(place == CHUNKS - 1, added_beyond, 0.0)
    rim = rim_ref[LANES:]
    rim = jnp.concatenate([rim, rim], axis=0).T
    to_segments(
        jnp.concatenate(
            [jnp.where(at_start, rim, 0.0), jnp.zeros_like(rim), jnp.where(at_end, rim, 0.0)],
            axis=0,
        ),
        NARROW,
        side_ref,
    )

    shape = (NARROW, 8, LANES)
    sample = lax.broadcasted_iota(jnp.int32, shape, 0) + (
        (lane_half() * 8 + sublane()) * NARROW + (begin - LENGTH)
    )
    sample_beyond = lax.broadcasted_iota(jnp.int32, (LENGTH, LANES), 0) + (begin + CHUNK + LENGTH)
    shrink = threshold_ref[...]
    shrink = jnp.concatenate([shrink, shrink], axis=1).reshape(1, 1, LANES)

    def mixed(rebuilt):
        return jnp.dot(rebuilt, mix_ref[...], precision=HIGHEST, preferred_element_type=F32)

    def projected(rebuilt):
        rows = (mixed(rebuilt) - cross_ref[...]).reshape(shape)
        return jnp.where(sample < total, rows, 0.0)

    def stepped(point, rows, rows_beyond=None):
        spread_later(rows, spread_ref, rows_beyond)
        short_inputs(NARROW, spread_ref, inputs_ref, 0)
        gradient = filter_rows(NARROW, inputs_ref, taps_ref, sums_ref, False)
        return jnp.maximum(point - rate * (gradient + shrink), 0.0)

    inertia = 1.0
    inertia_next = (1.0 + (1.0 + 4.0 * inertia * inertia) ** 0.5) / 2.0
    momentum = (inertia - 1.0) / inertia_next
    previous = (point_ref[...] + side_ref[...]).reshape(shape)
    beyond = jnp.where(sample_beyond < total, mixed(rebuilt_beyond) - beyond, 0.0)
    update = stepped(previous, projected(rebuilt), beyond)
    point = update + momentum * (update - previous)
    point = jnp.where(sample >= 0, point, 0.0)

    spread_earlier(point, spread_ref)
    short_inputs(NARROW, spread_ref, inputs_ref, 1)
    rebuilt = filter_rows(NARROW, inputs_ref, taps_ref, sums_ref, True)
    update = stepped(point, projected(rebuilt.reshape(8 * NARROW, LANES)))

    cross_ref[...] = update.reshape(8 * NARROW, LANES)
    columns = from_segments(cross_ref, NARROW).T
    for i in range(QUARTER):
        out_ref[i] = jnp.concatenate([columns[:ATOMS, 128:], columns[ATOMS:, :256]], axis=1)


def steps(
    total, begin, place, step_size, mine, inner, outer, rim, before_steps, temporal, threshold
):
    def body(*refs):
        steps_body(total, *refs)

    return pl.pallas_call(
        body,
        in_specs=[SMEM] * 3 + [VMEM] * 9,
        out_specs=VMEM,
        out_shape=jax.ShapeDtypeStruct((QUARTER, ATOMS, CHUNK), F32),
        scratch_shapes=filter_scratch(NARROW)
        + [pltpu.VMEM((8 * NARROW, LANES), F32)] * 2
        + [pltpu.VMEM((LANES, LANES), F32)],
        compiler_params=params(12),
        cost_estimate=cost(6 * 8 * NARROW * LANES * LENGTH, 2**20),
    )(begin, place, step_size, mine, inner, outer, rim, *before_steps, temporal, threshold)


def place_copies(half, chunks_ref, out_ref, sems):
    copies = []
    for i in range(QUARTER):
        column = pl.multiple_of((2 * i + half) * CHUNK, CHUNK)
        copies.append(
            pltpu.make_async_copy(chunks_ref.at[i], out_ref.at[:, pl.ds(column, CHUNK)], sems.at[i])
        )
    for copy in copies:
        copy.start()
    for copy in copies:
        copy.wait()


def place_mine_body(half_ref, chunks_ref, out_ref, sems):
    place_copies(half_ref[0], chunks_ref, out_ref, sems)


def place_other_body(half_ref, chunks_ref, begun_ref, out_ref, sems):
    place_copies(1 - half_ref[0], chunks_ref, out_ref, sems)


def place_half(half, chunks, begun=None):
    out_shape = jax.ShapeDtypeStruct((ATOMS, CHUNKS * CHUNK), F32)
    first = begun is None
    return pl.pallas_call(
        place_mine_body if first else place_other_body,
        in_specs=[SMEM, ANY] + ([] if first else [ANY]),
        out_specs=ANY,
        out_shape=out_shape,
        scratch_shapes=[pltpu.SemaphoreType.DMA((QUARTER,))],
        input_output_aliases={} if first else {2: 0},
        compiler_params=params(4),
        cost_estimate=cost(0, 2**20),
    )(half, chunks, *([] if first else [begun]))


def solution(mesh):
    blocks = mesh.shape["tm"]
    split = Mesh(mesh.devices.reshape(2, 4, 2, blocks), ("zh", "y", "c", "tm"))
    swap = [(0, 1), (1, 0)]
    line = ("zh", "y", "c", "tm")

    def device(zh, q, tm):
        return (zh * CHUNKS + q) * blocks + tm

    outside, rims = [], []
    for zh in range(2):
        for tm in range(blocks):
            for q in range(1, CHUNKS - 1, 2):
                outside.append((device(zh, q, tm), device(zh, q + 1, tm)))
            if tm + 1 < blocks:
                last = device(zh, CHUNKS - 1, tm)
                near = 1 - zh if (tm + 1) % RUN == 0 else zh
                outside.append((last, device(zh, 0, tm + 1)))
                rims.append((last, device(near, 0, tm + 1)))
    outside = outside + [(b, a) for a, b in outside]
    rims = rims + [(b, a) for a, b in rims]

    def per_device(signal, spatial, temporal, activations, threshold, step_size):
        half = lax.axis_index("c").astype(jnp.int32)
        place = lax.axis_index("y").astype(jnp.int32) * 2 + half
        time_block = lax.axis_index("tm").astype(jnp.int32)
        width = activations.shape[1]
        parts, gram_halves = two_parts(spatial.T)
        away, kept = project(half[None], parts, gram_halves, signal)
        summed = kept + lax.ppermute(away, "c", swap)

        activations, summed = lax.optimization_barrier((activations, summed))
        pieces = lax.all_to_all(summed, "y", 0, 0, tiled=True)
        *before_steps, rim = rebuild(place[None], temporal, activations)
        rim = lax.ppermute(rim, line, rims)
        group_sum = jnp.sum(pieces, axis=0)
        group_sum, before_steps = lax.optimization_barrier((group_sum, before_steps))
        mine = jnp.sum(lax.all_gather(group_sum, "zh", axis=0), axis=0)

        first = half == 0
        start, end, gram = mine[: BODY // 2], mine[BODY // 2 : BODY], mine[BODY:]
        outer = jnp.concatenate([jnp.where(first, start, end), gram], axis=0)
        outer = lax.ppermute(outer, line, outside)
        inner = jnp.concatenate([jnp.where(first, end, start), gram], axis=0)
        inner = lax.ppermute(inner, "c", swap)
        begin = time_block * width + place * CHUNK
        update = steps(
            blocks * width, begin[None], place[None], step_size, mine, inner, outer, rim,
            before_steps, temporal, threshold[None, :],
        )

        gathered = lax.all_to_all(update, "y", 0, 0, tiled=True)
        other = lax.ppermute(gathered, "c", swap)
        return place_half(half[None], other, place_half(half[None], gathered))

    chan = ("zh", "y", "c")
    in_specs = (P(chan, "tm"), P(chan, None), P(), P(None, "tm"), P(), P())
    return jax.shard_map(
        per_device, mesh=split, in_specs=in_specs, out_specs=P(None, "tm"), check_vma=False
    )
```

```python
import jax
import jax.numpy as jnp
from jax import lax
from jax.experimental import pallas as pl
from jax.experimental.pallas import tpu as pltpu
from jax.sharding import Mesh, PartitionSpec as P

ATOMS = 64
LENGTH = 128
CHUNK = 512
CHUNKS = 8
QUARTER = 4
LANES = 2 * ATOMS
TILES = CHUNK // LANES
BODY = TILES * ATOMS
ROWS = BODY + 16
RIM = LANES + ATOMS
NARROW, WIDE = 48, 56
RUN = 8
HIGHEST = lax.Precision.HIGHEST
F32 = jnp.float32
VMEM = pl.BlockSpec(memory_space=pltpu.VMEM)
SMEM = pl.BlockSpec(memory_space=pltpu.SMEM)
ANY = pl.BlockSpec(memory_space=pl.ANY)


def cost(flops, bytes_accessed):
    return pl.CostEstimate(flops=flops, bytes_accessed=bytes_accessed, transcendentals=0)


def params(mebibytes):
    return pltpu.CompilerParams(vmem_limit_bytes=mebibytes * 2**20)


def split_body(spatial_ref, parts_ref, gram_ref):
    spatial = spatial_ref[...]
    high = spatial.astype(jnp.bfloat16)
    low = (spatial - high.astype(F32)).astype(jnp.bfloat16)
    parts = jnp.concatenate([high, low], axis=0)
    parts_ref[...] = parts
    gram = lax.dot_general(parts, parts, (((1,), (1,)), ((), ())), preferred_element_type=F32)
    gram = gram[:ATOMS] + gram[ATOMS:]
    gram = gram[:, :ATOMS] + gram[:, ATOMS:]
    gram_ref[0] = jnp.concatenate([gram[:16], gram[16:32]], axis=1)
    gram_ref[1] = jnp.concatenate([gram[32:48], gram[48:]], axis=1)


def two_parts(spatial):
    rows, channels = spatial.shape
    return pl.pallas_call(
        split_body,
        in_specs=[VMEM],
        out_specs=[VMEM, VMEM],
        out_shape=[
            jax.ShapeDtypeStruct((2 * rows, channels), jnp.bfloat16),
            jax.ShapeDtypeStruct((2, 16, LANES), F32),
        ],
        compiler_params=params(8),
        cost_estimate=cost(2**30, 2**17),
    )(spatial)


def project_body(half_ref, parts_ref, gram_ref, signal_ref, away_ref, kept_ref):
    first = half_ref[0] == 0
    parts = parts_ref[...]
    upper, lower = gram_ref[0], gram_ref[1]
    away_gram, kept_gram = jnp.where(first, lower, upper), jnp.where(first, upper, lower)
    for i in range(QUARTER):
        away_ref[i, BODY:] = away_gram
        kept_ref[i, BODY:] = kept_gram
    for out_ref, which in ((away_ref, 1 - half_ref[0]), (kept_ref, half_ref[0])):
        for i in range(QUARTER):
            column = pl.multiple_of((2 * i + which) * CHUNK, CHUNK)
            product = jnp.dot(
                parts, signal_ref[:, pl.ds(column, CHUNK)], preferred_element_type=F32
            )
            product = product[:ATOMS] + product[ATOMS:]
            for t in range(TILES):
                out_ref[i, t * ATOMS : (t + 1) * ATOMS] = product[:, t * LANES : (t + 1) * LANES]


def project(half, parts, gram, signal):
    channels, width = signal.shape
    return pl.pallas_call(
        project_body,
        in_specs=[SMEM, VMEM, VMEM, VMEM],
        out_specs=[VMEM, VMEM],
        out_shape=[jax.ShapeDtypeStruct((QUARTER, ROWS, LANES), F32)] * 2,
        compiler_params=params(8),
        cost_estimate=cost(2 * channels * LANES * width, 2 * channels * width),
    )(half, parts, gram, signal)


def to_segments(rows, segment, out_ref):
    for s in range(8):
        out_ref[pl.ds(s, segment, stride=8)] = rows[s * segment : (s + 1) * segment]


def from_segments(ref, segment):
    return jnp.concatenate([ref[pl.ds(s, segment, stride=8)] for s in range(8)], axis=0)


def spread_taps(temporal_ref, taps_ref):
    temporal = temporal_ref[...]
    columns = jnp.concatenate([temporal, temporal], axis=0).T
    for i in range(LENGTH // 4):
        c0, c1, c2, c3 = (
            jnp.broadcast_to(columns[4 * i + p : 4 * i + p + 1], (8, LANES)) for p in range(4)
        )
        even, odd = c0 + c1, c2 + c3
        for k, tap in enumerate((c0, c0 + c2, c2, even, even + odd, odd, c1, c1 + c3, c3)):
            taps_ref[k, i] = tap


def lane_half():
    return lax.broadcasted_iota(jnp.int32, (1, 8, LANES), 2) // ATOMS


def sublane():
    return lax.broadcasted_iota(jnp.int32, (1, 8, LANES), 1)


def later_segment(rows):
    up = pltpu.roll(rows, 7, 1)
    return jnp.where(sublane() == 7, pltpu.roll(up, ATOMS, 2), up)


def earlier_segment(rows):
    down = pltpu.roll(rows, 1, 1)
    return jnp.where(sublane() == 0, pltpu.roll(down, ATOMS, 2), down)


def over_sublanes(rows):
    count = rows.shape[0]
    return jnp.broadcast_to(rows.reshape(count, 1, LANES), (count, 8, LANES))


def spread_later(rows, spread_ref, beyond=None):
    segment = rows.shape[0]
    reach = segment + LENGTH
    for first in range(0, reach, segment):
        count = min(segment, reach - first)
        rows = rows[:count]
        if first > 0:
            rows = later_segment(rows)
            if beyond is not None:
                last = (sublane() == 7) & (lane_half() == 1)
                start = first - segment
                rows = jnp.where(last, over_sublanes(beyond[start : start + count]), rows)
        spread_ref[first // 4 : (first + count) // 4] = rows.reshape(count // 4, 4, 8, LANES)


def spread_earlier(rows, spread_ref, before=None):
    segment = rows.shape[0]
    start = LENGTH
    while True:
        skip = max(0, -start)
        first, count = start + skip, segment - skip
        kept = rows[skip:]
        spread_ref[first // 4 : (first + count) // 4] = kept.reshape(count // 4, 4, 8, LANES)
        if start <= 0:
            return
        rows = earlier_segment(rows)
        start -= segment
        if before is not None:
            skip = max(0, -start)
            rim = over_sublanes(before[start + skip : start + segment])
            if skip:
                rim = jnp.concatenate([jnp.zeros((skip, 8, LANES), F32), rim], axis=0)
            rows = jnp.where((sublane() == 0) & (lane_half() == 0), rim, rows)


def short_inputs(segment, spread_ref, inputs_ref, offset):
    count = (segment + LENGTH) // 4 - 1

    def x(p):
        p = p + offset
        return spread_ref[p // 4 : p // 4 + count, p % 4]

    x0, x1, x2, x3, x4, x5, x6 = (x(p) for p in range(7))
    inputs_ref[0, :count] = (x0 - x1) - (x2 - x3)
    inputs_ref[1, :count] = x2 - x3
    inputs_ref[2, :count] = (x4 - x5) - (x2 - x3)
    inputs_ref[3, :count] = x1 - x3
    inputs_ref[4, :count] = x3
    inputs_ref[5, :count] = x5 - x3
    inputs_ref[6, :count] = (x2 - x1) - (x4 - x3)
    inputs_ref[7, :count] = x4 - x3
    inputs_ref[8, :count] = (x6 - x5) - (x4 - x3)


def filter_rows(segment, inputs_ref, taps_ref, sums_ref, reverse):
    taps = LENGTH // 4
    phase = segment // 4

    @pl.loop(0, 9, unroll=3)
    def _(k):
        sums = [None] * phase
        held = {}
        for j in range(phase + taps - 1):
            if j < taps:
                held[j] = taps_ref[8 - k, taps - 1 - j] if reverse else taps_ref[k, j]
            value = inputs_ref[k, j]
            for m in range(max(0, j - phase + 1), min(taps, j + 1)):
                term = value * held[m]
                sums[j - m] = term if sums[j - m] is None else sums[j - m] + term
        for i in range(phase):
            sums_ref[k, i] = sums[i]

    def total(i, k):
        return sums_ref[i, :phase] + sums_ref[k, :phase]

    a, b, c = total(0, 1), total(3, 4), total(6, 7)
    d, e, f = total(1, 2), total(4, 5), total(7, 8)
    rows = jnp.stack([a + b, b + c, d + e, e + f], axis=1)
    return rows.reshape(segment, 8, LANES)


def filter_scratch(segment):
    reach = (segment + LENGTH) // 4
    return [
        pltpu.VMEM((9, LENGTH // 4, 8, LANES), F32),
        pltpu.VMEM((reach, 4, 8, LANES), F32),
        pltpu.VMEM((9, reach, 8, LANES), F32),
        pltpu.VMEM((9, segment // 4, 8, LANES), F32),
    ]


def rebuild_body(
    place_ref, temporal_ref, before_ref, first_ref, second_ref, after_ref,
    rebuilt_ref, beyond_ref, point_ref, rim_ref, taps_ref, spread_ref, inputs_ref, sums_ref, wide_ref,
):
    place = place_ref[0]
    spread_taps(temporal_ref, taps_ref)
    before = jnp.where(place == 0, 0.0, before_ref[...])
    after = jnp.where(place == CHUNKS - 1, 0.0, after_ref[...])
    first, second = first_ref[...], second_ref[...]
    upper = jnp.concatenate([before[:, 128:], first], axis=1)
    lower = jnp.concatenate([second, after[:, :128]], axis=1)
    to_segments(jnp.concatenate([upper, lower], axis=0).T, NARROW, point_ref)

    upper = jnp.concatenate([upper, second[:, :128]], axis=1)
    lower = jnp.concatenate([second[:, 64:], after, after[:, :64]], axis=1)
    to_segments(jnp.concatenate([upper, lower], axis=0).T, WIDE, wide_ref)
    ahead = before[:, :128]
    ahead = jnp.concatenate([ahead, ahead], axis=0).T
    spread_earlier(wide_ref[...].reshape(WIDE, 8, LANES), spread_ref, ahead)
    short_inputs(WIDE, spread_ref, inputs_ref, 1)
    rebuilt = filter_rows(WIDE, inputs_ref, taps_ref, sums_ref, True)

    wide_ref[...] = rebuilt.reshape(8 * WIDE, LANES)
    rows = from_segments(wide_ref, WIDE)
    swapped = pltpu.roll(rows, ATOMS, 1)
    left = lax.broadcasted_iota(jnp.int32, (1, LANES), 1) < ATOMS
    lower = jnp.concatenate([swapped[384:], rows[:320]], axis=0)
    to_segments(jnp.where(left, rows[:384], lower), NARROW, rebuilt_ref)
    beyond_ref[...] = jnp.where(left, swapped[320:], rows[320:])

    starting = place % 2 == 0
    start = jnp.where(left, rows[128:256], swapped[256:384])
    end = jnp.where(left, swapped[64:192], rows[192:320])
    rim_ref[:LANES] = jnp.where(starting, start, end)
    rim_ref[LANES:] = jnp.where(starting, first[:, :128], second[:, 128:])


def rebuild(place, temporal, activations):
    atoms, width = activations.shape
    half = CHUNK // 2
    last = width // half - 1
    block = (atoms, half)
    shapes = [(8 * NARROW, LANES), (LENGTH, LANES), (8 * NARROW, LANES), (RIM, LANES)]
    return pl.pallas_call(
        rebuild_body,
        grid_spec=pltpu.PrefetchScalarGridSpec(
            num_scalar_prefetch=1,
            grid=(1,),
            in_specs=[
                pl.BlockSpec((ATOMS, LENGTH), lambda i, place: (0, 0)),
                pl.BlockSpec(block, lambda i, place: (0, jnp.maximum(2 * place[0] - 1, 0))),
                pl.BlockSpec(block, lambda i, place: (0, 2 * place[0])),
                pl.BlockSpec(block, lambda i, place: (0, 2 * place[0] + 1)),
                pl.BlockSpec(block, lambda i, place: (0, jnp.minimum(2 * place[0] + 2, last))),
            ],
            out_specs=[pl.BlockSpec(shape, lambda i, place: (0, 0)) for shape in shapes],
            scratch_shapes=filter_scratch(WIDE) + [pltpu.VMEM((8 * WIDE, LANES), F32)],
        ),
        out_shape=[jax.ShapeDtypeStruct(shape, F32) for shape in shapes],
        compiler_params=params(12),
        cost_estimate=cost(2 * 8 * WIDE * LANES * LENGTH, 2**20),
    )(place, temporal, activations, activations, activations, activations)


def steps_body(
    total, begin_ref, place_ref, step_ref, mine_ref, inner_ref, outer_ref, rim_ref, rebuilt_ref,
    beyond_ref, point_ref, temporal_ref, threshold_ref, out_ref, taps_ref, spread_ref, inputs_ref,
    sums_ref, cross_ref, side_ref, mix_ref,
):
    begin, place = begin_ref[0], place_ref[0]
    first = place % 2 == 0
    rate = step_ref[0]
    spread_taps(temporal_ref, taps_ref)

    own, other = mine_ref[BODY:], inner_ref[BODY // 2 :]
    upper, lower = jnp.where(first, own, other), jnp.where(first, other, own)
    gram = jnp.concatenate(
        [upper[:, :ATOMS], upper[:, ATOMS:], lower[:, :ATOMS], lower[:, ATOMS:]], axis=0
    )
    mix_ref[...] = jnp.zeros_like(mix_ref)
    mix_ref[:ATOMS, :ATOMS] = gram
    mix_ref[ATOMS:, ATOMS:] = gram

    near, far = slice(0, ATOMS), slice(ATOMS, 2 * ATOMS)
    left = jnp.where(first, outer_ref[far], inner_ref[far])
    right = jnp.where(first, inner_ref[near], outer_ref[near])
    beyond = jnp.where(first, inner_ref[far], outer_ref[far])
    tiles = [mine_ref[t * ATOMS : (t + 1) * ATOMS] for t in range(TILES)]
    upper = jnp.concatenate([left, tiles[0], tiles[1]], axis=1)
    lower = jnp.concatenate([tiles[2], tiles[3], right], axis=1)
    to_segments(jnp.concatenate([upper, lower], axis=0).T, NARROW, cross_ref)
    beyond = jnp.concatenate([beyond, beyond], axis=0).T

    left_half = lax.broadcasted_iota(jnp.int32, (1, LANES), 1) < ATOMS
    at_start = left_half & (place == 0)
    at_end = jnp.logical_not(left_half) & (place == CHUNKS - 1)
    added = rim_ref[:LANES]
    swapped = pltpu.roll(added, ATOMS, 1)
    to_segments(
        jnp.concatenate(
            [
                jnp.where(at_start, added, 0.0),
                jnp.where(at_start, swapped, 0.0),
                jnp.where(at_end, swapped, 0.0),
            ],
            axis=0,
        ),
        NARROW,
        side_ref,
    )
    rebuilt = rebuilt_ref[...] + side_ref[...]
    added_beyond = jnp.where(left_half, swapped, added)
    rebuilt_beyond = beyond_ref[...] + jnp.where(place == CHUNKS - 1, added_beyond, 0.0)
    rim = rim_ref[LANES:]
    rim = jnp.concatenate([rim, rim], axis=0).T
    to_segments(
        jnp.concatenate(
            [jnp.where(at_start, rim, 0.0), jnp.zeros_like(rim), jnp.where(at_end, rim, 0.0)],
            axis=0,
        ),
        NARROW,
        side_ref,
    )

    shape = (NARROW, 8, LANES)
    sample = lax.broadcasted_iota(jnp.int32, shape, 0) + (
        (lane_half() * 8 + sublane()) * NARROW + (begin - LENGTH)
    )
    sample_beyond = lax.broadcasted_iota(jnp.int32, (LENGTH, LANES), 0) + (begin + CHUNK + LENGTH)
    shrink = threshold_ref[...]
    shrink = jnp.concatenate([shrink, shrink], axis=1).reshape(1, 1, LANES)

    def mixed(rebuilt):
        return jnp.dot(rebuilt, mix_ref[...], precision=HIGHEST, preferred_element_type=F32)

    def projected(rebuilt):
        rows = (mixed(rebuilt) - cross_ref[...]).reshape(shape)
        return jnp.where(sample < total, rows, 0.0)

    def stepped(point, rows, rows_beyond=None):
        spread_later(rows, spread_ref, rows_beyond)
        short_inputs(NARROW, spread_ref, inputs_ref, 0)
        gradient = filter_rows(NARROW, inputs_ref, taps_ref, sums_ref, False)
        return jnp.maximum(point - rate * (gradient + shrink), 0.0)

    inertia = 1.0
    inertia_next = (1.0 + (1.0 + 4.0 * inertia * inertia) ** 0.5) / 2.0
    momentum = (inertia - 1.0) / inertia_next
    previous = (point_ref[...] + side_ref[...]).reshape(shape)
    beyond = jnp.where(sample_beyond < total, mixed(rebuilt_beyond) - beyond, 0.0)
    update = stepped(previous, projected(rebuilt), beyond)
    point = update + momentum * (update - previous)
    point = jnp.where(sample >= 0, point, 0.0)

    spread_earlier(point, spread_ref)
    short_inputs(NARROW, spread_ref, inputs_ref, 1)
    rebuilt = filter_rows(NARROW, inputs_ref, taps_ref, sums_ref, True)
    update = stepped(point, projected(rebuilt.reshape(8 * NARROW, LANES)))

    cross_ref[...] = update.reshape(8 * NARROW, LANES)
    columns = from_segments(cross_ref, NARROW).T
    for i in range(QUARTER):
        out_ref[i] = jnp.concatenate([columns[:ATOMS, 128:], columns[ATOMS:, :256]], axis=1)


def steps(
    total, begin, place, step_size, mine, inner, outer, rim, before_steps, temporal, threshold
):
    def body(*refs):
        steps_body(total, *refs)

    return pl.pallas_call(
        body,
        in_specs=[SMEM] * 3 + [VMEM] * 9,
        out_specs=VMEM,
        out_shape=jax.ShapeDtypeStruct((QUARTER, ATOMS, CHUNK), F32),
        scratch_shapes=filter_scratch(NARROW)
        + [pltpu.VMEM((8 * NARROW, LANES), F32)] * 2
        + [pltpu.VMEM((LANES, LANES), F32)],
        compiler_params=params(12),
        cost_estimate=cost(6 * 8 * NARROW * LANES * LENGTH, 2**20),
    )(begin, place, step_size, mine, inner, outer, rim, *before_steps, temporal, threshold)


def place_copies(half, chunks_ref, out_ref, sems):
    copies = []
    rows = ATOMS // 2
    for i in range(2 * QUARTER):
        chunk, part = i // 2, pl.ds(i % 2 * rows, rows)
        column = pl.multiple_of((2 * chunk + half) * CHUNK, CHUNK)
        copies.append(
            pltpu.make_async_copy(
                chunks_ref.at[chunk, part], out_ref.at[part, pl.ds(column, CHUNK)], sems.at[i]
            )
        )
    for copy in copies:
        copy.start()
    for copy in copies:
        copy.wait()


def place_mine_body(half_ref, chunks_ref, out_ref, sems):
    place_copies(half_ref[0], chunks_ref, out_ref, sems)


def place_other_body(half_ref, chunks_ref, begun_ref, out_ref, sems):
    place_copies(1 - half_ref[0], chunks_ref, out_ref, sems)


def place_half(half, chunks, begun=None):
    out_shape = jax.ShapeDtypeStruct((ATOMS, CHUNKS * CHUNK), F32)
    first = begun is None
    return pl.pallas_call(
        place_mine_body if first else place_other_body,
        in_specs=[SMEM, ANY] + ([] if first else [ANY]),
        out_specs=ANY,
        out_shape=out_shape,
        scratch_shapes=[pltpu.SemaphoreType.DMA((2 * QUARTER,))],
        input_output_aliases={} if first else {2: 0},
        compiler_params=params(4),
        cost_estimate=cost(0, 2**20),
    )(half, chunks, *([] if first else [begun]))


def solution(mesh):
    blocks = mesh.shape["tm"]
    split = Mesh(mesh.devices.reshape(2, 4, 2, blocks), ("zh", "y", "c", "tm"))
    swap = [(0, 1), (1, 0)]
    line = ("zh", "y", "c", "tm")

    def device(zh, q, tm):
        return (zh * CHUNKS + q) * blocks + tm

    outside, rims = [], []
    for zh in range(2):
        for tm in range(blocks):
            for q in range(1, CHUNKS - 1, 2):
                outside.append((device(zh, q, tm), device(zh, q + 1, tm)))
            if tm + 1 < blocks:
                last = device(zh, CHUNKS - 1, tm)
                near = 1 - zh if (tm + 1) % RUN == 0 else zh
                outside.append((last, device(zh, 0, tm + 1)))
                rims.append((last, device(near, 0, tm + 1)))
    outside = outside + [(b, a) for a, b in outside]
    rims = rims + [(b, a) for a, b in rims]

    def per_device(signal, spatial, temporal, activations, threshold, step_size):
        half = lax.axis_index("c").astype(jnp.int32)
        place = lax.axis_index("y").astype(jnp.int32) * 2 + half
        time_block = lax.axis_index("tm").astype(jnp.int32)
        width = activations.shape[1]
        parts, gram_halves = two_parts(spatial.T)
        away, kept = project(half[None], parts, gram_halves, signal)
        summed = kept + lax.ppermute(away, "c", swap)

        activations, summed = lax.optimization_barrier((activations, summed))
        pieces = lax.all_to_all(summed, "y", 0, 0, tiled=True)
        *before_steps, rim = rebuild(place[None], temporal, activations)
        rim = lax.ppermute(rim, line, rims)
        group_sum = jnp.sum(pieces, axis=0)
        group_sum, before_steps = lax.optimization_barrier((group_sum, before_steps))
        mine = jnp.sum(lax.all_gather(group_sum, "zh", axis=0), axis=0)

        first = half == 0
        start, end, gram = mine[: BODY // 2], mine[BODY // 2 : BODY], mine[BODY:]
        outer = jnp.concatenate([jnp.where(first, start, end), gram], axis=0)
        outer = lax.ppermute(outer, line, outside)
        inner = jnp.concatenate([jnp.where(first, end, start), gram], axis=0)
        inner = lax.ppermute(inner, "c", swap)
        begin = time_block * width + place * CHUNK
        update = steps(
            blocks * width, begin[None], place[None], step_size, mine, inner, outer, rim,
            before_steps, temporal, threshold[None, :],
        )

        gathered = lax.all_to_all(update, "y", 0, 0, tiled=True)
        other = lax.ppermute(gathered, "c", swap)
        return place_half(half[None], other, place_half(half[None], gathered))

    chan = ("zh", "y", "c")
    in_specs = (P(chan, "tm"), P(chan, None), P(), P(None, "tm"), P(), P())
    return jax.shard_map(
        per_device, mesh=split, in_specs=in_specs, out_specs=P(None, "tm"), check_vma=False
    )
```
